32 devices in a mesh: batch: 4 (over y, x), seq: 8 (over z, core).
Axes of the slice: x: 2, y: 2, z: 4, core: 2. Of those that a mesh axis runs over, the one named last changes fastest.
Arguments:
- inputs: bfloat16 [8, 1024, 512], P('batch', 'seq'), may hold values from -6 to 6
- doc_starts: int32 [8, 4], P('batch'), may hold values from 0 to 1023, as said below
- cotangent: bfloat16 [8, 1024, 512], P('batch', 'seq'), may hold values from -6 to 6
- norm_gain: bfloat16 [2, 2, 512], replicated, may hold values from 0.099609375 to 1.8984375
- norm_bias: bfloat16 [2, 2, 512], replicated, may hold values from -1 to 1
- qkv_weight: bfloat16 [2, 512, 1536], replicated, may hold values from -0.25 to 0.25
- qkv_bias: bfloat16 [2, 3, 512], replicated, may hold values from -1 to 1
- out_weight: bfloat16 [2, 512, 512], replicated, may hold values from -1 to 1
- out_bias: bfloat16 [2, 512], replicated, may hold values from -1 to 1
- in_weight: bfloat16 [2, 512, 2048], replicated, may hold values from -0.25 to 0.25
- in_bias: bfloat16 [2, 2048], replicated, may hold values from -1.5 to 1.5
- down_weight: bfloat16 [2, 2048, 512], replicated, may hold values from -0.125 to 0.125
- down_bias: bfloat16 [2, 512], replicated, may hold values from -1 to 1
Outputs:
- result: bfloat16 [8, 1024, 512], P('batch', 'seq')
- grad_inputs: float32 [8, 1024, 512], P('batch', 'seq')
- grad_norm_gain: float32 [2, 2, 512], P(None, None, 'seq')
- grad_norm_bias: float32 [2, 2, 512], P(None, None, 'seq')
- grad_qkv_weight: float32 [2, 512, 1536], P(None, 'seq')
- grad_qkv_bias: float32 [2, 3, 512], P(None, None, 'seq')
- grad_out_weight: float32 [2, 512, 512], P(None, 'seq')
- grad_out_bias: float32 [2, 512], P(None, 'seq')
- grad_in_weight: float32 [2, 512, 2048], P(None, 'seq')
- grad_in_bias: float32 [2, 2048], P(None, 'seq')
- grad_down_weight: float32 [2, 2048, 512], P(None, 'seq')
- grad_down_bias: float32 [2, 512], P(None, 'seq')
The draws below stay inside these ranges and needn't reach their ends.
Inputs may be any that keep to these rules, and one draw needn't show every extreme that they name: `doc_starts`: in each row the entries are nondecreasing and the first is 0; an entry p > 0 marks the first token of a document at place p of the row, and repeated entries mark one start. In each aligned block of 2 rows that share an index of batch, at least one row holds only zeros.
All inputs are finite; a program needn't handle non-finite values.
Results may differ from the reference program's by a relative error of at most 0.008.
Values sent between devices are 32-bit elements; how exact they have to be, the bound alone decides.
No kernel may reach another device: no remote copies, remote signals or barrier semaphores. Data moves between devices by JAX's collectives and lax.ppermute only.
A program may use at most 192 MiB of HBM per device.

```python
import math
import jax
import jax.numpy as jnp
from jax import lax

D = 512
HEADS = 8
HEAD = 64
FF = 2048
FEAT = 64
ROT = 16
GROUP = 64
LAYERS = 2
NDOC = 4
B_LOC = 2
ROWS = 8
ROW_LEN = 1024


def draw_doc_starts(key, part):
    key = jax.random.fold_in(key, 7)
    inner_key, pick_key = jax.random.split(key)
    inner = jnp.sort(jax.random.randint(inner_key, (ROWS, NDOC - 1), 1, ROW_LEN), axis=1)
    picked = jax.random.randint(pick_key, (ROWS // B_LOC,), 0, B_LOC)
    lone_row = jnp.arange(ROWS) % B_LOC == jnp.repeat(picked, B_LOC, total_repeat_length=ROWS)
    inner = jnp.where(lone_row[:, None], 0, inner)
    return jnp.concatenate([jnp.zeros((ROWS, 1), jnp.int32), inner.astype(jnp.int32)], axis=1)


def with_spikes(drawn, key, source, target, blocks, factor):
    def block_of(position):
        return (jnp.arange(drawn.shape[position]) // (drawn.shape[position] // blocks)).reshape((-1,) + (1,) * (drawn.ndim - 1 - position))

    one_side = jax.random.permutation(key, blocks)[block_of(target)]
    far = (block_of(target) + blocks // 2) % blocks
    return jnp.where((block_of(source) == one_side) | (block_of(source) == far), factor * drawn, drawn)


def block_scale(key, shape, cuts, least, high):
    level, own = 1.0, jax.random.fold_in(key, 6)
    for position, parts in cuts:
        heights = jnp.exp(jax.random.uniform(jax.random.fold_in(own, position), (parts,), jnp.float32, least / len(cuts), high / len(cuts)))
        level = level * jnp.repeat(heights, shape[position] // parts).reshape([-1 if axis == position else 1 for axis in range(len(shape))])
    return level


def scatter_about(stream_key, extent, deviation, limit, cuts=(), held_as=jnp.bfloat16):
    values = jax.random.normal(stream_key, extent, jnp.float32) * deviation
    if len(cuts) > 0:
        values = block_scale(stream_key, extent, cuts, -0.22, 0.18) * values
    return jnp.clip(values, min=-limit, max=limit).astype(held_as)


def gaussian_with(stream_key, dims, spread, reach, cuts, heavy, kind=jnp.bfloat16):
    values = spread * jax.random.normal(stream_key, dims, jnp.float32)
    if cuts:
        values = values * block_scale(stream_key, dims, cuts, -0.22, 0.18)
    return jnp.clip(with_spikes(values, jax.random.fold_in(stream_key, 3), *heavy), -reach, reach).astype(kind)


def setup_inputs(seed: int = 0) -> dict:
    splits = jax.random.split(jax.random.key(seed), 14)
    inputs = scatter_about(splits[0], (ROWS, ROW_LEN, D), 1.0, 6.0, ((0, 4), (1, 8)))
    doc_starts = draw_doc_starts(jax.random.fold_in(splits[13], 71), 0)
    cotangent = gaussian_with(splits[2], (ROWS, ROW_LEN, D), 1.0, 6.0, ((0, 4), (1, 8)), (1, 2, 8, 2.0))
    norm_gain = jnp.clip(1.0 + 0.18 * jax.random.normal(splits[3], (LAYERS, 2, D), jnp.float32), 0.099609375, 1.8984375).astype(jnp.bfloat16)
    norm_bias = scatter_about(splits[4], (LAYERS, 2, D), 0.2, 1.0)
    qkv_weight = scatter_about(splits[5], (LAYERS, D, 3 * D), D ** -0.5, 0.25)
    qkv_bias = scatter_about(splits[6], (LAYERS, 3, D), 0.2, 1.0)
    out_weight = scatter_about(splits[7], (LAYERS, D, D), (D // 16) ** -0.5, 1.0)
    out_bias = scatter_about(splits[8], (LAYERS, D), 0.2, 1.0)
    in_weight = scatter_about(splits[9], (LAYERS, D, FF), D ** -0.5, 0.25)
    in_bias = scatter_about(splits[10], (LAYERS, FF), 0.3, 1.5)
    down_weight = scatter_about(splits[11], (LAYERS, FF, D), FF ** -0.5, 0.125)
    down_bias = scatter_about(splits[12], (LAYERS, D), 0.2, 1.0)
    return {"inputs": inputs, "doc_starts": doc_starts, "cotangent": cotangent, "norm_gain": norm_gain, "norm_bias": norm_bias, "qkv_weight": qkv_weight, "qkv_bias": qkv_bias, "out_weight": out_weight, "out_bias": out_bias, "in_weight": in_weight, "in_bias": in_bias, "down_weight": down_weight, "down_bias": down_bias}


epsilon = 1e-05
PRECISE = lax.Precision.HIGHEST

@jax.custom_vjp
def low(v):
    return lax.optimization_barrier(v.astype(jnp.bfloat16)).astype(jnp.float32)

@jax.custom_vjp
def low_back(v):
    return v

def low_keep(v):
    return (low(v), None)

def low_pass(kept, grad):
    return (grad,)

def back_keep(v):
    return (v, None)

def back_low(kept, grad):
    return (low(grad),)
low.defvjp(low_keep, low_pass)
low_back.defvjp(back_keep, back_low)

def cosine_table():
    frequency = jnp.arange(FEAT, dtype=jnp.float32)[:, None]
    columns = jnp.arange(HEAD, dtype=jnp.float32)[None, :]
    entries = jnp.cos(math.pi * (2.0 * columns + 1.0) * frequency / (2.0 * HEAD)) * math.sqrt(2.0 / HEAD)
    first_row = jnp.where(jnp.arange(FEAT) == 0, math.sqrt(0.5), 1.0)
    return entries * first_row[:, None]

def rotate(heads_x, places):
    half_rot = ROT // 2
    inverse = 10000.0 ** (-(jnp.arange(half_rot, dtype=jnp.float32) * 2.0 / ROT))
    angles = places.astype(jnp.float32)[..., None, None] * inverse
    cosine = jnp.cos(angles)
    sine_part = jnp.sin(angles)
    leading = heads_x[..., :half_rot]
    trailing = heads_x[..., half_rot:ROT]
    return jnp.concatenate([leading * cosine - trailing * sine_part, trailing * cosine + leading * sine_part, heads_x[..., ROT:]], axis=-1)

def layer_norm(values, gain, shift):
    centred = values - lax.optimization_barrier(jnp.mean(values, axis=-1, keepdims=True))
    variance = lax.optimization_barrier(jnp.mean(centred * centred, axis=-1, keepdims=True))
    return centred * lax.rsqrt(variance + epsilon) * gain + shift

def exact_gelu(values):
    return jax.nn.gelu(values, approximate=False)

def block_step(running, pieces):
    state, norm_state = running
    feat_query, feat_key, value_rows, segment, block_start = pieces
    positions = jnp.arange(GROUP)
    causal = (positions[None, :] <= positions[:, None]) & (segment[None, :] == segment[:, None])
    scores = low_back(causal.astype(jnp.float32)[None] * jnp.einsum('ihf,jhf->hij', feat_query, feat_key, precision=PRECISE))
    denominator = jnp.swapaxes(lax.optimization_barrier(jnp.sum(scores, axis=-1)), 0, 1)
    numerator = jnp.einsum('hij,jhd->ihd', low(scores), value_rows, precision=PRECISE)
    cross_mask = (segment < block_start).astype(jnp.float32)
    numerator = numerator + cross_mask[:, None, None] * jnp.einsum('ihf,hfd->ihd', feat_query, state, precision=PRECISE)
    denominator = denominator + cross_mask[:, None] * jnp.einsum('ihf,hf->ih', feat_query, norm_state, precision=PRECISE)
    tail_mask = (segment == segment[GROUP - 1]).astype(jnp.float32)
    carried = (segment[GROUP - 1] < block_start).astype(jnp.float32)
    tail_keys = feat_key * tail_mask[:, None, None]
    state = carried * state + jnp.einsum('jhf,jhd->hfd', tail_keys, value_rows, precision=PRECISE)
    norm_state = carried * norm_state + lax.optimization_barrier(jnp.sum(tail_keys, axis=0))
    return ((state, norm_state), (numerator, denominator))

def linear_attention(feat_query, feat_key, value_rows, segment):
    block_count = segment.shape[0] // GROUP
    block_starts = (jnp.arange(block_count) * GROUP).astype(jnp.int32)
    initial = (jnp.zeros((HEADS, FEAT, HEAD), jnp.float32), jnp.zeros((HEADS, FEAT), jnp.float32))
    blocks_in = (feat_query.reshape(block_count, GROUP, HEADS, FEAT), feat_key.reshape(block_count, GROUP, HEADS, FEAT), value_rows.reshape(block_count, GROUP, HEADS, HEAD), segment.reshape(block_count, GROUP), block_starts)
    finals, (numerator, denominator) = lax.scan(jax.checkpoint(block_step), initial, blocks_in)
    return (numerator.reshape(-1, HEADS, HEAD), denominator.reshape(-1, HEADS))

def layer_forward(hidden, gain, shift, qkv_w, qkv_b, out_w, out_b, in_w, in_b, down_w, down_b, segment, places, cosines):
    tokens = hidden.shape[0]
    first = low(layer_norm(hidden, gain[0], shift[0]))
    second = low(layer_norm(hidden, gain[1], shift[1]))
    packed = low_back(jnp.dot(first, qkv_w, precision=PRECISE) + qkv_b.reshape(3 * D))
    queries = packed[:, :D].reshape(tokens, HEADS, HEAD)
    keys_part = packed[:, D:2 * D].reshape(tokens, HEADS, HEAD)
    value_rows = low(packed[:, 2 * D:].reshape(tokens, HEADS, HEAD))
    feat_query = low(jnp.exp(jnp.einsum('thj,fj->thf', rotate(queries, places), cosines, precision=PRECISE)))
    feat_key = low(jnp.exp(jnp.einsum('thj,fj->thf', rotate(keys_part, places), cosines, precision=PRECISE)))
    numerator, denominator = linear_attention(feat_query, feat_key, value_rows, segment)
    numerator = low_back(numerator)
    attended = low((numerator / denominator[..., None]).reshape(tokens, D))
    attn_out = low_back(jnp.dot(attended, out_w, precision=PRECISE) + out_b)
    lifted = low_back(jnp.dot(second, in_w, precision=PRECISE) + in_b)
    feed = low_back(jnp.dot(low(exact_gelu(lifted)), down_w, precision=PRECISE) + down_b)
    return hidden + attn_out + feed

def reference(inputs, doc_starts, cotangent, norm_gain, norm_bias, qkv_weight, qkv_bias, out_weight, out_bias, in_weight, in_bias, down_weight, down_bias):
    cosines = cosine_table()
    weights = tuple((tensor.astype(jnp.float32) for tensor in (norm_gain, norm_bias, qkv_weight, qkv_bias, out_weight, out_bias, in_weight, in_bias, down_weight, down_bias)))
    positions = jnp.arange(ROW_LEN, dtype=jnp.int32)

    def forward(row_value, segment, places, params_all):
        hidden = row_value
        for level_index in range(LAYERS):
            hidden = layer_forward(hidden, *[tensor[level_index] for tensor in params_all], segment, places, cosines)
        return hidden

    def per_row(totals, row_items):
        row_input, row_starts, row_upstream = row_items
        segment = lax.optimization_barrier(jnp.max(jnp.where(row_starts[None, :] <= positions[:, None], row_starts[None, :], 0), axis=1))
        places = positions - segment

        def closed(row_value, params_all):
            return forward(row_value, segment, places, params_all)
        outcome, backward = jax.vjp(closed, row_input.astype(jnp.float32), weights)
        grad_row, grad_params = backward(row_upstream.astype(jnp.float32))
        totals = jax.tree.map(jnp.add, totals, grad_params)
        return (totals, (outcome.astype(jnp.bfloat16), grad_row))
    start_totals = tuple((jnp.zeros_like(tensor) for tensor in weights))
    totals, (outputs, grad_inputs) = lax.scan(per_row, start_totals, (inputs, doc_starts, cotangent))
    return (outputs, grad_inputs, totals[0], totals[1], totals[2], totals[3], totals[4], totals[5], totals[6], totals[7], totals[8], totals[9])
```

```python
import functools
import math

import jax
import jax.numpy as jnp
import numpy as np
from jax import lax
from jax.experimental import pallas as pl
from jax.experimental.pallas import tpu as pltpu
from jax.sharding import PartitionSpec as P

D = 512
HEADS = 8
HEAD = 64
FF = 2048
ROT = 16
LAYERS = 2
NDOC = 4
LEN = 128
PAIRS = HEADS // 2
PACK = 2 * HEAD + 8
WIDE = 512

epsilon = 1e-05
f32, bf16 = jnp.float32, jnp.bfloat16
NN = (((1,), (0,)), ((), ()))
NT = (((1,), (1,)), ((), ()))
TN = (((0,), (0,)), ((), ()))


def dot(a, b, dims=NN):
    return lax.dot_general(a, b, dims, preferred_element_type=f32)


def split(x):
    high = x.astype(bf16)
    return high, (x - high.astype(f32)).astype(bf16)


def sds(shape, dtype=f32):
    return jax.ShapeDtypeStruct(shape, dtype)


def norm_parts(hidden):
    centred = hidden - jnp.mean(hidden, axis=-1, keepdims=True)
    variance = jnp.mean(centred * centred, axis=-1, keepdims=True)
    inverse = lax.rsqrt(variance + epsilon)
    return centred * inverse, inverse


def segment_of(position, starts, row):
    found = jnp.zeros_like(position)
    for k in range(NDOC):
        entry = starts[row, k]
        found = jnp.maximum(found, jnp.where(entry <= position, entry, 0))
    return found


def masks_of(row, meta, starts):
    begin = meta[0]
    at_i = begin + lax.broadcasted_iota(jnp.int32, (LEN, 128), 0)
    at_j = begin + lax.broadcasted_iota(jnp.int32, (LEN, 128), 1)
    seg_i, seg_j = segment_of(at_i, starts, row), segment_of(at_j, starts, row)
    last = jnp.int32(0)
    for k in range(NDOC):
        entry = starts[row, k]
        last = jnp.maximum(last, jnp.where(entry <= begin + (LEN - 1), entry, 0))
    intra = jnp.where((at_j <= at_i) & (seg_i == seg_j), 1.0, 0.0).astype(f32)
    cross = jnp.where(seg_i < begin, 1.0, 0.0).astype(f32)
    tail = jnp.where(seg_i == last, 1.0, 0.0).astype(f32)
    return intra, cross, tail


def low_lanes(rows):
    return lax.broadcasted_iota(jnp.int32, (rows, 128), 1) < HEAD


def rotate(x, tables):
    base, ahead, behind = tables
    return x * base + pltpu.roll(x, 120, 1) * ahead + pltpu.roll(x, 8, 1) * behind


def rotate_back(g, tables):
    base, ahead, behind = tables
    return g * base + pltpu.roll(g * ahead, 8, 1) + pltpu.roll(g * behind, 120, 1)


def featurize(x, tables, high, low):
    pieces = [rotate(x[:, g * 128 : (g + 1) * 128], tables) for g in range(4)]
    found = []
    for g in range(2):
        a, b = split(jnp.concatenate(pieces[2 * g : 2 * g + 2], axis=1))
        found.append(jnp.exp(dot(a, high) + dot(b, high) + dot(a, low)))
    return jnp.concatenate(found, axis=1)


def unfeaturize(g, tables, high, low):
    found = []
    for k in range(2):
        a, b = split(g[:, k * 256 : (k + 1) * 256])
        back = dot(a, high, NT) + dot(b, high, NT) + dot(a, low, NT)
        found += [rotate_back(back[:, :128], tables), rotate_back(back[:, 128:], tables)]
    return jnp.concatenate(found, axis=1)


def head_ones():
    across = lax.broadcasted_iota(jnp.int32, (256, 256), 0) // HEAD
    along = lax.broadcasted_iota(jnp.int32, (256, 256), 1) // HEAD
    return jnp.where(across == along, 1.0, 0.0).astype(bf16)


def head_sum(x, ones):
    found = []
    for g in range(2):
        a, b = split(x[:, g * 256 : (g + 1) * 256])
        found.append(dot(a, ones) + dot(b, ones))
    return jnp.concatenate(found, axis=1)


def store_halves(meta, keep_ref, send_ref, halves):
    def put(ref, half):
        for row, at, value in halves[half]:
            ref[row, at[0] : at[1], :] = value

    core = meta[1]
    for mine in range(2):

        @pl.when(core == mine)
        def _():
            put(keep_ref, mine)
            put(send_ref, 1 - mine)


def pack_states(rows, left_of, right, norm_of):
    low = low_lanes(HEAD)
    halves = [[], []]
    for row in range(rows):
        at = slice(row * LEN, (row + 1) * LEN)
        left, norm = left_of(row), norm_of(row)
        for pair in range(PAIRS):
            lanes = slice(pair * 128, (pair + 1) * 128)
            both = dot(left[:, lanes], right[at, lanes], TN)
            half, place = pair // 2, pair % 2
            halves[half].append(
                (row, (place * HEAD, (place + 1) * HEAD), jnp.where(low, both[:HEAD], both[HEAD:]))
            )
        for half in range(2):
            pieces = [norm[:, (2 * half + k) * 128 : (2 * half + k + 1) * 128] for k in range(2)]
            block = jnp.concatenate(pieces + [jnp.zeros((6, 128), f32)], axis=0)
            halves[half].append((row, (2 * HEAD, PACK), block))
    return halves


def unpack_state(meta, mine_ref, theirs_ref, row):
    low = low_lanes(HEAD)
    blocks, norms = [], []
    for half in range(2):
        packed = jnp.where(meta[1] == half, mine_ref[row], theirs_ref[row])
        for place in range(2):
            state = packed[place * HEAD : (place + 1) * HEAD]
            both = jnp.concatenate(
                [jnp.where(low, state, 0.0), jnp.where(low, 0.0, state)], axis=0
            )
            blocks.append(split(both))
            norms.append(packed[2 * HEAD + place : 2 * HEAD + place + 1])
    return blocks, jnp.concatenate(norms, axis=1)


def cross_dot(x, block, dims=NN):
    return dot(x, block[0], dims) + dot(x, block[1], dims)


def gelu_parts(lifted):
    phi = 0.5 + 0.5 * lax.erf(lifted * math.sqrt(0.5))
    slope = phi + lifted * (jnp.exp(-0.5 * lifted * lifted) * (1.0 / math.sqrt(2.0 * math.pi)))
    return lifted * phi, slope


def norm_back(grad, xhat, inverse, gain):
    u = grad * gain
    mean_u = jnp.mean(u, axis=-1, keepdims=True)
    mean_ux = jnp.mean(u * xhat, axis=-1, keepdims=True)
    down = (u - mean_u - xhat * mean_ux) * inverse
    return down, jnp.sum(grad * xhat, axis=0, keepdims=True), jnp.sum(grad, axis=0, keepdims=True)


def front_body(meta, starts, hidden, gain, shift, w, b, tables, dct, outs):
    first_ref, second_ref, fq_ref, fk_ref, v_ref, eq_ref, ek_ref, keep_ref, send_ref = outs
    xhat, _ = norm_parts(hidden)
    gains, shifts = gain[...].astype(f32), shift[...].astype(f32)
    first = (xhat * gains[0:1] + shifts[0:1]).astype(bf16)
    first_ref[...] = first
    second_ref[...] = (xhat * gains[1:2] + shifts[1:2]).astype(bf16)
    bias = b[...].astype(f32)
    tabs = tuple(t[...] for t in tables)
    high, low = dct[0][...], dct[1][...]
    keys = dot(first, w[:, D : 2 * D]) + bias[1:2]
    values = (dot(first, w[:, 2 * D :]) + bias[2:3]).astype(bf16)
    v_ref[...] = values
    exp_k = featurize(keys, tabs, high, low)
    ek_ref[...] = exp_k
    feat_k = exp_k.astype(bf16)
    fk_ref[...] = feat_k
    rows = hidden.shape[0] // LEN
    wide = feat_k.astype(f32)

    def tailed(row):
        tail = masks_of(row, meta, starts)[2]
        return wide[row * LEN : (row + 1) * LEN] * jnp.concatenate([tail] * 4, axis=1)

    kept = [tailed(row) for row in range(rows)]
    halves = pack_states(
        rows,
        lambda row: kept[row].astype(bf16),
        values,
        lambda row: jnp.sum(kept[row], axis=0, keepdims=True),
    )
    store_halves(meta, keep_ref, send_ref, halves)
    queries = dot(first, w[:, :D]) + bias[0:1]
    exp_q = featurize(queries, tabs, high, low)
    eq_ref[...] = exp_q
    fq_ref[...] = exp_q.astype(bf16)


def front_kernel(meta, starts, h, gain, shift, w, b, ta, tb, tc, dh, dl, *outs):
    front_body(meta, starts, h[...].astype(f32), gain, shift, w, b, (ta, tb, tc), (dh, dl), outs)


def attend(meta, starts, num_ref, kt_ref, fq_ref, mine_ref, theirs_ref, den_ref, att_ref, low_ref):
    rows = num_ref.shape[0] // LEN
    ones = head_ones()
    for row in range(rows):
        at = slice(row * LEN, (row + 1) * LEN)
        cross = masks_of(row, meta, starts)[1]
        cross4 = jnp.concatenate([cross] * 4, axis=1)
        blocks, norm = unpack_state(meta, mine_ref, theirs_ref, row)
        fq = fq_ref[at]
        far = jnp.concatenate(
            [cross_dot(fq[:, p * 128 : (p + 1) * 128], blocks[p]) for p in range(PAIRS)], axis=1
        )
        num = num_ref[at] + cross4 * far
        den = head_sum(fq.astype(f32) * (kt_ref[at] + cross4 * norm), ones)
        att = num / den
        den_ref[at] = den
        att_ref[at] = att
        low_ref[at] = att.astype(bf16)


def middle_kernel(
    meta, starts, h, feed, num, kt, fq0, mine, theirs, ow, ob, gain, shift, w, b, ta, tb, tc, dh, dl,
    den, att, att_low, h2, *outs,
):
    attend(meta, starts, num, kt, fq0, mine, theirs, den, att, att_low)
    hidden = h[...].astype(f32) + (dot(att_low[...], ow[...]) + ob[...].astype(f32)) + feed[...]
    h2[...] = hidden
    front_body(meta, starts, hidden, gain, shift, w, b, (ta, tb, tc), (dh, dl), outs)


def attend_back(meta, starts, up, ow, den, att, fq, gnum, gden, keep_ref, send_ref):
    ga = dot(up, ow[...], NT)
    den_v = den[...]
    gn = (ga / den_v).astype(bf16)
    gnum[...] = gn
    gd = -head_sum(ga * att[...], head_ones()) / den_v
    gden[...] = gd
    rows = up.shape[0] // LEN
    wide = fq[...].astype(f32)

    def crossed(row):
        cross = masks_of(row, meta, starts)[1]
        return wide[row * LEN : (row + 1) * LEN] * jnp.concatenate([cross] * 4, axis=1)

    kept = [crossed(row) for row in range(rows)]
    halves = pack_states(
        rows,
        lambda row: kept[row].astype(bf16),
        gn,
        lambda row: jnp.sum(kept[row] * gd[row * LEN : (row + 1) * LEN], axis=0, keepdims=True),
    )
    store_halves(meta, keep_ref, send_ref, halves)


def turn_kernel(
    meta, starts, h, feed, num, kt, fq, mine, theirs, ow, ob, cot,
    den, att, att_low, result, gnum, gden, keep, send, gob,
):
    attend(meta, starts, num, kt, fq, mine, theirs, den, att, att_low)
    attend_back(meta, starts, cot[...], ow, den, att, fq, gnum, gden, keep, send)
    hidden = h[...] + (dot(att_low[...], ow[...]) + ob[...].astype(f32)) + feed[...]
    result[...] = hidden.astype(bf16)
    gob[...] = jnp.sum(cot[...].astype(f32), axis=0, keepdims=True)


def feed_kernel(second, iw, ib, dw, db, act, slope, feed):
    total = jnp.broadcast_to(db[...].astype(f32), feed.shape)
    for g in range(FF // WIDE):
        lanes = slice(g * WIDE, (g + 1) * WIDE)
        lifted = dot(second[...], iw[:, lanes]) + ib[:, lanes].astype(f32)
        value, grad = gelu_parts(lifted)
        low = value.astype(bf16)
        act[:, lanes] = low
        slope[:, lanes] = grad
        total = total + dot(low, dw[lanes, :])
    feed[...] = total


def feed_back_kernel(slope, up, iw, dw, lift, gsecond, gib):
    total = jnp.zeros(gsecond.shape, f32)
    for g in range(FF // WIDE):
        lanes = slice(g * WIDE, (g + 1) * WIDE)
        low = (dot(up[...], dw[lanes, :], NT) * slope[:, lanes]).astype(bf16)
        lift[:, lanes] = low
        gib[:, lanes] = jnp.sum(low.astype(f32), axis=0, keepdims=True)
        total = total + dot(low, iw[:, lanes], NT)
    gsecond[...] = total


def feed_both_kernel(second, iw, ib, dw, db, up, act, feed, lift, gsecond, gib):
    total = jnp.broadcast_to(db[...].astype(f32), feed.shape)
    back = jnp.zeros(gsecond.shape, f32)
    for g in range(FF // WIDE):
        lanes = slice(g * WIDE, (g + 1) * WIDE)
        lifted = dot(second[...], iw[:, lanes]) + ib[:, lanes].astype(f32)
        value, grad = gelu_parts(lifted)
        low = value.astype(bf16)
        act[:, lanes] = low
        total = total + dot(low, dw[lanes, :])
        low = (dot(up[...], dw[lanes, :], NT) * grad).astype(bf16)
        lift[:, lanes] = low
        gib[:, lanes] = jnp.sum(low.astype(f32), axis=0, keepdims=True)
        back = back + dot(low, iw[:, lanes], NT)
    feed[...] = total
    gsecond[...] = back


def intra_kernel(meta, starts, fq, fk, v, scores, num, kt):
    low = low_lanes(LEN)
    even = jnp.where(low, 1.0, 0.0).astype(bf16)
    odd = jnp.where(low, 0.0, 1.0).astype(bf16)
    for row in range(fq.shape[0] // LEN):
        at = slice(row * LEN, (row + 1) * LEN)
        intra = masks_of(row, meta, starts)[0]
        kt[at] = dot(intra.astype(bf16), fk[at])
        twice = jnp.concatenate([intra, intra], axis=0)
        for pair in range(PAIRS):
            lanes = slice(pair * 128, (pair + 1) * 128)
            q = fq[at, lanes]
            both = jnp.concatenate([q * even, q * odd], axis=0)
            rounded = (dot(both, fk[at, lanes], NT) * twice).astype(bf16)
            scores[row, pair] = rounded
            out = dot(rounded, v[at, lanes])
            num[at, lanes] = jnp.where(low, out[:LEN], out[LEN:])


def intra_back_kernel(meta, starts, fq, fk, v, scores, gnum, gden, mine, theirs, gfq, gfk, gval):
    low = low_lanes(LEN)
    even = jnp.where(low, 1.0, 0.0).astype(bf16)
    odd = jnp.where(low, 0.0, 1.0).astype(bf16)
    for row in range(fq.shape[0] // LEN):
        at = slice(row * LEN, (row + 1) * LEN)
        intra, cross, _ = masks_of(row, meta, starts)
        twice = jnp.concatenate([intra, intra], axis=0)
        blocks, norm = unpack_state(meta, mine, theirs, row)
        for pair in range(PAIRS):
            lanes = slice(pair * 128, (pair + 1) * 128)
            gn, gd, q, k = gnum[at, lanes], gden[at, lanes], fq[at, lanes], fk[at, lanes]
            both = jnp.concatenate([gn * even, gn * odd], axis=0)
            turned = pltpu.roll(gd, HEAD, 1)
            dens = jnp.concatenate(
                [jnp.where(low, gd, turned), jnp.where(low, turned, gd)], axis=0
            )
            gs = ((dot(both, v[at, lanes], NT) + dens) * twice).astype(bf16)
            near = dot(gs, k)
            far = cross_dot(gn, blocks[pair], NT) + gd * norm[:, lanes]
            gfq[at, lanes] = jnp.where(low, near[:LEN], near[LEN:]) + cross * far
            gfk[at, lanes] = jnp.where(low, dot(gs[:LEN], q, TN), dot(gs[LEN:], q, TN))
            sl = scores[row, pair]
            gval[at, lanes] = jnp.where(low, dot(sl[:LEN], gn, TN), dot(sl[LEN:], gn, TN))


def packed_back(meta, starts, mine, theirs, gfq, gfk, gval, fk, v, eq, ek, tables, dct, gp, gqb):
    tabs = tuple(t[...] for t in tables)
    high, low = dct[0][...], dct[1][...]
    for row in range(fk.shape[0] // LEN):
        at = slice(row * LEN, (row + 1) * LEN)
        tail = masks_of(row, meta, starts)[2]
        blocks, norm = unpack_state(meta, mine, theirs, row)
        keys, values = [], []
        for pair in range(PAIRS):
            lanes = slice(pair * 128, (pair + 1) * 128)
            far = cross_dot(v[at, lanes], blocks[pair], NT) + norm[:, lanes]
            keys.append(gfk[at, lanes] + tail * far)
            values.append(gval[at, lanes] + tail * cross_dot(fk[at, lanes], blocks[pair]))
        turned = tuple(t[at] for t in tabs)
        gp[at, :D] = unfeaturize(gfq[at] * eq[at], turned, high, low).astype(bf16)
        gk = jnp.concatenate(keys, axis=1)
        gp[at, D : 2 * D] = unfeaturize(gk * ek[at], turned, high, low).astype(bf16)
        gp[at, 2 * D :] = jnp.concatenate(values, axis=1).astype(bf16)
    gqb[...] = jnp.sum(gp[...].astype(f32), axis=0, keepdims=True)


def upstream_back(hidden, up, gfirst, gsecond, gain, ggain, gshift):
    xhat, inverse = norm_parts(hidden)
    gains = gain[...].astype(f32)
    one, ggain[0:1, :], gshift[0:1, :] = norm_back(gfirst, xhat, inverse, gains[0:1])
    two, ggain[1:2, :], gshift[1:2, :] = norm_back(gsecond, xhat, inverse, gains[1:2])
    return up + one + two


def turn_back_kernel(
    meta, starts, mine, theirs, gfq, gfk, gval, fk, v, eq, ek, ta, tb, tc, dh, dl, w, h, gain, gsecond, cot,
    ow, den, att, fq,
    gp, gqb, ggain, gshift, up_ref, up_low, gnum, gden, keep, send, gob,
):
    packed_back(
        meta, starts, mine, theirs, gfq, gfk, gval, fk, v, eq, ek, (ta, tb, tc), (dh, dl), gp, gqb
    )
    gfirst = dot(gp[...], w[...], NT)
    up = upstream_back(h[...], cot[...].astype(f32), gfirst, gsecond[...], gain, ggain, gshift)
    up_ref[...] = up
    low = up.astype(bf16)
    up_low[...] = low
    attend_back(meta, starts, low, ow, den, att, fq, gnum, gden, keep, send)
    gob[...] = jnp.sum(low.astype(f32), axis=0, keepdims=True)


def last_kernel(
    meta, starts, mine, theirs, gfq, gfk, gval, fk, v, eq, ek, ta, tb, tc, dh, dl, w, h, gain, gsecond, up,
    gp, gqb, ggain, gshift, ginputs,
):
    packed_back(
        meta, starts, mine, theirs, gfq, gfk, gval, fk, v, eq, ek, (ta, tb, tc), (dh, dl), gp, gqb
    )
    gfirst = dot(gp[...], w[...], NT)
    ginputs[...] = upstream_back(
        h[...].astype(f32), up[...], gfirst, gsecond[...], gain, ggain, gshift
    )


def reversed_bits(value, count):
    return sum(((value >> k) & 1) << (count - 1 - k) for k in range(count))


def gathered(size, meta, x, flat, held):
    count = size.bit_length() - 1
    block = flat.shape[0] // size
    flat[...] = x.astype(f32).T
    for place in range(size):
        source = reversed_bits(place, count) ^ meta[2]
        held[place * block : (place + 1) * block, :] = flat[
            pl.ds(pl.multiple_of(source * block, block), block), :
        ]
    return held[...].astype(bf16)


def feed_grad_kernel(size, meta, second, act, lift, up, in_keep, in_send, down_keep, down_send, f1, h1, f2, h2):
    left = gathered(size, meta, second[...], f1, h1)
    for k in range(2):
        for g in range(2):
            at = pl.multiple_of((k ^ meta[3]) * (FF // 2) + g * WIDE, WIDE)
            out = dot(left, lift[:, pl.ds(at, WIDE)])
            in_keep[k, :, g * WIDE : (g + 1) * WIDE] = out[: D // 2]
            in_send[k, :, g * WIDE : (g + 1) * WIDE] = out[D // 2 :]
    left = gathered(size, meta, act[...], f2, h2)
    for k in range(2):
        right = up[:, pl.ds(pl.multiple_of((k ^ meta[4]) * (D // 2), D // 2), D // 2)]
        for g in range(4):
            out = dot(left[g * WIDE : (g + 1) * WIDE], right)
            ref = (down_keep, down_send)[g // 2]
            ref[k, (g % 2) * WIDE : (g % 2 + 1) * WIDE, :] = out


def packed_grad_kernel(size, meta, first, att_low, gp, up, a_keep, a_send, b_keep, b_send, f1, h1):
    for source, wide, begin in ((first, 384, 0), (att_low, 128, 384)):
        left = gathered(size, meta, source[...], f1, h1)
        right = gp if wide == 384 else up
        for part, (keep, send) in enumerate(((a_keep, a_send), (b_keep, b_send))):
            for k in range(2):
                at = pl.multiple_of((2 * part + (k ^ meta[3 + part])) * wide, wide)
                out = dot(left, right[:, pl.ds(at, wide)])
                keep[k, :, begin : begin + wide] = out[: D // 2]
                send[k, :, begin : begin + wide] = out[D // 2 :]


class Layer:
    def __init__(self, array, index):
        self.array, self.index = array, index


class Scalars:
    def __init__(self, array):
        self.array = array


def call(kernel, name, operands, outs, flops, scratch=()):
    specs, arrays = [], []
    for operand in operands:
        if isinstance(operand, Scalars):
            specs.append(pl.BlockSpec(memory_space=pltpu.SMEM))
            arrays.append(operand.array)
        elif isinstance(operand, Layer):
            array, index = operand.array, operand.index
            rest = array.shape[1:]
            specs.append(
                pl.BlockSpec(
                    (None,) + rest, lambda i, n=len(rest), index=index: (index,) + (0,) * n
                )
            )
            arrays.append(array)
        else:
            specs.append(pl.BlockSpec(operand.shape, lambda i, n=operand.ndim: (0,) * n))
            arrays.append(operand)
    moved = sum(a.size * a.dtype.itemsize for a in arrays)
    moved += sum(math.prod(o.shape) * o.dtype.itemsize for o in outs)
    return pl.pallas_call(
        kernel,
        name=name,
        grid=(1,),
        in_specs=specs,
        out_specs=[pl.BlockSpec(o.shape, lambda i, n=len(o.shape): (0,) * n) for o in outs],
        out_shape=list(outs),
        scratch_shapes=list(scratch),
        cost_estimate=pl.CostEstimate(flops=int(flops), bytes_accessed=moved, transcendentals=0),
        compiler_params=pltpu.CompilerParams(vmem_limit_bytes=40 * 1024 * 1024),
    )(*arrays)


def cosine_table():
    frequency = np.arange(HEAD, dtype=np.float64)[:, None]
    columns = np.arange(HEAD, dtype=np.float64)[None, :]
    entries = np.cos(math.pi * (2.0 * columns + 1.0) * frequency / (2.0 * HEAD))
    entries = entries * math.sqrt(2.0 / HEAD)
    entries[0] *= math.sqrt(0.5)
    wide = np.kron(np.eye(4), entries.T)
    high = wide.astype(np.float32).astype(bf16)
    low = (wide.astype(np.float32) - high.astype(np.float32)).astype(bf16)
    return jnp.asarray(high), jnp.asarray(low)


def rotary_tables(places):
    lane = jnp.arange(128) % HEAD
    half = ROT // 2
    inverse = 10000.0 ** (-((lane % half).astype(f32) * 2.0 / ROT))
    inverse = jnp.where(lane < ROT, inverse, 0.0)
    angles = places.astype(f32)[:, None] * inverse[None, :]
    sine = jnp.sin(angles)
    ahead = jnp.where(lane < half, -sine, 0.0)
    behind = jnp.where((lane >= half) & (lane < ROT), sine, 0.0)
    return jnp.cos(angles), ahead, behind


def flip(value, axis, bit):
    size = lax.axis_size(axis)
    return lax.ppermute(value, axis, [(i, i ^ bit) for i in range(size)])


def chips_on(value, step):
    size = lax.axis_size("seq")
    pairs = [(i, i + 2 * step) for i in range(size) if 0 <= i + 2 * step < size]
    return lax.ppermute(value, "seq", pairs)


def exchange(keep, send, flag, core, chip, backward):
    chips = lax.axis_size("seq") // 2
    begin, span = chip * 2 * LEN, 2 * LEN
    got = flip(send, "seq", 1)
    even, odd = jnp.where(core == 0, keep, got), jnp.where(core == 0, got, keep)
    sign = -1 if backward else 1
    if backward:
        whole = even + flag(begin + LEN - 1, begin) * odd
    else:
        whole = odd + flag(begin + span - 1, begin + LEN) * even
    entered = chips_on(whole, sign)
    step = 2
    while step < chips:
        partial = whole + flag(begin + span - 1, begin) * entered
        more = chips_on(partial, sign * step)
        if backward:
            entered = entered + flag(begin + span * step - 1, begin + span) * more
        else:
            entered = entered + flag(begin - 1, begin - span * (step - 1)) * more
        step *= 2
    if backward:
        for_even, for_odd = odd + flag(begin + span - 1, begin + LEN) * entered, entered
    else:
        for_even, for_odd = entered, even + flag(begin + LEN - 1, begin) * entered
    mine = jnp.where(core == 0, for_even, for_odd)
    theirs = flip(jnp.where(core == 0, for_odd, for_even), "seq", 1)
    return mine, theirs


def reduce_chunk(keep, send, bit):
    size = lax.axis_size("seq")
    got = flip(send, "seq", 1)
    got_first = flip(keep[1] + got[1], "batch", bit)
    total = keep[0] + got[0] + got_first
    step = 2
    while step < size:
        half = total.shape[0] // 2
        total = total[:half] + flip(total[half:], "seq", step)
        step *= 2
    total = total + flip(total, "batch", 3 - bit)
    return total, flip(total, "batch", bit)


def per_device(
    inputs,
    doc_starts,
    cotangent,
    norm_gain,
    norm_bias,
    qkv_weight,
    qkv_bias,
    out_weight,
    out_bias,
    in_weight,
    in_bias,
    down_weight,
    down_bias,
):
    rows, length = inputs.shape[0], inputs.shape[1]
    tokens = rows * length
    size = lax.axis_size("seq")
    me, column = lax.axis_index("seq"), lax.axis_index("batch")
    core, chip = me % 2, me // 2
    bits = (column % 2, column // 2)
    begin = me * length
    absolute = begin + jnp.arange(length, dtype=jnp.int32)

    def segment_at(position):
        return jnp.max(jnp.where(doc_starts <= position, doc_starts, 0), axis=1)

    def flag(position, limit):
        return (segment_at(position) < limit).astype(f32)[:, None, None]

    segment = jnp.max(
        jnp.where(doc_starts[:, None, :] <= absolute[None, :, None], doc_starts[:, None, :], 0),
        axis=2,
    )
    tables = rotary_tables((absolute[None, :] - segment).reshape(tokens))
    dct = cosine_table()
    meta = Scalars(jnp.stack([begin, core, me, bits[0], bits[1]]).astype(jnp.int32))
    starts = Scalars(doc_starts)
    hidden0 = inputs.reshape(tokens, D)
    cot = cotangent.reshape(tokens, D)
    out_bias2, in_bias2, down_bias2 = (
        out_bias[:, None, :],
        in_bias[:, None, :],
        down_bias[:, None, :],
    )

    tall, fat = sds((tokens, D)), sds((tokens, D), bf16)
    packed_state = sds((rows, PACK, 128))
    front_outs = [fat, fat, fat, fat, fat, tall, tall, packed_state, packed_state]
    matmul = 2.0 * tokens * D * D

    def front_of(layer):
        return [
            Layer(norm_gain, layer),
            Layer(norm_bias, layer),
            Layer(qkv_weight, layer),
            Layer(qkv_bias, layer),
            *tables,
            *dct,
        ]

    first, second, fq, fk, v, eq, ek, keep, send = call(
        front_kernel, "front", [meta, starts, hidden0, *front_of(0)], front_outs, 6 * matmul
    )
    entered0 = exchange(keep, send, flag, core, chip, False)
    feed_weights = [
        [Layer(x, layer) for x in (in_weight, in_bias2, down_weight, down_bias2)]
        for layer in range(2)
    ]
    act0, slope0, feed0 = call(
        feed_kernel,
        "feed",
        [second, *feed_weights[0]],
        [sds((tokens, FF), bf16), sds((tokens, FF)), tall],
        8 * matmul,
    )
    intra_outs = [sds((rows, PAIRS, 2 * LEN, LEN), bf16), tall, tall]
    scores0, num0, kt0 = call(
        intra_kernel, "intra", [meta, starts, fq, fk, v], intra_outs, 2 * matmul
    )
    first0, second0, fq0, fk0, v0, eq0, ek0 = first, second, fq, fk, v, eq, ek
    den0, att0, att_low0, hidden1, first1, second1, fq1, fk1, v1, eq1, ek1, keep, send = call(
        middle_kernel,
        "middle",
        [meta, starts, hidden0, feed0, num0, kt0, fq0, *entered0]
        + [Layer(out_weight, 0), Layer(out_bias2, 0), *front_of(1)],
        [tall, tall, fat, tall] + front_outs,
        8 * matmul,
    )
    entered1 = exchange(keep, send, flag, core, chip, False)
    act1, feed1, lift1, gsecond1, gib1 = call(
        feed_both_kernel,
        "feed_both",
        [second1, *feed_weights[1], cot],
        [sds((tokens, FF), bf16), tall, sds((tokens, FF), bf16), tall, sds((1, FF))],
        16 * matmul,
    )
    scores1, num1, kt1 = call(
        intra_kernel, "intra", [meta, starts, fq1, fk1, v1], intra_outs, 2 * matmul
    )

    def feed_grad(second, act, lift, up):
        wide, narrow = sds((2, D // 2, FF // 2)), sds((2, FF // 2, D // 2))
        flat = [pltpu.VMEM((D, tokens), f32)] * 2 + [pltpu.VMEM((FF, tokens), f32)] * 2
        a_keep, a_send, b_keep, b_send = call(
            functools.partial(feed_grad_kernel, size),
            "feed_grad",
            [meta, second, act, lift, up],
            [wide, wide, narrow, narrow],
            8 * matmul,
            flat,
        )
        return reduce_chunk(a_keep, a_send, 1), reduce_chunk(b_keep, b_send, 2)

    chunk_feed1 = feed_grad(second1, act1, lift1, cot)
    den1, att1, att_low1, result, gnum1, gden1, keep, send, gob1 = call(
        turn_kernel,
        "turn",
        [meta, starts, hidden1, feed1, num1, kt1, fq1, *entered1]
        + [Layer(out_weight, 1), Layer(out_bias2, 1), cot],
        [tall, tall, fat, fat, fat, tall, packed_state, packed_state, sds((1, D))],
        3 * matmul,
    )
    later1 = exchange(keep, send, flag, core, chip, True)
    gfq1, gfk1, gval1 = call(
        intra_back_kernel,
        "intra_back",
        [meta, starts, fq1, fk1, v1, scores1, gnum1, gden1, *entered1],
        [tall, tall, tall],
        4 * matmul,
    )
    vector_outs = [sds((1, 3 * D)), sds((2, D)), sds((2, D))]
    packed = sds((tokens, 3 * D), bf16)
    gp1, gqb1, ggain1, gshift1, up0, up_low0, gnum0, gden0, keep, send, gob0 = call(
        turn_back_kernel,
        "turn_back",
        [meta, starts, *later1, gfq1, gfk1, gval1, fk1, v1, eq1, ek1, *tables, *dct]
        + [Layer(qkv_weight, 1), hidden1, Layer(norm_gain, 1), gsecond1, cot]
        + [Layer(out_weight, 0), den0, att0, fq0],
        [packed, *vector_outs, tall, fat, fat, tall, packed_state, packed_state, sds((1, D))],
        8 * matmul,
    )
    later0 = exchange(keep, send, flag, core, chip, True)
    lift0, gsecond0, gib0 = call(
        feed_back_kernel,
        "feed_back",
        [slope0, up_low0, Layer(in_weight, 0), Layer(down_weight, 0)],
        [sds((tokens, FF), bf16), tall, sds((1, FF))],
        8 * matmul,
    )
    gfq0, gfk0, gval0 = call(
        intra_back_kernel,
        "intra_back",
        [meta, starts, fq0, fk0, v0, scores0, gnum0, gden0, *entered0],
        [tall, tall, tall],
        4 * matmul,
    )

    def packed_grad(first, att_low, gp, up):
        quarter = sds((2, D // 2, D))
        flat = [pltpu.VMEM((D, tokens), f32)] * 2
        return call(
            functools.partial(packed_grad_kernel, size),
            "packed_grad",
            [meta, first, att_low, gp, up],
            [quarter] * 4,
            4 * matmul,
            flat,
        )

    a_keep, a_send, b_keep, b_send = packed_grad(first1, att_low1, gp1, cot)
    chunk_packed1 = reduce_chunk(a_keep, a_send, 1), reduce_chunk(b_keep, b_send, 2)
    chunk_feed0 = feed_grad(second0, act0, lift0, up_low0)
    gp0, gqb0, ggain0, gshift0, ginputs = call(
        last_kernel,
        "last",
        [meta, starts, *later0, gfq0, gfk0, gval0, fk0, v0, eq0, ek0, *tables, *dct]
        + [Layer(qkv_weight, 0), hidden0, Layer(norm_gain, 0), gsecond0, up0],
        [packed, *vector_outs, tall],
        6 * matmul,
    )
    a_keep, a_send, b_keep, b_send = packed_grad(first0, att_low0, gp0, up_low0)

    slot = D // size
    vectors = jnp.concatenate(
        [
            part.reshape(-1, size, slot)
            if part.shape[-1] != FF
            else part.reshape(size, FF // D, slot).swapaxes(0, 1)
            for layer in (
                (ggain0, gshift0, gqb0.reshape(3, D), gob0, gib0),
                (ggain1, gshift1, gqb1.reshape(3, D), gob1, gib1),
            )
            for part in layer
        ],
        axis=0,
    ).swapaxes(0, 1)
    count = size.bit_length() - 1
    order = np.array([reversed_bits(k, count) for k in range(size)], np.int32) ^ me
    vectors = jnp.take(vectors, order, axis=0).reshape(size, 2, -1)
    vectors = jnp.where(bits[0] == 0, vectors, vectors[:, ::-1]).swapaxes(0, 1)
    held = vectors.shape[2]
    under = -(-held // (8 * D)) * 8
    vectors = jnp.pad(vectors, ((0, 0), (0, 0), (0, under * D - held)))
    vectors = vectors.reshape(2, size, under, D)

    def with_vectors(part, lines):
        part = part.reshape(2, size // 2, slot, D)
        return jnp.concatenate([part, lines], axis=2).reshape(2, -1, D)

    a_keep = with_vectors(a_keep, vectors[:, : size // 2])
    a_send = with_vectors(a_send, vectors[:, size // 2 :])
    own, other = reduce_chunk(a_keep, a_send, 1)
    chunk_packed0 = (own[:slot], other[:slot]), reduce_chunk(b_keep, b_send, 2)
    lines = [part[slot:].reshape(-1)[:held] for part in (own, other)]
    summed = jnp.where(
        bits[0] == 0, jnp.concatenate(lines), jnp.concatenate(lines[::-1])
    ).reshape(2, 12, slot)

    def joined(chunk, bit):
        own, other = chunk
        return jnp.where(
            bit == 0,
            jnp.concatenate([own, other], axis=-1),
            jnp.concatenate([other, own], axis=-1),
        )

    def of_layers(make):
        return jnp.stack([make(0), make(1)])

    chunks_feed, chunks_packed = (chunk_feed0, chunk_feed1), (chunk_packed0, chunk_packed1)

    def columns(layer, begin, wide):
        pieces = []
        for part in range(2):
            own, other = chunks_packed[layer][part]
            pieces.append(
                joined((own[:, begin : begin + wide], other[:, begin : begin + wide]), bits[part])
            )
        return jnp.concatenate(pieces, axis=-1)

    grad_gain, grad_shift = summed[:, 0:2], summed[:, 2:4]
    grad_qkv_b, grad_out_b = summed[:, 4:7], summed[:, 7]
    grad_in_b = summed[:, 8:12].reshape(2, FF // size)
    return (
        result.reshape(rows, length, D),
        ginputs.reshape(rows, length, D),
        grad_gain,
        grad_shift,
        of_layers(lambda layer: columns(layer, 0, 384)),
        grad_qkv_b,
        of_layers(lambda layer: columns(layer, 384, 128)),
        grad_out_b,
        of_layers(lambda layer: joined(chunks_feed[layer][0], bits[0])),
        grad_in_b,
        of_layers(lambda layer: joined(chunks_feed[layer][1], bits[1])),
        grad_out_b,
    )


def solution(mesh):
    placed = (
        P("batch", "seq", None),
        P("batch", None),
        P("batch", "seq", None),
        P(),
        P(),
        P(),
        P(),
        P(),
        P(),
        P(),
        P(),
        P(),
        P(),
    )
    return jax.shard_map(
        per_device,
        mesh=mesh,
        in_specs=placed,
        out_specs=(
            P("batch", "seq", None),
            P("batch", "seq", None),
            P(None, None, "seq"),
            P(None, None, "seq"),
            P(None, "seq", None),
            P(None, None, "seq"),
            P(None, "seq", None),
            P(None, "seq"),
            P(None, "seq", None),
            P(None, "seq"),
            P(None, "seq", None),
            P(None, "seq"),
        ),
        check_vma=False,
    )
```

```python
import functools
import math

import jax
import jax.numpy as jnp
import numpy as np
from jax import lax
from jax.experimental import pallas as pl
from jax.experimental.pallas import tpu as pltpu
from jax.sharding import PartitionSpec as P

D = 512
HEADS = 8
HEAD = 64
FF = 2048
ROT = 16
LAYERS = 2
NDOC = 4
LEN = 128
PAIRS = HEADS // 2
PACK = 2 * HEAD + 8
WIDE = 512

epsilon = 1e-05
f32, bf16 = jnp.float32, jnp.bfloat16
NN = (((1,), (0,)), ((), ()))
NT = (((1,), (1,)), ((), ()))
TN = (((0,), (0,)), ((), ()))


def dot(a, b, dims=NN):
    return lax.dot_general(a, b, dims, preferred_element_type=f32)


def split(x):
    high = x.astype(bf16)
    return high, (x - high.astype(f32)).astype(bf16)


def sds(shape, dtype=f32):
    return jax.ShapeDtypeStruct(shape, dtype)


def norm_parts(hidden):
    centred = hidden - jnp.mean(hidden, axis=-1, keepdims=True)
    variance = jnp.mean(centred * centred, axis=-1, keepdims=True)
    inverse = lax.rsqrt(variance + epsilon)
    return centred * inverse, inverse


def segment_of(position, starts, row):
    found = jnp.zeros_like(position)
    for k in range(NDOC):
        entry = starts[row, k]
        found = jnp.maximum(found, jnp.where(entry <= position, entry, 0))
    return found


def masks_of(row, meta, starts):
    begin = meta[0]
    at_i = begin + lax.broadcasted_iota(jnp.int32, (LEN, 128), 0)
    at_j = begin + lax.broadcasted_iota(jnp.int32, (LEN, 128), 1)
    seg_i, seg_j = segment_of(at_i, starts, row), segment_of(at_j, starts, row)
    last = jnp.int32(0)
    for k in range(NDOC):
        entry = starts[row, k]
        last = jnp.maximum(last, jnp.where(entry <= begin + (LEN - 1), entry, 0))
    intra = jnp.where((at_j <= at_i) & (seg_i == seg_j), 1.0, 0.0).astype(f32)
    cross = jnp.where(seg_i < begin, 1.0, 0.0).astype(f32)
    tail = jnp.where(seg_i == last, 1.0, 0.0).astype(f32)
    return intra, cross, tail


def low_lanes(rows):
    return lax.broadcasted_iota(jnp.int32, (rows, 128), 1) < HEAD


def rotate(x, tables):
    base, ahead, behind = tables
    return x * base + pltpu.roll(x, 120, 1) * ahead + pltpu.roll(x, 8, 1) * behind


def rotate_back(g, tables):
    base, ahead, behind = tables
    return g * base + pltpu.roll(g * ahead, 8, 1) + pltpu.roll(g * behind, 120, 1)


def featurize(x, tables, high, low):
    pieces = [rotate(x[:, g * 128 : (g + 1) * 128], tables) for g in range(4)]
    found = []
    for g in range(2):
        a, b = split(jnp.concatenate(pieces[2 * g : 2 * g + 2], axis=1))
        found.append(jnp.exp(dot(a, high) + dot(b, high) + dot(a, low)))
    return jnp.concatenate(found, axis=1)


def unfeaturize(g, tables, high, low):
    found = []
    for k in range(2):
        a, b = split(g[:, k * 256 : (k + 1) * 256])
        back = dot(a, high, NT) + dot(b, high, NT) + dot(a, low, NT)
        found += [rotate_back(back[:, :128], tables), rotate_back(back[:, 128:], tables)]
    return jnp.concatenate(found, axis=1)


def head_ones():
    across = lax.broadcasted_iota(jnp.int32, (256, 256), 0) // HEAD
    along = lax.broadcasted_iota(jnp.int32, (256, 256), 1) // HEAD
    return jnp.where(across == along, 1.0, 0.0).astype(bf16)


def head_sum(x, ones):
    found = []
    for g in range(2):
        a, b = split(x[:, g * 256 : (g + 1) * 256])
        found.append(dot(a, ones) + dot(b, ones))
    return jnp.concatenate(found, axis=1)


def store_halves(meta, keep_ref, send_ref, halves):
    def put(ref, half):
        for row, at, value in halves[half]:
            ref[row, at[0] : at[1], :] = value

    core = meta[1]
    for mine in range(2):

        @pl.when(core == mine)
        def _():
            put(keep_ref, mine)
            put(send_ref, 1 - mine)


def pack_states(rows, left_of, right, norm_of):
    low = low_lanes(HEAD)
    halves = [[], []]
    for row in range(rows):
        at = slice(row * LEN, (row + 1) * LEN)
        left, norm = left_of(row), norm_of(row)
        for pair in range(PAIRS):
            lanes = slice(pair * 128, (pair + 1) * 128)
            both = dot(left[:, lanes], right[at, lanes], TN)
            half, place = pair // 2, pair % 2
            halves[half].append(
                (row, (place * HEAD, (place + 1) * HEAD), jnp.where(low, both[:HEAD], both[HEAD:]))
            )
        for half in range(2):
            pieces = [norm[:, (2 * half + k) * 128 : (2 * half + k + 1) * 128] for k in range(2)]
            block = jnp.concatenate(pieces + [jnp.zeros((6, 128), f32)], axis=0)
            halves[half].append((row, (2 * HEAD, PACK), block))
    return halves


def unpack_state(meta, mine_ref, theirs_ref, row):
    low = low_lanes(HEAD)
    blocks, norms = [], []
    for half in range(2):
        packed = jnp.where(meta[1] == half, mine_ref[row], theirs_ref[row])
        for place in range(2):
            state = packed[place * HEAD : (place + 1) * HEAD]
            both = jnp.concatenate(
                [jnp.where(low, state, 0.0), jnp.where(low, 0.0, state)], axis=0
            )
            blocks.append(split(both))
            norms.append(packed[2 * HEAD + place : 2 * HEAD + place + 1])
    return blocks, jnp.concatenate(norms, axis=1)


def cross_dot(x, block, dims=NN):
    return dot(x, block[0], dims) + dot(x, block[1], dims)


def gelu_parts(lifted):
    phi = 0.5 + 0.5 * lax.erf(lifted * math.sqrt(0.5))
    slope = phi + lifted * (jnp.exp(-0.5 * lifted * lifted) * (1.0 / math.sqrt(2.0 * math.pi)))
    return lifted * phi, slope


def norm_back(grad, xhat, inverse, gain):
    u = grad * gain
    mean_u = jnp.mean(u, axis=-1, keepdims=True)
    mean_ux = jnp.mean(u * xhat, axis=-1, keepdims=True)
    down = (u - mean_u - xhat * mean_ux) * inverse
    return down, jnp.sum(grad * xhat, axis=0, keepdims=True), jnp.sum(grad, axis=0, keepdims=True)


def front_body(meta, starts, hidden, gain, shift, w, b, tables, dct, outs):
    first_ref, second_ref, fq_ref, fk_ref, v_ref, eq_ref, ek_ref, keep_ref, send_ref, *_ = outs
    xhat, _ = norm_parts(hidden)
    gains, shifts = gain[...].astype(f32), shift[...].astype(f32)
    first = (xhat * gains[0:1] + shifts[0:1]).astype(bf16)
    first_ref[...] = first
    second_ref[...] = (xhat * gains[1:2] + shifts[1:2]).astype(bf16)
    bias = b[...].astype(f32)
    tabs = tuple(t[...] for t in tables)
    high, low = dct[0][...], dct[1][...]
    keys = dot(first, w[:, D : 2 * D]) + bias[1:2]
    values = (dot(first, w[:, 2 * D :]) + bias[2:3]).astype(bf16)
    v_ref[...] = values
    exp_k = featurize(keys, tabs, high, low)
    ek_ref[...] = exp_k
    feat_k = exp_k.astype(bf16)
    fk_ref[...] = feat_k
    rows = hidden.shape[0] // LEN
    wide = feat_k.astype(f32)

    def tailed(row):
        tail = masks_of(row, meta, starts)[2]
        return wide[row * LEN : (row + 1) * LEN] * jnp.concatenate([tail] * 4, axis=1)

    kept = [tailed(row) for row in range(rows)]
    halves = pack_states(
        rows,
        lambda row: kept[row].astype(bf16),
        values,
        lambda row: jnp.sum(kept[row], axis=0, keepdims=True),
    )
    store_halves(meta, keep_ref, send_ref, halves)
    queries = dot(first, w[:, :D]) + bias[0:1]
    exp_q = featurize(queries, tabs, high, low)
    eq_ref[...] = exp_q
    fq_ref[...] = exp_q.astype(bf16)


def front_kernel(meta, starts, h, cot, gain, shift, w, b, ta, tb, tc, dh, dl, *outs):
    front_body(meta, starts, h[...].astype(f32), gain, shift, w, b, (ta, tb, tc), (dh, dl), outs)
    early = outs[9]
    early[0] = outs[1][...].astype(f32)
    early[1] = cot[...].astype(f32)


def attend(meta, starts, num_ref, kt_ref, fq_ref, mine_ref, theirs_ref, den_ref, att_ref, low_ref):
    rows = num_ref.shape[0] // LEN
    ones = head_ones()
    for row in range(rows):
        at = slice(row * LEN, (row + 1) * LEN)
        cross = masks_of(row, meta, starts)[1]
        cross4 = jnp.concatenate([cross] * 4, axis=1)
        blocks, norm = unpack_state(meta, mine_ref, theirs_ref, row)
        fq = fq_ref[at]
        far = jnp.concatenate(
            [cross_dot(fq[:, p * 128 : (p + 1) * 128], blocks[p]) for p in range(PAIRS)], axis=1
        )
        num = num_ref[at] + cross4 * far
        den = head_sum(fq.astype(f32) * (kt_ref[at] + cross4 * norm), ones)
        att = num / den
        den_ref[at] = den
        att_ref[at] = att
        low_ref[at] = att.astype(bf16)


def middle_kernel(
    meta, starts, h, feed, num, kt, fq0, mine, theirs, ow, ob, gain, shift, w, b, ta, tb, tc, dh, dl,
    den, att, att_low, h2, *outs,
):
    attend(meta, starts, num, kt, fq0, mine, theirs, den, att, att_low)
    hidden = h[...].astype(f32) + (dot(att_low[...], ow[...]) + ob[...].astype(f32)) + feed[...]
    h2[...] = hidden
    front_body(meta, starts, hidden, gain, shift, w, b, (ta, tb, tc), (dh, dl), outs)
    store_rows(outs[1], outs[9:])


def store_rows(x, refs):
    for row, ref in enumerate(refs):
        ref[...] = x[row * LEN : (row + 1) * LEN].astype(f32)


def attend_back(meta, starts, up, ow, den, att, fq, gnum, gden, keep_ref, send_ref):
    ga = dot(up, ow[...], NT)
    den_v = den[...]
    gn = (ga / den_v).astype(bf16)
    gnum[...] = gn
    gd = -head_sum(ga * att[...], head_ones()) / den_v
    gden[...] = gd
    rows = up.shape[0] // LEN
    wide = fq[...].astype(f32)

    def crossed(row):
        cross = masks_of(row, meta, starts)[1]
        return wide[row * LEN : (row + 1) * LEN] * jnp.concatenate([cross] * 4, axis=1)

    kept = [crossed(row) for row in range(rows)]
    halves = pack_states(
        rows,
        lambda row: kept[row].astype(bf16),
        gn,
        lambda row: jnp.sum(kept[row] * gd[row * LEN : (row + 1) * LEN], axis=0, keepdims=True),
    )
    store_halves(meta, keep_ref, send_ref, halves)


def turn_kernel(
    meta, starts, h, feed, num, kt, fq, mine, theirs, ow, ob, cot,
    den, att, att_low, result, gnum, gden, keep, send, gob,
):
    attend(meta, starts, num, kt, fq, mine, theirs, den, att, att_low)
    attend_back(meta, starts, cot[...], ow, den, att, fq, gnum, gden, keep, send)
    hidden = h[...] + (dot(att_low[...], ow[...]) + ob[...].astype(f32)) + feed[...]
    result[...] = hidden.astype(bf16)
    gob[...] = jnp.sum(cot[...].astype(f32), axis=0, keepdims=True)


def feed_kernel(second, iw, ib, dw, db, act, slope, feed):
    total = jnp.broadcast_to(db[...].astype(f32), feed.shape)
    for g in range(FF // WIDE):
        lanes = slice(g * WIDE, (g + 1) * WIDE)
        lifted = dot(second[...], iw[:, lanes]) + ib[:, lanes].astype(f32)
        value, grad = gelu_parts(lifted)
        low = value.astype(bf16)
        act[:, lanes] = low
        slope[:, lanes] = grad
        total = total + dot(low, dw[lanes, :])
    feed[...] = total


def feed_back_kernel(slope, up, iw, dw, lift, gsecond, gib):
    total = jnp.zeros(gsecond.shape, f32)
    for g in range(FF // WIDE):
        lanes = slice(g * WIDE, (g + 1) * WIDE)
        low = (dot(up[...], dw[lanes, :], NT) * slope[:, lanes]).astype(bf16)
        lift[:, lanes] = low
        gib[:, lanes] = jnp.sum(low.astype(f32), axis=0, keepdims=True)
        total = total + dot(low, iw[:, lanes], NT)
    gsecond[...] = total


def feed_both_kernel(second, iw, ib, dw, db, up, act, feed, lift, gsecond, gib):
    total = jnp.broadcast_to(db[...].astype(f32), feed.shape)
    back = jnp.zeros(gsecond.shape, f32)
    for g in range(FF // WIDE):
        lanes = slice(g * WIDE, (g + 1) * WIDE)
        lifted = dot(second[...], iw[:, lanes]) + ib[:, lanes].astype(f32)
        value, grad = gelu_parts(lifted)
        low = value.astype(bf16)
        act[:, lanes] = low
        total = total + dot(low, dw[lanes, :])
        low = (dot(up[...], dw[lanes, :], NT) * grad).astype(bf16)
        lift[:, lanes] = low
        gib[:, lanes] = jnp.sum(low.astype(f32), axis=0, keepdims=True)
        back = back + dot(low, iw[:, lanes], NT)
    feed[...] = total
    gsecond[...] = back


def intra_kernel(meta, starts, fq, fk, v, scores, num, kt):
    low = low_lanes(LEN)
    even = jnp.where(low, 1.0, 0.0).astype(bf16)
    odd = jnp.where(low, 0.0, 1.0).astype(bf16)
    for row in range(fq.shape[0] // LEN):
        at = slice(row * LEN, (row + 1) * LEN)
        intra = masks_of(row, meta, starts)[0]
        kt[at] = dot(intra.astype(bf16), fk[at])
        twice = jnp.concatenate([intra, intra], axis=0)
        for pair in range(PAIRS):
            lanes = slice(pair * 128, (pair + 1) * 128)
            q = fq[at, lanes]
            both = jnp.concatenate([q * even, q * odd], axis=0)
            rounded = (dot(both, fk[at, lanes], NT) * twice).astype(bf16)
            scores[row, pair] = rounded
            out = dot(rounded, v[at, lanes])
            num[at, lanes] = jnp.where(low, out[:LEN], out[LEN:])


def intra_back_kernel(meta, starts, fq, fk, v, scores, gnum, gden, mine, theirs, gfq, gfk, gval):
    low = low_lanes(LEN)
    even = jnp.where(low, 1.0, 0.0).astype(bf16)
    odd = jnp.where(low, 0.0, 1.0).astype(bf16)
    for row in range(fq.shape[0] // LEN):
        at = slice(row * LEN, (row + 1) * LEN)
        intra, cross, _ = masks_of(row, meta, starts)
        twice = jnp.concatenate([intra, intra], axis=0)
        blocks, norm = unpack_state(meta, mine, theirs, row)
        for pair in range(PAIRS):
            lanes = slice(pair * 128, (pair + 1) * 128)
            gn, gd, q, k = gnum[at, lanes], gden[at, lanes], fq[at, lanes], fk[at, lanes]
            both = jnp.concatenate([gn * even, gn * odd], axis=0)
            turned = pltpu.roll(gd, HEAD, 1)
            dens = jnp.concatenate(
                [jnp.where(low, gd, turned), jnp.where(low, turned, gd)], axis=0
            )
            gs = ((dot(both, v[at, lanes], NT) + dens) * twice).astype(bf16)
            near = dot(gs, k)
            far = cross_dot(gn, blocks[pair], NT) + gd * norm[:, lanes]
            gfq[at, lanes] = jnp.where(low, near[:LEN], near[LEN:]) + cross * far
            gfk[at, lanes] = jnp.where(low, dot(gs[:LEN], q, TN), dot(gs[LEN:], q, TN))
            sl = scores[row, pair]
            gval[at, lanes] = jnp.where(low, dot(sl[:LEN], gn, TN), dot(sl[LEN:], gn, TN))


def packed_back(meta, starts, mine, theirs, gfq, gfk, gval, fk, v, eq, ek, tables, dct, gp, gqb):
    tabs = tuple(t[...] for t in tables)
    high, low = dct[0][...], dct[1][...]
    for row in range(fk.shape[0] // LEN):
        at = slice(row * LEN, (row + 1) * LEN)
        tail = masks_of(row, meta, starts)[2]
        blocks, norm = unpack_state(meta, mine, theirs, row)
        keys, values = [], []
        for pair in range(PAIRS):
            lanes = slice(pair * 128, (pair + 1) * 128)
            far = cross_dot(v[at, lanes], blocks[pair], NT) + norm[:, lanes]
            keys.append(gfk[at, lanes] + tail * far)
            values.append(gval[at, lanes] + tail * cross_dot(fk[at, lanes], blocks[pair]))
        turned = tuple(t[at] for t in tabs)
        gp[at, :D] = unfeaturize(gfq[at] * eq[at], turned, high, low).astype(bf16)
        gk = jnp.concatenate(keys, axis=1)
        gp[at, D : 2 * D] = unfeaturize(gk * ek[at], turned, high, low).astype(bf16)
        gp[at, 2 * D :] = jnp.concatenate(values, axis=1).astype(bf16)
    gqb[...] = jnp.sum(gp[...].astype(f32), axis=0, keepdims=True)


def upstream_back(hidden, up, gfirst, gsecond, gain, ggain, gshift):
    xhat, inverse = norm_parts(hidden)
    gains = gain[...].astype(f32)
    one, ggain[0:1, :], gshift[0:1, :] = norm_back(gfirst, xhat, inverse, gains[0:1])
    two, ggain[1:2, :], gshift[1:2, :] = norm_back(gsecond, xhat, inverse, gains[1:2])
    return up + one + two


def turn_back_kernel(
    meta, starts, mine, theirs, gfq, gfk, gval, fk, v, eq, ek, ta, tb, tc, dh, dl, w, h, gain, gsecond, cot,
    ow, den, att, fq,
    gp, gqb, ggain, gshift, up_ref, up_low, gnum, gden, keep, send, gob, *up_rows,
):
    packed_back(
        meta, starts, mine, theirs, gfq, gfk, gval, fk, v, eq, ek, (ta, tb, tc), (dh, dl), gp, gqb
    )
    gfirst = dot(gp[...], w[...], NT)
    up = upstream_back(h[...], cot[...].astype(f32), gfirst, gsecond[...], gain, ggain, gshift)
    up_ref[...] = up
    low = up.astype(bf16)
    up_low[...] = low
    store_rows(up_low, up_rows)
    attend_back(meta, starts, low, ow, den, att, fq, gnum, gden, keep, send)
    gob[...] = jnp.sum(low.astype(f32), axis=0, keepdims=True)


def last_kernel(
    meta, starts, mine, theirs, gfq, gfk, gval, fk, v, eq, ek, ta, tb, tc, dh, dl, w, h, gain, gsecond, up,
    gp, gqb, ggain, gshift, ginputs,
):
    packed_back(
        meta, starts, mine, theirs, gfq, gfk, gval, fk, v, eq, ek, (ta, tb, tc), (dh, dl), gp, gqb
    )
    gfirst = dot(gp[...], w[...], NT)
    ginputs[...] = upstream_back(
        h[...].astype(f32), up[...], gfirst, gsecond[...], gain, ggain, gshift
    )


def reversed_bits(value, count):
    return sum(((value >> k) & 1) << (count - 1 - k) for k in range(count))


def gathered(size, meta, x, flat, held):
    count = size.bit_length() - 1
    block = flat.shape[0] // size
    flat[...] = x.astype(f32).T
    for place in range(size):
        source = reversed_bits(place, count) ^ meta[2]
        held[place * block : (place + 1) * block, :] = flat[
            pl.ds(pl.multiple_of(source * block, block), block), :
        ]
    return held[...].astype(bf16)


def feed_grad_kernel(size, early_is_second, meta, *refs):
    *sources, iw, ib, dw, keep, send, s_all, u_all, act, lift, out = refs
    load_tokens(meta, early_is_second, sources, s_all, u_all)
    tokens = s_all.shape[0] // 4
    for k in range(4):
        at = slice(k * tokens, (k + 1) * tokens)
        lifted = dot(s_all[at], iw[...]) + ib[...].astype(f32)
        value, slope = gelu_parts(lifted)
        act[at] = value.astype(bf16)
        lift[at] = (dot(u_all[at], dw[...], NT) * slope).astype(bf16)
    block = D // size
    count = size.bit_length() - 1
    for part, grads in enumerate(
        (dot(s_all[...], lift[...], TN), dot(act[...], u_all[...], TN))
    ):
        for s in range(size):
            place = reversed_bits(s ^ meta[2], count)
            at = pl.multiple_of((2 * place + part) * block, block)
            out[pl.ds(at, block), :] = grads[s * block : (s + 1) * block]
    half = out.shape[0] // 2
    keep[...] = out[:half]
    send[...] = out[half:]


def load_tokens(meta, early_is_second, sources, s_all, u_all):
    early_ref, own0, own1, a1, a2, b1, b2 = sources
    fresh, early = (u_all, s_all) if early_is_second else (s_all, u_all)
    tokens = s_all.shape[0] // 4
    for k in range(4):
        early[k * tokens : (k + 1) * tokens] = early_ref[
            k ^ meta[5], 0 if early_is_second else 1
        ].astype(bf16)
    half = tokens // 2
    places = (own0[...], own1[...], a1[...], b2[:half], a2[:half], b1[...], a2[half:], b2[half:])
    for k, value in enumerate(places):
        fresh[k * half : (k + 1) * half] = value.astype(bf16)


def chosen(refs, index):
    value = refs[0][...]
    for k in range(1, len(refs)):
        value = jnp.where(index == k, refs[k][...], value)
    return value


def join_kernel(meta, *refs):
    pieces, outs = refs[:-4], refs[-4:]
    in_out, down_out, qkv_out, out_out = outs
    block = in_out.shape[1]
    low = low_lanes(block)
    for layer in range(2):
        own, first, rest, a_own, a_other, b_own, b_other = pieces[7 * layer : 7 * layer + 7]
        both = (rest.at[: 2 * block], rest.at[2 * block :])
        held = (own, first, *both) if layer == 1 else (own, both[0], first, both[1])
        for pair in range(2):
            left, right = (chosen(held, q ^ meta[5]) for q in (2 * pair, 2 * pair + 1))
            down_out[layer, 2 * pair * block : (2 * pair + 1) * block, :] = left[block:]
            down_out[layer, (2 * pair + 1) * block : (2 * pair + 2) * block, :] = right[block:]
            for tile in range(D // 128):
                lanes = slice(tile * 128, (tile + 1) * 128)
                a, b = left[:block, lanes], right[:block, lanes]
                at = 2 * tile * 256 + pair * 128
                in_out[layer, :, at : at + 128] = jnp.where(low, a, pltpu.roll(b, 64, 1))
                in_out[layer, :, at + 256 : at + 384] = jnp.where(low, pltpu.roll(a, 64, 1), b)
        for part, (mine, other) in enumerate(((a_own, a_other), (b_own, b_other))):
            for k in range(2):
                value = jnp.where(meta[3 + part] == k, mine[:block], other[:block])
                q = 2 * part + k
                qkv_out[layer, :, q * 384 : (q + 1) * 384] = value[:, :384]
                out_out[layer, :, q * 128 : (q + 1) * 128] = value[:, 384:]


def packed_grad_kernel(size, meta, first, att_low, gp, up, a_keep, a_send, b_keep, b_send, f1, h1):
    for source, wide, begin in ((first, 384, 0), (att_low, 128, 384)):
        left = gathered(size, meta, source[...], f1, h1)
        right = gp if wide == 384 else up
        for part, (keep, send) in enumerate(((a_keep, a_send), (b_keep, b_send))):
            for k in range(2):
                at = pl.multiple_of((2 * part + (k ^ meta[3 + part])) * wide, wide)
                out = dot(left, right[:, pl.ds(at, wide)])
                keep[k, :, begin : begin + wide] = out[: D // 2]
                send[k, :, begin : begin + wide] = out[D // 2 :]


class Layer:
    def __init__(self, array, index):
        self.array, self.index = array, index


class Scalars:
    def __init__(self, array):
        self.array = array


def call(kernel, name, operands, outs, flops, scratch=()):
    specs, arrays = [], []
    for operand in operands:
        if isinstance(operand, Scalars):
            specs.append(pl.BlockSpec(memory_space=pltpu.SMEM))
            arrays.append(operand.array)
        elif isinstance(operand, Layer):
            array, index = operand.array, operand.index
            rest = array.shape[1:]
            specs.append(
                pl.BlockSpec(
                    (None,) + rest, lambda i, n=len(rest), index=index: (index,) + (0,) * n
                )
            )
            arrays.append(array)
        else:
            specs.append(pl.BlockSpec(operand.shape, lambda i, n=operand.ndim: (0,) * n))
            arrays.append(operand)
    moved = sum(a.size * a.dtype.itemsize for a in arrays)
    moved += sum(math.prod(o.shape) * o.dtype.itemsize for o in outs)
    return pl.pallas_call(
        kernel,
        name=name,
        grid=(1,),
        in_specs=specs,
        out_specs=[pl.BlockSpec(o.shape, lambda i, n=len(o.shape): (0,) * n) for o in outs],
        out_shape=list(outs),
        scratch_shapes=list(scratch),
        cost_estimate=pl.CostEstimate(flops=int(flops), bytes_accessed=moved, transcendentals=0),
        compiler_params=pltpu.CompilerParams(vmem_limit_bytes=62 * 1024 * 1024),
    )(*arrays)


def cosine_table():
    frequency = np.arange(HEAD, dtype=np.float64)[:, None]
    columns = np.arange(HEAD, dtype=np.float64)[None, :]
    entries = np.cos(math.pi * (2.0 * columns + 1.0) * frequency / (2.0 * HEAD))
    entries = entries * math.sqrt(2.0 / HEAD)
    entries[0] *= math.sqrt(0.5)
    wide = np.kron(np.eye(4), entries.T)
    high = wide.astype(np.float32).astype(bf16)
    low = (wide.astype(np.float32) - high.astype(np.float32)).astype(bf16)
    return jnp.asarray(high), jnp.asarray(low)


def rotary_tables(places):
    lane = jnp.arange(128) % HEAD
    half = ROT // 2
    inverse = 10000.0 ** (-((lane % half).astype(f32) * 2.0 / ROT))
    inverse = jnp.where(lane < ROT, inverse, 0.0)
    angles = places.astype(f32)[:, None] * inverse[None, :]
    sine = jnp.sin(angles)
    ahead = jnp.where(lane < half, -sine, 0.0)
    behind = jnp.where((lane >= half) & (lane < ROT), sine, 0.0)
    return jnp.cos(angles), ahead, behind


def flip(value, axis, bit):
    size = lax.axis_size(axis)
    return lax.ppermute(value, axis, [(i, i ^ bit) for i in range(size)])


def tie(*values):
    return lax.optimization_barrier(values)


def exchange(keep, send, flag, core, chip, backward, works=()):
    chips = lax.axis_size("seq") // 2
    begin, span = chip * 2 * LEN, 2 * LEN
    got = flip(send, "seq", 1)
    even, odd = jnp.where(core == 0, keep, got), jnp.where(core == 0, got, keep)
    if backward:
        total = even + flag(begin + LEN - 1, begin) * odd
    else:
        total = odd + flag(begin + span - 1, begin + LEN) * even
    entered, made, step = None, [], 1
    while step < chips:
        other = flip(total, "seq", 2 * step)
        if len(made) < len(works):
            found = works[len(made)](lambda x, total=total: tie(total, x)[1])
            leaves, tree = jax.tree.flatten(found)
            other, *leaves = tie(other, *leaves)
            made.append(jax.tree.unflatten(tree, leaves))
        upper = (chip // step) % 2 == 1
        first = chip - chip % (2 * step)
        middle = first + step
        later, earlier = jnp.where(upper, total, other), jnp.where(upper, other, total)
        if backward:
            passed = jnp.where(upper, 0.0, flag(middle * span - 1, (chip + 1) * span))
            total = earlier + flag(middle * span - 1, first * span) * later
        else:
            passed = jnp.where(upper, flag(chip * span - 1, middle * span), 0.0)
            total = later + flag((middle + step) * span - 1, middle * span) * earlier
        entered = passed * other if entered is None else entered + passed * other
        step *= 2
    if backward:
        for_even, for_odd = odd + flag(begin + span - 1, begin + LEN) * entered, entered
    else:
        for_even, for_odd = entered, even + flag(begin + LEN - 1, begin) * entered
    mine = jnp.where(core == 0, for_even, for_odd)
    theirs = flip(jnp.where(core == 0, for_odd, for_even), "seq", 1)
    return (mine, theirs), made


def halved(total):
    step = 2
    while step < lax.axis_size("seq"):
        half = total.shape[0] // 2
        total = total[:half] + flip(total[half:], "seq", step)
        step *= 2
    return total


def reduce_chunk(keep, send, bit):
    got = flip(send, "seq", 1)
    got_first = flip(keep[1] + got[1], "batch", bit)
    total = halved(keep[0] + got[0] + got_first)
    total = total + flip(total, "batch", 3 - bit)
    return total, flip(total, "batch", bit)


def reduce_quarter(keep, send, bit):
    total = halved(keep + flip(send, "seq", 1))
    other = flip(total, "batch", bit)
    return total, other, flip(jnp.concatenate([total, other], axis=0), "batch", 3 - bit)


def join(pieces, column, bits, size):
    slot = D // size
    made = [[], [], [], []]
    for layer in range(2):
        own, first, rest, a_own, a_other, b_own, b_other = pieces[7 * layer : 7 * layer + 7]
        both = (rest[: 2 * slot], rest[2 * slot :])
        held = (own, first, *both) if layer == 1 else (own, both[0], first, both[1])
        held = jnp.take(jnp.stack(held), np.arange(4) ^ column, axis=0)
        made[0].append(
            held[:, :slot].reshape(4, slot, size, slot).transpose(1, 2, 0, 3).reshape(slot, FF)
        )
        made[1].append(held[:, slot:].reshape(4 * slot, D))
        quarters = []
        for bit, mine, other in ((bits[0], a_own, a_other), (bits[1], b_own, b_other)):
            mine, other = mine[:slot], other[:slot]
            quarters += [jnp.where(bit == 0, mine, other), jnp.where(bit == 0, other, mine)]
        made[2].append(jnp.concatenate([q[:, :384] for q in quarters], axis=1))
        made[3].append(jnp.concatenate([q[:, 384:] for q in quarters], axis=1))
    return [jnp.stack(part) for part in made]


def per_device(
    inputs,
    doc_starts,
    cotangent,
    norm_gain,
    norm_bias,
    qkv_weight,
    qkv_bias,
    out_weight,
    out_bias,
    in_weight,
    in_bias,
    down_weight,
    down_bias,
):
    rows, length = inputs.shape[0], inputs.shape[1]
    tokens = rows * length
    size = lax.axis_size("seq")
    me, column = lax.axis_index("seq"), lax.axis_index("batch")
    core, chip = me % 2, me // 2
    bits = (column % 2, column // 2)
    begin = me * length
    absolute = begin + jnp.arange(length, dtype=jnp.int32)

    def segment_at(position):
        return jnp.max(jnp.where(doc_starts <= position, doc_starts, 0), axis=1)

    def flag(position, limit):
        return (segment_at(position) < limit).astype(f32)[:, None, None]

    segment = jnp.max(
        jnp.where(doc_starts[:, None, :] <= absolute[None, :, None], doc_starts[:, None, :], 0),
        axis=2,
    )
    tables = rotary_tables((absolute[None, :] - segment).reshape(tokens))
    dct = cosine_table()
    meta = Scalars(jnp.stack([begin, core, me, bits[0], bits[1], column]).astype(jnp.int32))
    starts = Scalars(doc_starts)
    hidden0 = inputs.reshape(tokens, D)
    cot = cotangent.reshape(tokens, D)
    out_bias2, in_bias2, down_bias2 = (
        out_bias[:, None, :],
        in_bias[:, None, :],
        down_bias[:, None, :],
    )

    tall, fat = sds((tokens, D)), sds((tokens, D), bf16)
    packed_state = sds((rows, PACK, 128))
    front_outs = [fat, fat, fat, fat, fat, tall, tall, packed_state, packed_state]
    matmul = 2.0 * tokens * D * D

    def front_of(layer):
        return [
            Layer(norm_gain, layer),
            Layer(norm_bias, layer),
            Layer(qkv_weight, layer),
            Layer(qkv_bias, layer),
            *tables,
            *dct,
        ]

    quarter_wide = FF // size // 4
    feed_weights = [
        [Layer(x, layer) for x in (in_weight, in_bias2, down_weight, down_bias2)]
        for layer in range(2)
    ]

    def quarter_weights(layer):
        shape = (size, 4, quarter_wide)
        pick = functools.partial(lax.dynamic_index_in_dim, index=column, keepdims=False)
        return [
            pick(in_weight[layer].reshape((D,) + shape), axis=2).reshape(D, D),
            pick(in_bias[layer].reshape(shape), axis=1).reshape(1, D),
            pick(down_weight[layer].reshape(shape + (D,)), axis=1).reshape(D, D),
        ]

    def gather_first(rows):
        return flip(rows[0], "batch", 1), flip(rows[1], "batch", 2)

    def gather_second(rows, firsts):
        a = jnp.concatenate([rows[0], firsts[0]], axis=0)
        b = jnp.concatenate([rows[1], firsts[1]], axis=0)
        return flip(a, "batch", 2), flip(b, "batch", 1)

    def feed_grad(early, fresh, firsts, seconds, layer):
        halves = [sds((D, D))] * 2
        operands = [early, *fresh, firsts[0], seconds[0], firsts[1], seconds[1]]
        return call(
            functools.partial(feed_grad_kernel, size, layer == 0),
            "feed_grad",
            [meta, *operands, *quarter_weights(layer)],
            halves,
            16 * matmul,
            [pltpu.VMEM((4 * tokens, D), bf16)] * 4 + [pltpu.VMEM((2 * D, D), f32)],
        )

    def packed_grad(first, att_low, gp, up):
        quarter = sds((2, D // 2, D))
        flat = [pltpu.VMEM((D, tokens), f32)] * 2
        return call(
            functools.partial(packed_grad_kernel, size),
            "packed_grad",
            [meta, first, att_low, gp, up],
            [quarter] * 4,
            4 * matmul,
            flat,
        )

    line = sds((LEN, D))
    first0, second0, fq0, fk0, v0, eq0, ek0, keep, send, early = call(
        front_kernel,
        "front",
        [meta, starts, hidden0, cot, *front_of(0)],
        front_outs + [sds((2, tokens, D))],
        6 * matmul,
    )
    early = lax.all_gather(early, "batch")
    intra_outs = [sds((rows, PAIRS, 2 * LEN, LEN), bf16), tall, tall]

    def do_feed(gate):
        return call(
            feed_kernel,
            "feed",
            [gate(second0), *feed_weights[0]],
            [sds((tokens, FF), bf16), sds((tokens, FF)), tall],
            8 * matmul,
        )

    def do_intra(fq, fk, v):
        return lambda gate: call(
            intra_kernel, "intra", [meta, starts, gate(fq), fk, v], intra_outs, 2 * matmul
        )

    entered0, made = exchange(
        keep, send, flag, core, chip, False, [do_feed, do_intra(fq0, fk0, v0)]
    )
    (_, slope0, feed0), (scores0, num0, kt0) = made
    (
        den0, att0, att_low0, hidden1, first1, second1, fq1, fk1, v1, eq1, ek1, keep, send, *rows1
    ) = call(
        middle_kernel,
        "middle",
        [meta, starts, hidden0, feed0, num0, kt0, fq0, *entered0]
        + [Layer(out_weight, 0), Layer(out_bias2, 0), *front_of(1)],
        [tall, tall, fat, tall] + front_outs + [line] * 2,
        8 * matmul,
    )

    def do_feed_both(gate):
        return gather_first([gate(row) for row in rows1]), call(
            feed_both_kernel,
            "feed_both",
            [gate(second1), *feed_weights[1], cot],
            [sds((tokens, FF), bf16), tall, sds((tokens, FF), bf16), tall, sds((1, FF))],
            16 * matmul,
        )

    entered1, made = exchange(
        keep, send, flag, core, chip, False, [do_feed_both, do_intra(fq1, fk1, v1)]
    )
    (firsts1, (_, feed1, _, gsecond1, gib1)), (scores1, num1, kt1) = made
    seconds1 = gather_second(rows1, firsts1)
    den1, att1, att_low1, result, gnum1, gden1, keep, send, gob1 = call(
        turn_kernel,
        "turn",
        [meta, starts, hidden1, feed1, num1, kt1, fq1, *entered1]
        + [Layer(out_weight, 1), Layer(out_bias2, 1), cot],
        [tall, tall, fat, fat, fat, tall, packed_state, packed_state, sds((1, D))],
        3 * matmul,
    )

    def do_intra_back(fq, fk, v, scores, gnum, gden, entered):
        return lambda gate: call(
            intra_back_kernel,
            "intra_back",
            [meta, starts, gate(fq), fk, v, scores, gnum, gden, *entered],
            [tall, tall, tall],
            4 * matmul,
        )

    later1, made = exchange(
        keep, send, flag, core, chip, True,
        [do_intra_back(fq1, fk1, v1, scores1, gnum1, gden1, entered1)],
    )
    ((gfq1, gfk1, gval1),) = made
    vector_outs = [sds((1, 3 * D)), sds((2, D)), sds((2, D))]
    packed = sds((tokens, 3 * D), bf16)
    gp1, gqb1, ggain1, gshift1, up0, up_low0, gnum0, gden0, keep, send, gob0, *rows0 = call(
        turn_back_kernel,
        "turn_back",
        [meta, starts, *later1, gfq1, gfk1, gval1, fk1, v1, eq1, ek1, *tables, *dct]
        + [Layer(qkv_weight, 1), hidden1, Layer(norm_gain, 1), gsecond1, cot]
        + [Layer(out_weight, 0), den0, att0, fq0],
        [packed, *vector_outs, tall, fat, fat, tall, packed_state, packed_state, sds((1, D))]
        + [line] * 2,
        8 * matmul,
    )
    feed_keep1, feed_send1 = feed_grad(early, rows1, firsts1, seconds1, 1)
    chunk_feed1 = reduce_quarter(feed_keep1, feed_send1, 1)

    def do_feed_back(gate):
        firsts = gather_first([gate(row) for row in rows0])
        return firsts, call(
            feed_back_kernel,
            "feed_back",
            [slope0, gate(up_low0), Layer(in_weight, 0), Layer(down_weight, 0)],
            [sds((tokens, FF), bf16), tall, sds((1, FF))],
            8 * matmul,
        )

    later0, made = exchange(
        keep, send, flag, core, chip, True,
        [do_feed_back, do_intra_back(fq0, fk0, v0, scores0, gnum0, gden0, entered0)],
    )
    (firsts0, (_, gsecond0, gib0)), (gfq0, gfk0, gval0) = made
    seconds0 = gather_second(rows0, firsts0)
    a_keep, a_send, b_keep, b_send = packed_grad(first1, att_low1, gp1, cot)
    chunk_packed1 = reduce_chunk(a_keep, a_send, 1), reduce_chunk(b_keep, b_send, 2)
    gp0, gqb0, ggain0, gshift0, ginputs = call(
        last_kernel,
        "last",
        [meta, starts, *later0, gfq0, gfk0, gval0, fk0, v0, eq0, ek0, *tables, *dct]
        + [Layer(qkv_weight, 0), hidden0, Layer(norm_gain, 0), gsecond0, up0],
        [packed, *vector_outs, tall],
        6 * matmul,
    )
    a_keep, a_send, b_keep, b_send = packed_grad(first0, att_low0, gp0, up_low0)
    feed_keep0, feed_send0 = feed_grad(early, rows0, firsts0, seconds0, 0)
    chunk_feed0 = reduce_quarter(feed_keep0, feed_send0, 2)

    slot, count = D // size, size.bit_length() - 1
    order = np.array([reversed_bits(k, count) for k in range(size)], np.int32) ^ me

    def lines_of(gain, shift, qkv_b, out_b, in_b):
        vectors = jnp.concatenate([gain, shift, qkv_b.reshape(3, D), out_b], axis=0)
        vectors = vectors.reshape(8, size, slot).swapaxes(0, 1)
        wide = in_b.reshape(size, 4, slot)
        wide = jnp.pad(wide, ((0, 0), (0, 4), (0, 0)))
        lines = jnp.concatenate([vectors, wide], axis=2)
        return jnp.pad(lines, ((0, 0), (0, 0), (0, D - 2 * slot)))

    lines0 = lines_of(ggain0, gshift0, gqb0, gob0, gib0)
    lines1 = lines_of(ggain1, gshift1, gqb1, gob1, gib1)
    lines = jnp.where(
        bits[0] == 0, jnp.stack([lines0, lines1]), jnp.stack([lines1, lines0])
    )
    lines = jnp.take(lines, order, axis=1)

    def with_lines(part, lines):
        part = part.reshape(2, size // 2, slot, D)
        return jnp.concatenate([part, lines], axis=2).reshape(2, -1, D)

    a_keep = with_lines(a_keep, lines[:, : size // 2])
    a_send = with_lines(a_send, lines[:, size // 2 :])
    chunk_packed0 = reduce_chunk(a_keep, a_send, 1), reduce_chunk(b_keep, b_send, 2)
    own, other = (part[slot:] for part in chunk_packed0[0])
    summed = jnp.where(bits[0] == 0, jnp.stack([own, other]), jnp.stack([other, own]))
    grad_in_b = summed[:, :4, slot : 2 * slot].reshape(2, FF // size)
    summed = summed[:, :, :slot]
    grad_out_b = summed[:, 7]

    pieces = [
        piece
        for feed, (a, b) in ((chunk_feed0, chunk_packed0), (chunk_feed1, chunk_packed1))
        for piece in (*feed, *a, *b)
    ]
    outs = [
        sds((2, slot, FF)),
        sds((2, FF // size, D)),
        sds((2, slot, 3 * D)),
        sds((2, slot, D)),
    ]
    if quarter_wide == HEAD:
        grad_in, grad_down, grad_qkv, grad_out = call(
            join_kernel, "join", [meta, *pieces], outs, matmul
        )
    else:
        grad_in, grad_down, grad_qkv, grad_out = join(pieces, column, bits, size)
    return (
        result.reshape(rows, length, D),
        ginputs.reshape(rows, length, D),
        summed[:, 0:2],
        summed[:, 2:4],
        grad_qkv,
        summed[:, 4:7],
        grad_out,
        grad_out_b,
        grad_in,
        grad_in_b,
        grad_down,
        grad_out_b,
    )


def solution(mesh):
    placed = (
        P("batch", "seq", None),
        P("batch", None),
        P("batch", "seq", None),
        P(),
        P(),
        P(),
        P(),
        P(),
        P(),
        P(),
        P(),
        P(),
        P(),
    )
    return jax.shard_map(
        per_device,
        mesh=mesh,
        in_specs=placed,
        out_specs=(
            P("batch", "seq", None),
            P("batch", "seq", None),
            P(None, None, "seq"),
            P(None, None, "seq"),
            P(None, "seq", None),
            P(None, None, "seq"),
            P(None, "seq", None),
            P(None, "seq"),
            P(None, "seq", None),
            P(None, "seq"),
            P(None, "seq", None),
            P(None, "seq"),
        ),
        check_vma=False,
    )
```

```python
import functools
import math

import jax
import jax.numpy as jnp
import numpy as np
from jax import lax
from jax.experimental import pallas as pl
from jax.experimental.pallas import tpu as pltpu
from jax.sharding import PartitionSpec as P

D = 512
HEADS = 8
HEAD = 64
FF = 2048
ROT = 16
LAYERS = 2
NDOC = 4
LEN = 128
PAIRS = HEADS // 2
PACK = 2 * HEAD + 8
WIDE = 512

epsilon = 1e-05
f32, bf16 = jnp.float32, jnp.bfloat16
NN = (((1,), (0,)), ((), ()))
NT = (((1,), (1,)), ((), ()))
TN = (((0,), (0,)), ((), ()))


def dot(a, b, dims=NN):
    return lax.dot_general(a, b, dims, preferred_element_type=f32)


def split(x):
    high = x.astype(bf16)
    return high, (x - high.astype(f32)).astype(bf16)


def sds(shape, dtype=f32):
    return jax.ShapeDtypeStruct(shape, dtype)


def norm_parts(hidden):
    centred = hidden - jnp.mean(hidden, axis=-1, keepdims=True)
    variance = jnp.mean(centred * centred, axis=-1, keepdims=True)
    inverse = lax.rsqrt(variance + epsilon)
    return centred * inverse, inverse


def segment_of(position, starts, row):
    found = jnp.zeros_like(position)
    for k in range(NDOC):
        entry = starts[row, k]
        found = jnp.maximum(found, jnp.where(entry <= position, entry, 0))
    return found


def prepare_kernel(starts, masks, tables):
    begin = lax.axis_index("seq") * LEN
    for row in range(masks.shape[1]):
        at_i = begin + lax.broadcasted_iota(jnp.int32, (LEN, 128), 0)
        at_j = begin + lax.broadcasted_iota(jnp.int32, (LEN, 128), 1)
        seg_i, seg_j = segment_of(at_i, starts, row), segment_of(at_j, starts, row)
        last = jnp.int32(0)
        for k in range(NDOC):
            entry = starts[row, k]
            last = jnp.maximum(last, jnp.where(entry <= begin + (LEN - 1), entry, 0))
        masks[0, row] = jnp.where((at_j <= at_i) & (seg_i == seg_j), 1.0, 0.0).astype(f32)
        masks[1, row] = jnp.where(seg_i < begin, 1.0, 0.0).astype(f32)
        masks[2, row] = jnp.where(seg_i == last, 1.0, 0.0).astype(f32)
        lane = lax.broadcasted_iota(jnp.int32, (LEN, 128), 1) % HEAD
        inverse = jnp.exp((lane % (ROT // 2)).astype(f32) * (-2.0 / ROT * math.log(10000.0)))
        angles = (at_i - seg_i).astype(f32) * jnp.where(lane < ROT, inverse, 0.0)
        at = slice(row * LEN, (row + 1) * LEN)
        tables[0, at] = jnp.cos(angles)
        tables[1, at] = jnp.sin(angles)


def masks_of(row, masks):
    return masks[0, row], masks[1, row], masks[2, row]


def low_lanes(rows):
    return lax.broadcasted_iota(jnp.int32, (rows, 128), 1) < HEAD


def read_tables(tables):
    sine = tables[1]
    lane = lax.broadcasted_iota(jnp.int32, sine.shape, 1) % HEAD
    ahead = jnp.where(lane < ROT // 2, -sine, 0.0)
    behind = jnp.where((lane >= ROT // 2) & (lane < ROT), sine, 0.0)
    return tables[0], ahead, behind


def rotate(x, tables):
    base, ahead, behind = tables
    return x * base + pltpu.roll(x, 120, 1) * ahead + pltpu.roll(x, 8, 1) * behind


def rotate_back(g, tables):
    base, ahead, behind = tables
    return g * base + pltpu.roll(g * ahead, 8, 1) + pltpu.roll(g * behind, 120, 1)


def featurize(x, tables, high, low):
    pieces = [rotate(x[:, g * 128 : (g + 1) * 128], tables) for g in range(4)]
    found = []
    for g in range(2):
        a, b = split(jnp.concatenate(pieces[2 * g : 2 * g + 2], axis=1))
        found.append(jnp.exp(dot(a, high) + dot(b, high) + dot(a, low)))
    return jnp.concatenate(found, axis=1)


def unfeaturize(g, tables, high, low):
    found = []
    for k in range(2):
        a, b = split(g[:, k * 256 : (k + 1) * 256])
        back = dot(a, high, NT) + dot(b, high, NT) + dot(a, low, NT)
        found += [rotate_back(back[:, :128], tables), rotate_back(back[:, 128:], tables)]
    return jnp.concatenate(found, axis=1)


def head_ones():
    across = lax.broadcasted_iota(jnp.int32, (256, 256), 0) // HEAD
    along = lax.broadcasted_iota(jnp.int32, (256, 256), 1) // HEAD
    return jnp.where(across == along, 1.0, 0.0).astype(bf16)


def head_sum(x, ones):
    found = []
    for g in range(2):
        a, b = split(x[:, g * 256 : (g + 1) * 256])
        found.append(dot(a, ones) + dot(b, ones))
    return jnp.concatenate(found, axis=1)


def store_halves(keep_ref, send_ref, halves):
    def put(ref, half):
        for row, at, value in halves[half]:
            ref[row, at[0] : at[1], :] = value

    core = lax.axis_index("seq") % 2
    for mine in range(2):

        @pl.when(core == mine)
        def _():
            put(keep_ref, mine)
            put(send_ref, 1 - mine)


def pack_states(rows, left_of, right, norm_of):
    low = low_lanes(HEAD)
    halves = [[], []]
    for row in range(rows):
        at = slice(row * LEN, (row + 1) * LEN)
        left, norm = left_of(row), norm_of(row)
        for pair in range(PAIRS):
            lanes = slice(pair * 128, (pair + 1) * 128)
            both = dot(left[:, lanes], right[at, lanes], TN)
            half, place = pair // 2, pair % 2
            halves[half].append(
                (row, (place * HEAD, (place + 1) * HEAD), jnp.where(low, both[:HEAD], both[HEAD:]))
            )
        for half in range(2):
            pieces = [norm[:, (2 * half + k) * 128 : (2 * half + k + 1) * 128] for k in range(2)]
            block = jnp.concatenate(pieces + [jnp.zeros((6, 128), f32)], axis=0)
            halves[half].append((row, (2 * HEAD, PACK), block))
    return halves


def unpack_state(mine_ref, theirs_ref, row):
    low = low_lanes(HEAD)
    blocks, norms = [], []
    for half in range(2):
        here = lax.axis_index("seq") % 2 == half
        packed = jnp.where(here, mine_ref[row], theirs_ref[row])
        for place in range(2):
            state = packed[place * HEAD : (place + 1) * HEAD]
            both = jnp.concatenate(
                [jnp.where(low, state, 0.0), jnp.where(low, 0.0, state)], axis=0
            )
            blocks.append(split(both))
            norms.append(packed[2 * HEAD + place : 2 * HEAD + place + 1])
    return blocks, jnp.concatenate(norms, axis=1)


def cross_dot(x, block, dims=NN):
    return dot(x, block[0], dims) + dot(x, block[1], dims)


def gelu_parts(lifted):
    phi = 0.5 + 0.5 * lax.erf(lifted * math.sqrt(0.5))
    slope = phi + lifted * (jnp.exp(-0.5 * lifted * lifted) * (1.0 / math.sqrt(2.0 * math.pi)))
    return lifted * phi, slope


def norm_back(grad, xhat, inverse, gain):
    u = grad * gain
    mean_u = jnp.mean(u, axis=-1, keepdims=True)
    mean_ux = jnp.mean(u * xhat, axis=-1, keepdims=True)
    down = (u - mean_u - xhat * mean_ux) * inverse
    return down, jnp.sum(grad * xhat, axis=0, keepdims=True), jnp.sum(grad, axis=0, keepdims=True)


def front_body(layer, masks, hidden, gain, shift, w, b, tables, dct, outs):
    first_ref, second_ref, fq_ref, fk_ref, v_ref, eq_ref, ek_ref, keep_ref, send_ref, *_ = outs
    xhat, _ = norm_parts(hidden)
    gains, shifts = gain[...].astype(f32), shift[...].astype(f32)
    first = (xhat * gains[0:1] + shifts[0:1]).astype(bf16)
    first_ref[...] = first
    second_ref[...] = (xhat * gains[1:2] + shifts[1:2]).astype(bf16)
    bias = [b[k][layer : layer + 1].astype(f32) for k in range(3)]
    tabs = read_tables(tables)
    high, low = dct[0], dct[1]
    keys = dot(first, w[:, D : 2 * D]) + bias[1]
    values = (dot(first, w[:, 2 * D :]) + bias[2]).astype(bf16)
    v_ref[...] = values
    exp_k = featurize(keys, tabs, high, low)
    ek_ref[...] = exp_k
    feat_k = exp_k.astype(bf16)
    fk_ref[...] = feat_k
    rows = hidden.shape[0] // LEN
    wide = feat_k.astype(f32)

    def tailed(row):
        tail = masks_of(row, masks)[2]
        return wide[row * LEN : (row + 1) * LEN] * jnp.concatenate([tail] * 4, axis=1)

    kept = [tailed(row) for row in range(rows)]
    halves = pack_states(
        rows,
        lambda row: kept[row].astype(bf16),
        values,
        lambda row: jnp.sum(kept[row], axis=0, keepdims=True),
    )
    store_halves(keep_ref, send_ref, halves)
    queries = dot(first, w[:, :D]) + bias[0]
    exp_q = featurize(queries, tabs, high, low)
    eq_ref[...] = exp_q
    fq_ref[...] = exp_q.astype(bf16)


def front_kernel(masks, h, cot, gain, shift, w, b, tables, dct, *outs):
    hidden = h[...].astype(f32)
    front_body(0, masks, hidden, gain, shift, w, b, tables, dct, outs[:9])
    outs[9][...] = outs[1][...].astype(f32)
    outs[10][...] = cot[...].astype(f32)


def attend(masks, num_ref, kt_ref, fq_ref, mine_ref, theirs_ref, den_ref, att_ref, low_ref):
    rows = num_ref.shape[0] // LEN
    ones = head_ones()
    for row in range(rows):
        at = slice(row * LEN, (row + 1) * LEN)
        cross = masks_of(row, masks)[1]
        cross4 = jnp.concatenate([cross] * 4, axis=1)
        blocks, norm = unpack_state(mine_ref, theirs_ref, row)
        fq = fq_ref[at]
        far = jnp.concatenate(
            [cross_dot(fq[:, p * 128 : (p + 1) * 128], blocks[p]) for p in range(PAIRS)], axis=1
        )
        num = num_ref[at] + cross4 * far
        den = head_sum(fq.astype(f32) * (kt_ref[at] + cross4 * norm), ones)
        att = num / den
        den_ref[at] = den
        att_ref[at] = att
        low_ref[at] = att.astype(bf16)


def middle_kernel(
    masks, num, kt, fq0, mine, theirs, ow, ob, h, feed, gain, shift, w, b, tables, dct,
    den, att, att_low, h2, *outs,
):
    attend(masks, num, kt, fq0, mine, theirs, den, att, att_low)
    hidden = h[...].astype(f32) + (dot(att_low[...], ow[...]) + ob[0:1].astype(f32)) + feed[...]
    h2[...] = hidden
    front_body(1, masks, hidden, gain, shift, w, b, tables, dct, outs)
    outs[9][...] = outs[1][...].astype(f32)


def attend_back(masks, up, ow, den, att, fq, gnum, gden, keep_ref, send_ref):
    ga = dot(up, ow[...], NT)
    den_v = den[...]
    gn = (ga / den_v).astype(bf16)
    gnum[...] = gn
    gd = -head_sum(ga * att[...], head_ones()) / den_v
    gden[...] = gd
    rows = up.shape[0] // LEN
    wide = fq[...].astype(f32)

    def crossed(row):
        cross = masks_of(row, masks)[1]
        return wide[row * LEN : (row + 1) * LEN] * jnp.concatenate([cross] * 4, axis=1)

    kept = [crossed(row) for row in range(rows)]
    halves = pack_states(
        rows,
        lambda row: kept[row].astype(bf16),
        gn,
        lambda row: jnp.sum(kept[row] * gd[row * LEN : (row + 1) * LEN], axis=0, keepdims=True),
    )
    store_halves(keep_ref, send_ref, halves)


def turn_kernel(
    masks, num, kt, fq, mine, theirs, ow, cot, att_low, gnum, gden, keep, send, den, att,
):
    attend(masks, num, kt, fq, mine, theirs, den, att, att_low)
    attend_back(masks, cot[...], ow, den, att, fq, gnum, gden, keep, send)


def feed_kernel(second, iw, ib, dw, db, feed):
    total = jnp.broadcast_to(db[0:1].astype(f32), feed.shape)
    for g in range(FF // WIDE):
        lanes = slice(g * WIDE, (g + 1) * WIDE)
        lifted = dot(second[...], iw[:, lanes]) + ib[0:1, lanes].astype(f32)
        total = total + dot(gelu_parts(lifted)[0].astype(bf16), dw[lanes, :])
    feed[...] = total


def feed_back_kernel(layer, second, iw, ib, dw, db, up_low, up, h, gain, *outs):
    base, gain_out, shift_out, gib, *feed = outs
    total = jnp.broadcast_to(db[layer : layer + 1].astype(f32), base.shape)
    back = jnp.zeros(base.shape, f32)
    low_up = up_low[...]
    for g in range(FF // WIDE):
        lanes = slice(g * WIDE, (g + 1) * WIDE)
        lifted = dot(second[...], iw[:, lanes]) + ib[layer : layer + 1, lanes].astype(f32)
        value, slope = gelu_parts(lifted)
        rows = dw[lanes, :]
        if feed:
            total = total + dot(value.astype(bf16), rows)
        low = (dot(low_up, rows, NT) * slope).astype(bf16)
        gib[:, lanes] = jnp.sum(low.astype(f32), axis=0, keepdims=True)
        back = back + dot(low, iw[:, lanes], NT)
    if feed:
        feed[0][...] = total
    xhat, inverse = norm_parts(h[...].astype(f32))
    gains = gain[...].astype(f32)
    part, gain_out[...], shift_out[...] = norm_back(back, xhat, inverse, gains[1:2])
    base[...] = up[...].astype(f32) + part


def intra_kernel(masks, fq, fk, v, scores, num, kt):
    low = low_lanes(LEN)
    even = jnp.where(low, 1.0, 0.0).astype(bf16)
    odd = jnp.where(low, 0.0, 1.0).astype(bf16)
    for row in range(fq.shape[0] // LEN):
        at = slice(row * LEN, (row + 1) * LEN)
        intra = masks_of(row, masks)[0]
        kt[at] = dot(intra.astype(bf16), fk[at])
        twice = jnp.concatenate([intra, intra], axis=0)
        for pair in range(PAIRS):
            lanes = slice(pair * 128, (pair + 1) * 128)
            q = fq[at, lanes]
            both = jnp.concatenate([q * even, q * odd], axis=0)
            rounded = (dot(both, fk[at, lanes], NT) * twice).astype(bf16)
            scores[row, pair] = rounded
            out = dot(rounded, v[at, lanes])
            num[at, lanes] = jnp.where(low, out[:LEN], out[LEN:])


def intra_back_kernel(
    masks, fq, fk, v, scores, gnum, gden, mine, theirs, eq, tables, dct, gq, gfk, gval
):
    low = low_lanes(LEN)
    even = jnp.where(low, 1.0, 0.0).astype(bf16)
    odd = jnp.where(low, 0.0, 1.0).astype(bf16)
    grad = []
    for row in range(fq.shape[0] // LEN):
        at = slice(row * LEN, (row + 1) * LEN)
        intra, cross, _ = masks_of(row, masks)
        twice = jnp.concatenate([intra, intra], axis=0)
        blocks, norm = unpack_state(mine, theirs, row)
        queries = []
        for pair in range(PAIRS):
            lanes = slice(pair * 128, (pair + 1) * 128)
            gn, gd, q, k = gnum[at, lanes], gden[at, lanes], fq[at, lanes], fk[at, lanes]
            both = jnp.concatenate([gn * even, gn * odd], axis=0)
            turned = pltpu.roll(gd, HEAD, 1)
            dens = jnp.concatenate(
                [jnp.where(low, gd, turned), jnp.where(low, turned, gd)], axis=0
            )
            gs = ((dot(both, v[at, lanes], NT) + dens) * twice).astype(bf16)
            near = dot(gs, k)
            far = cross_dot(gn, blocks[pair], NT) + gd * norm[:, lanes]
            queries.append(jnp.where(low, near[:LEN], near[LEN:]) + cross * far)
            gfk[at, lanes] = jnp.where(low, dot(gs[:LEN], q, TN), dot(gs[LEN:], q, TN))
            sl = scores[row, pair]
            gval[at, lanes] = jnp.where(low, dot(sl[:LEN], gn, TN), dot(sl[LEN:], gn, TN))
        grad.append(jnp.concatenate(queries, axis=1))
    turned = unfeaturize(
        jnp.concatenate(grad, axis=0) * eq[...], read_tables(tables), dct[0], dct[1]
    )
    gq[...] = turned.astype(bf16)


def packed_back(masks, mine, theirs, gq, gfk, gval, fk, v, ek, tables, dct, gp, gqb):
    keys, values = [], []
    for row in range(fk.shape[0] // LEN):
        at = slice(row * LEN, (row + 1) * LEN)
        tail = masks_of(row, masks)[2]
        blocks, norm = unpack_state(mine, theirs, row)
        key_row, value_row = [], []
        for pair in range(PAIRS):
            lanes = slice(pair * 128, (pair + 1) * 128)
            far = cross_dot(v[at, lanes], blocks[pair], NT) + norm[:, lanes]
            key_row.append(gfk[at, lanes] + tail * far)
            value_row.append(gval[at, lanes] + tail * cross_dot(fk[at, lanes], blocks[pair]))
        keys.append(jnp.concatenate(key_row, axis=1))
        values.append(jnp.concatenate(value_row, axis=1))
    gp[:, 2 * D :] = jnp.concatenate(values, axis=0).astype(bf16)
    gp[:, :D] = gq[...]
    keys = unfeaturize(
        jnp.concatenate(keys, axis=0) * ek[...], read_tables(tables), dct[0], dct[1]
    )
    gp[:, D : 2 * D] = keys.astype(bf16)
    gqb[...] = jnp.sum(gp[...].astype(f32), axis=0, keepdims=True)


def upstream_back(base, hidden, gp, w, gain, gain_out, shift_out):
    gfirst = dot(gp[...], w[...], NT)
    xhat, inverse = norm_parts(hidden)
    part, gain_out[...], shift_out[...] = norm_back(
        gfirst, xhat, inverse, gain[...].astype(f32)[0:1]
    )
    return base[...] + part


def turn_back_kernel(
    masks, mine, theirs, gfk, gval, fk, v, ek, tables, dct, gq, w, h, gain, base, ow, den, att, fq,
    gp, gqb, ggain, gshift, up_ref, up_low, gnum, gden, keep, send,
):
    packed_back(masks, mine, theirs, gq, gfk, gval, fk, v, ek, tables, dct, gp, gqb)
    up = upstream_back(base, h[...], gp, w, gain, ggain, gshift)
    up_ref[...] = up
    low = up.astype(bf16)
    up_low[...] = low
    attend_back(masks, low, ow, den, att, fq, gnum, gden, keep, send)


def result_kernel(h, feed, att_low, ow, ob, result):
    hidden = h[...] + (dot(att_low[...], ow[...]) + ob[1:2].astype(f32)) + feed[...]
    result[...] = hidden.astype(bf16)


def last_kernel(
    masks, mine, theirs, gfk, gval, fk, v, ek, tables, dct, gq, w, h, gain, base,
    gp, gqb, ggain, gshift, ginputs,
):
    packed_back(masks, mine, theirs, gq, gfk, gval, fk, v, ek, tables, dct, gp, gqb)
    ginputs[...] = upstream_back(base, h[...].astype(f32), gp, w, gain, ggain, gshift)


def gathered(size, x, flat, held):
    block = flat.shape[0] // size
    flat[...] = x.astype(f32).T
    for place in range(size):
        source = block_at(size, place)
        held[place * block : (place + 1) * block, :] = flat[
            pl.ds(pl.multiple_of(source * block, block), block), :
        ]
    return held[...].astype(bf16)


def reversed_bits(value, count):
    return sum(((value >> k) & 1) << (count - 1 - k) for k in range(count))


def block_at(size, place):
    return reversed_bits(place, size.bit_length() - 1) ^ lax.axis_index("seq")


def pick_quarter(size, layer, q, iw, ib, dw, iw_q, ib_q, dw_q):
    wide = FF // size
    rows = lax.broadcasted_iota(jnp.int32, (128, 128), 0) - HEAD * (q % 2)
    lanes = lax.broadcasted_iota(jnp.int32, (128, 128), 1)
    left = jnp.where((rows == lanes) & (lanes < HEAD), 1.0, 0.0).astype(bf16)
    right = jnp.where((rows == lanes - HEAD) & (lanes >= HEAD), 1.0, 0.0).astype(bf16)
    for pair in range(size // 2):
        at = [
            pl.ds(pl.multiple_of((2 * pair + k) * wide + (q // 2) * 128, 128), 128)
            for k in range(2)
        ]
        here = slice(pair * 128, (pair + 1) * 128)
        iw_q[:, here] = (dot(iw[:, at[0]], left) + dot(iw[:, at[1]], right)).astype(bf16)
        bias = [ib[:, at[k]] for k in range(2)]
        ib_q[:, here] = (dot(bias[0], left) + dot(bias[1], right))[layer : layer + 1]
    quarter = wide // 4
    for s in range(size):
        rows = pl.ds(pl.multiple_of(s * wide + q * quarter, quarter), quarter)
        dw_q[s * quarter : (s + 1) * quarter, :] = dw[rows, :]


def feed_grad_kernel(size, layer, *refs):
    seconds, ups = refs[:4], refs[4:8]
    iw, ib, dw, keep, send, s_all, u_all, act, lift, out, *own = refs[8:]
    if own:
        pick_quarter(size, layer, lax.axis_index("batch"), iw, ib, dw, *own)
        iw, ib, dw = own
    tokens = s_all.shape[0] // 4
    for k in range(4):
        at = slice(k * tokens, (k + 1) * tokens)
        s_all[at], u_all[at] = seconds[k][...].astype(bf16), ups[k][...].astype(bf16)
        lifted = dot(s_all[at], iw[...]) + ib[...].astype(f32)
        value, slope = gelu_parts(lifted)
        act[at] = value.astype(bf16)
        lift[at] = (dot(u_all[at], dw[...], NT) * slope).astype(bf16)
    block = D // size
    for part, grads in enumerate(
        (dot(s_all[...], lift[...], TN), dot(act[...], u_all[...], TN))
    ):
        for s in range(size):
            place = reversed_bits(s ^ lax.axis_index("seq"), size.bit_length() - 1)
            at = pl.multiple_of((2 * place + part) * block, block)
            out[pl.ds(at, block), :] = grads[s * block : (s + 1) * block]
    keep[...] = out[:D]
    send[...] = out[D:]


def chosen(refs, index):
    value = refs[0][...]
    for k in range(1, len(refs)):
        value = jnp.where(index == k, refs[k][...], value)
    return value


def join_kernel(*refs):
    pieces, outs = refs[:16], refs[16:]
    me = lax.axis_index("batch")
    in_out, down_out, qkv_out, out_out, gain_out, shift_out, qkvb_out = outs[:7]
    outb_out, downb_out, inb_out = outs[7:]
    block = in_out.shape[1]
    low = low_lanes(block)
    for layer in range(2):
        held = pieces[8 * layer : 8 * layer + 8]
        for q in range(4):
            packed = chosen(held[4:], q ^ me)
            qkv_out[layer, :, q * 384 : (q + 1) * 384] = packed[:block, :384]
            out_out[layer, :, q * 128 : (q + 1) * 128] = packed[:block, 384:]
            if layer == 0 and q < 2:
                lines = packed[block:]
                gain_out[q] = lines[0:2, :block]
                shift_out[q] = lines[2:4, :block]
                for k in range(3):
                    qkvb_out[k, q : q + 1, :] = lines[4 + k : 5 + k, :block]
                outb_out[q : q + 1, :] = lines[7:8, :block]
                downb_out[q : q + 1, :] = lines[7:8, :block]
                inb_out[q : q + 1, :] = lines[0:1, 256 : 256 + inb_out.shape[1]]
        for pair in range(2):
            left, right = (chosen(held[:4], (2 * pair + k) ^ me) for k in range(2))
            down_out[layer, 2 * pair * block : (2 * pair + 1) * block, :] = left[block:]
            down_out[layer, (2 * pair + 1) * block : (2 * pair + 2) * block, :] = right[block:]
            for tile in range(D // 128):
                lanes = slice(tile * 128, (tile + 1) * 128)
                a, b = left[:block, lanes], right[:block, lanes]
                at = 2 * tile * 256 + pair * 128
                in_out[layer, :, at : at + 128] = jnp.where(low, a, pltpu.roll(b, 64, 1))
                in_out[layer, :, at + 256 : at + 384] = jnp.where(low, pltpu.roll(a, 64, 1), b)


PARTS = ((0, 256), (256, 512))


def standing(quarter, bit):
    return jnp.where(bit == 1, (quarter % 2) * 2 + quarter // 2, quarter)


def packed_grad_kernel(size, bits, first, att_low, gp, up, *refs):
    *vectors, keep_a, send_a, keep_b, send_b, f1, h1 = refs
    block, under = D // size, 8 if vectors else 0
    half, me = size // 2, lax.axis_index("batch")
    for source, right, wide, begin in ((first, gp, 384, 0), (att_low, up, 128, 384)):
        left = gathered(size, source[...], f1, h1)
        for q in range(4):
            out = dot(left, right[:, q * wide : (q + 1) * wide])
            for (low, high), bit, refs in zip(PARTS, bits, ((keep_a, send_a), (keep_b, send_b))):
                lanes = max(low, begin), min(high, begin + wide)
                if lanes[0] >= lanes[1]:
                    continue
                at = standing(q ^ me, bit)
                for place in range(size):
                    here = (place % half) * (block + under)
                    refs[place // half][
                        at, here : here + block, lanes[0] - low : lanes[1] - low
                    ] = out[
                        place * block : (place + 1) * block, lanes[0] - begin : lanes[1] - begin
                    ]
    if vectors:
        put_lines(size, bits, vectors, up, ((keep_a, send_a), (keep_b, send_b)))


def put_lines(size, bits, vectors, up, parts):
    block, wide, me = D // size, FF // size, lax.axis_index("batch")
    held = []
    for *norms, gqb, gib, ups in ((*vectors[:6], up), vectors[6:]):
        gob = jnp.sum(ups[...].astype(f32), axis=0, keepdims=True)
        rows = [part[...] for part in norms]
        rows += [gqb[:, k * D : (k + 1) * D] for k in range(3)] + [gob]
        held.append((jnp.concatenate(rows, axis=0), jnp.broadcast_to(gib[...], (8, FF))))
    for place in range(size):
        source = block_at(size, place)
        here = (place % (size // 2)) * (block + 8) + block
        a_ref, b_ref = (refs[place // (size // 2)] for refs in parts)
        for layer, (rows, line) in enumerate(held):
            a_ref[standing(layer ^ me, bits[0]), here : here + 8, :128] = pltpu.roll(
                rows, (D - source * block) % D, 1
            )[:, :128]
            b_ref[standing(layer ^ me, bits[1]), here : here + 8, :] = pltpu.roll(
                line, (FF - source * wide) % FF, 1
            )[:, :256]
            a_ref[standing(layer ^ me, bits[0]), here : here + 8, 128:] = jnp.zeros((8, 128), f32)
        for k in (2, 3):
            for ref, bit in ((a_ref, bits[0]), (b_ref, bits[1])):
                ref[standing(k ^ me, bit), here : here + 8, :] = jnp.zeros((8, 256), f32)


class Layer:
    def __init__(self, array, index=None):
        self.array, self.index = array, index
        self.shape = array.shape if index is None else jax.eval_shape(lambda x: x[index], array).shape


class Far:
    def __init__(self, shape, dtype=f32):
        self.shape, self.dtype = shape, dtype


class Scalars:
    def __init__(self, array):
        self.array = array


class Source:
    def __init__(self, here, there, semaphore):
        self.here, self.copy = here, pltpu.make_async_copy(there, here, semaphore)
        self.shape, self.copying = here.shape, True
        self.copy.start()

    def __getitem__(self, at):
        if self.copying:
            self.copy.wait()
            self.copying = False
        return self.here[at]


class Target:
    def __init__(self, here, there, semaphore):
        self.here, self.copy = here, pltpu.make_async_copy(here, there, semaphore)
        self.shape, self.started = here.shape, False

    def __getitem__(self, at):
        return self.here[at]

    def __setitem__(self, at, value):
        assert not self.started
        self.here[at] = value
        if at is Ellipsis:
            self.start()

    def start(self):
        if not self.started:
            self.copy.start()
            self.started = True


def call(kernel, name, operands, outs, scratch=()):
    arrays = [getattr(operand, "array", operand) for operand in operands]
    copied = [k for k, operand in enumerate(operands) if isinstance(operand, Layer)]
    written = [k for k, out in enumerate(outs) if isinstance(out, Far)]
    arrays = [
        a
        if isinstance(o, Scalars)
        else pltpu.with_memory_space_constraint(a, pltpu.HBM if isinstance(o, Layer) else pltpu.VMEM)
        for o, a in zip(operands, arrays)
    ]
    vmem, smem = pl.BlockSpec(memory_space=pltpu.VMEM), pl.BlockSpec(memory_space=pltpu.SMEM)
    hbm = pl.BlockSpec(memory_space=pltpu.HBM)
    own = 1 + len(copied) + len(written)

    def body(*refs):
        ins, results = list(refs[: len(operands)]), list(refs[len(operands) :][: len(outs)])
        semaphores, *buffers = refs[len(operands) + len(outs) :]
        for n, k in enumerate(copied):
            index = operands[k].index
            there = ins[k] if index is None else ins[k].at[index]
            ins[k] = Source(buffers[n], there, semaphores.at[n])
        for n, k in enumerate(written):
            n += len(copied)
            results[k] = Target(buffers[n], results[k], semaphores.at[n])
        kernel(*ins, *results, *buffers[own - 1 :])
        assert not any(ins[k].copying for k in copied), name
        for k in written:
            results[k].start()
        for k in written:
            results[k].copy.wait()

    found = pl.pallas_call(
        body,
        name=name,
        in_specs=[
            smem if isinstance(o, Scalars) else hbm if isinstance(o, Layer) else vmem
            for o in operands
        ],
        out_specs=[hbm if isinstance(o, Far) else vmem for o in outs],
        out_shape=[(pltpu.HBM if isinstance(o, Far) else pltpu.VMEM)(o.shape, o.dtype) for o in outs],
        scratch_shapes=[
            pltpu.SemaphoreType.DMA((max(own - 1, 1),)),
            *[pltpu.VMEM(operands[k].shape, arrays[k].dtype) for k in copied],
            *[pltpu.VMEM(outs[k].shape, outs[k].dtype) for k in written],
            *scratch,
        ],
        cost_estimate=pl.CostEstimate(flops=1024, bytes_accessed=1024, transcendentals=0),
        compiler_params=pltpu.CompilerParams(vmem_limit_bytes=26 * 1024 * 1024),
    )(*arrays)
    return [Layer(x) if isinstance(o, Far) else x for x, o in zip(found, outs)]


def cosine_table():
    frequency = np.arange(HEAD, dtype=np.float64)[:, None]
    columns = np.arange(HEAD, dtype=np.float64)[None, :]
    entries = np.cos(math.pi * (2.0 * columns + 1.0) * frequency / (2.0 * HEAD))
    entries = entries * math.sqrt(2.0 / HEAD)
    entries[0] *= math.sqrt(0.5)
    wide = np.kron(np.eye(4), entries.T)
    high = wide.astype(np.float32).astype(bf16)
    low = (wide.astype(np.float32) - high.astype(np.float32)).astype(bf16)
    return jnp.asarray(np.stack([high, low]))


def rotary_tables(places):
    lane = jnp.arange(128) % HEAD
    half = ROT // 2
    inverse = 10000.0 ** (-((lane % half).astype(f32) * 2.0 / ROT))
    inverse = jnp.where(lane < ROT, inverse, 0.0)
    angles = places.astype(f32)[:, None] * inverse[None, :]
    return jnp.stack([jnp.cos(angles), jnp.sin(angles)])


def flip(value, axis, bit):
    size = lax.axis_size(axis)
    return lax.ppermute(value, axis, [(i, i ^ bit) for i in range(size)])


def tie(*values):
    return lax.optimization_barrier(values)


def after(first, x):
    if isinstance(x, Layer):
        return Layer(tie(first, x.array)[1], x.index)
    return tie(first, x)[1]


jax.tree_util.register_pytree_node(
    Layer, lambda x: ((x.array,), x.index), lambda index, leaves: Layer(*leaves, index)
)


def together(*values):
    leaves, tree = jax.tree.flatten(values)
    return jax.tree.unflatten(tree, tie(*leaves))


def exchange(keep, send, flag, core, chip, backward, works=()):
    chips = lax.axis_size("seq") // 2
    begin, span = chip * 2 * LEN, 2 * LEN
    got = flip(send, "seq", 1)
    even, odd = jnp.where(core == 0, keep, got), jnp.where(core == 0, got, keep)
    if backward:
        total = even + flag(begin + LEN - 1, begin) * odd
    else:
        total = odd + flag(begin + span - 1, begin + LEN) * even
    entered, made, step = None, [], 1
    while step < chips:
        other = flip(total, "seq", 2 * step)
        if len(made) < len(works):
            found = works[len(made)](lambda x, total=total: after(total, x))
            leaves, tree = jax.tree.flatten(found)
            other, *leaves = tie(other, *leaves)
            made.append(jax.tree.unflatten(tree, leaves))
        upper = (chip // step) % 2 == 1
        first = chip - chip % (2 * step)
        middle = first + step
        later, earlier = jnp.where(upper, total, other), jnp.where(upper, other, total)
        if backward:
            passed = jnp.where(upper, 0.0, flag(middle * span - 1, (chip + 1) * span))
            total = earlier + flag(middle * span - 1, first * span) * later
        else:
            passed = jnp.where(upper, flag(chip * span - 1, middle * span), 0.0)
            total = later + flag((middle + step) * span - 1, middle * span) * earlier
        entered = passed * other if entered is None else entered + passed * other
        step *= 2
    if backward:
        for_even, for_odd = odd + flag(begin + span - 1, begin + LEN) * entered, entered
    else:
        for_even, for_odd = entered, even + flag(begin + LEN - 1, begin) * entered
    mine = jnp.where(core == 0, for_even, for_odd)
    theirs = flip(jnp.where(core == 0, for_odd, for_even), "seq", 1)
    return (mine, theirs), made


def spread(x):
    return [x] + [flip(x, "batch", bit) for bit in (1, 2, 3)]


class Halving:
    def __init__(self, total):
        self.total, self.step = total, 2

    def send(self):
        return flip(self.total[self.total.shape[0] // 2 :], "seq", self.step)

    def add(self, got):
        self.total = self.total[: self.total.shape[0] // 2] + got
        self.step *= 2

    def finish(self):
        while self.step < lax.axis_size("seq"):
            self.add(self.send())
        return self.total


def join(pieces, size):
    order = np.arange(4) ^ lax.axis_index("batch")
    pieces = [jnp.take(jnp.stack(pieces[k : k + 4]), order, axis=0) for k in range(0, 16, 4)]
    slot = D // size
    made = [[], [], [], []]
    for feed, packed in (pieces[:2], pieces[2:]):
        made[0].append(
            feed[:, :slot].reshape(4, slot, size, slot).transpose(1, 2, 0, 3).reshape(slot, FF)
        )
        made[1].append(feed[:, slot:].reshape(4 * slot, D))
        packed = packed[:, :slot]
        made[2].append(packed[:, :, :384].swapaxes(0, 1).reshape(slot, 3 * D))
        made[3].append(packed[:, :, 384:].swapaxes(0, 1).reshape(slot, D))
    made = [jnp.stack(part) for part in made]
    lines = pieces[1][:2, slot:]
    vectors = lines[:, :, :slot]
    made += [vectors[:, 0:2], vectors[:, 2:4], vectors[:, 4:7].swapaxes(0, 1)]
    return made + [vectors[:, 7], vectors[:, 7], lines[:, 0, 256 : 256 + FF // size]]


def per_device(
    inputs,
    doc_starts,
    cotangent,
    norm_gain,
    norm_bias,
    qkv_weight,
    qkv_bias,
    out_weight,
    out_bias,
    in_weight,
    in_bias,
    down_weight,
    down_bias,
):
    rows, length = inputs.shape[0], inputs.shape[1]
    tokens = rows * length
    size = lax.axis_size("seq")
    me, column = lax.axis_index("seq"), lax.axis_index("batch")
    core, chip = me % 2, me // 2
    def segment_at(position):
        return jnp.max(jnp.where(doc_starts <= position, doc_starts, 0), axis=1)

    def flag(position, limit):
        return (segment_at(position) < limit).astype(f32)[:, None, None]

    dct = Layer(cosine_table())
    masks, tables = call(
        prepare_kernel,
        "prepare",
        [Scalars(doc_starts)],
        [sds((3, rows, LEN, 128)), sds((2, tokens, 128))],
    )
    hidden0 = Layer(inputs.reshape(tokens, D))
    cot = Layer(cotangent.reshape(tokens, D))
    qkv_bias_t, out_bias = Layer(qkv_bias.swapaxes(0, 1)), Layer(out_bias)
    in_bias, down_bias = Layer(in_bias), Layer(down_bias)

    tall, fat = sds((tokens, D)), sds((tokens, D), bf16)
    far, far_low = Far((tokens, D)), Far((tokens, D), bf16)
    packed_state = sds((rows, PACK, 128))
    front_outs = [far_low] * 5 + [far, far, packed_state, packed_state]

    def front_of(layer):
        return [
            Layer(norm_gain, layer),
            Layer(norm_bias, layer),
            Layer(qkv_weight, layer),
            qkv_bias_t,
            tables,
            dct,
        ]

    quarter_wide = FF // size // 4
    feed_weights = [
        [Layer(in_weight, layer), in_bias, Layer(down_weight, layer), down_bias]
        for layer in range(2)
    ]

    def quarter_weights(layer):
        shape = (size, 4, quarter_wide)
        pick = functools.partial(lax.dynamic_index_in_dim, index=column, keepdims=False)
        return [
            pick(in_weight[layer].reshape((D,) + shape), axis=2).reshape(D, D),
            pick(in_bias.array[layer].reshape(shape), axis=1).reshape(1, D),
            pick(down_weight[layer].reshape(shape + (D,)), axis=1).reshape(D, D),
        ]

    def feed_grad(seconds, ups, layer):
        scratch = [pltpu.VMEM((4 * tokens, D), bf16)] * 4 + [pltpu.VMEM((2 * D, D), f32)]
        if quarter_wide == HEAD:
            weights = [Layer(in_weight, layer), in_bias, Layer(down_weight, layer)]
            scratch += [pltpu.VMEM((D, D), bf16), pltpu.VMEM((1, D), f32), pltpu.VMEM((D, D), bf16)]
        else:
            weights = quarter_weights(layer)
        return call(
            functools.partial(feed_grad_kernel, size, layer),
            "feed_grad",
            [*seconds, *ups, *weights],
            [sds((D, D)), Far((D, D))],
            scratch,
        )

    def packed_grad(first, att_low, gp, up, bits, vectors=()):
        rows_of = D // 2 + (size // 2 * 8 if vectors else 0)
        return call(
            functools.partial(packed_grad_kernel, size, bits),
            "packed_grad",
            [first, att_low, gp, up, *vectors],
            [sds((4, rows_of, D // 2)), Far((4, rows_of, D // 2))] * 2,
            [pltpu.VMEM((D, tokens), f32)] * 2,
        )

    first0, second0, fq0, fk0, v0, eq0, ek0, keep, send, wide0, cot_wide = call(
        front_kernel,
        "front",
        [masks, hidden0, cot, *front_of(0)],
        front_outs + [far, far],
    )
    intra_outs = [Far((rows, PAIRS, 2 * LEN, LEN), bf16), tall, tall]

    def near_two(x):
        return [flip(x, "batch", bit) for bit in (1, 2)]

    def last_one(x):
        return flip(x, "batch", 3)

    def do_feed(gate):
        (feed,) = call(feed_kernel, "feed", [gate(second0), *feed_weights[0]], [tall])
        cots.extend(near_two(tie(feed, cot_wide.array)[1]))
        return feed

    def do_intra0(gate):
        made = intra(gate(fq0), fk0, v0)
        cots.append(last_one(tie(made[1], cot_wide.array)[1]))
        return made, cots[:2]

    cots = []

    def intra(fq, fk, v):
        return call(intra_kernel, "intra", [masks, fq, fk, v], intra_outs)

    entered0, made = exchange(
        keep, send, flag, core, chip, False, [do_feed, do_intra0]
    )
    feed0, ((scores0, num0, kt0), cots[:2]) = made
    (
        den0, att0, att_low0, hidden1, first1, second1, fq1, fk1, v1, eq1, ek1, keep, send, wide1,
    ) = call(
        middle_kernel,
        "middle",
        [masks, num0, kt0, fq0, *entered0, Layer(out_weight, 0), out_bias]
        + [hidden0, feed0, *front_of(1)],
        [far, far, far_low, far] + front_outs + [far],
    )
    row, wide_row = Far((1, D)), Far((1, FF))

    def feed_back(layer, second, up_low, up, hidden, more):
        return call(
            functools.partial(feed_back_kernel, layer),
            "feed_back",
            [second, *feed_weights[layer], up_low, up, hidden, Layer(norm_gain, layer)],
            [tall, row, row, wide_row] + more,
        )

    def do_intra1(gate):
        made = intra(gate(fq1), fk1, v1)
        seconds1.extend(near_two(tie(made[1], wide1.array)[1]))
        return made, cots[2]

    def do_feed_back1(gate):
        made = feed_back(1, gate(second1), cot, cot, hidden1, [far])
        return made, seconds1[:2]

    seconds1 = []
    entered1, made = exchange(
        keep, send, flag, core, chip, False, [do_intra1, do_feed_back1]
    )
    ((scores1, num1, kt1), cots[2]) = made[0]
    ((base1, sgain1, sshift1, gib1, feed1), seconds1[:2]) = made[1]
    seconds1.append(last_one(tie(base1, wide1.array)[1]))
    att_low1, gnum1, gden1, keep, send = call(
        turn_kernel,
        "turn",
        [masks, num1, kt1, fq1, *entered1, Layer(out_weight, 1), cot],
        [far_low, fat, tall, packed_state, packed_state],
        [pltpu.VMEM((tokens, D), f32)] * 2,
    )

    def intra_back(fq, fk, v, scores, gnum, gden, entered, eq):
        return call(
            intra_back_kernel,
            "intra_back",
            [masks, fq, fk, v, scores, gnum, gden, *entered, eq, tables, dct],
            [fat, tall, tall],
        )

    def do_intra_back1(gate):
        made = intra_back(gate(fq1), fk1, v1, scores1, gnum1, gden1, entered1, eq1)
        seconds0.extend(near_two(tie(made[1], wide0.array)[1]))
        return made

    def do_seconds(gate):
        seconds0.append(last_one(gate(wide0.array)))
        return seconds1[2], seconds0[:2]

    seconds0 = []
    (mine, theirs), made = exchange(
        keep, send, flag, core, chip, True, [do_intra_back1, do_seconds]
    )
    (gq1, gfk1, gval1), (seconds1[2], seconds0[:2]) = made
    vector_outs = [Far((1, 3 * D)), row, row]
    packed = sds((tokens, 3 * D), bf16)
    gp1, gqb1, ggain1, gshift1, up0, up_low0, gnum0, gden0, keep, send = call(
        turn_back_kernel,
        "turn_back",
        [masks, mine, theirs, gfk1, gval1, fk1, v1, ek1, tables, dct, gq1]
        + [Layer(qkv_weight, 1), hidden1, Layer(norm_gain, 1), base1]
        + [Layer(out_weight, 0), den0, att0, fq0],
        [packed, *vector_outs, tall, fat, fat, tall, packed_state, packed_state],
    )
    ups0 = [up0]

    def do_feed_back(gate):
        ups0.extend(flip(gate(up0), "batch", bit) for bit in (1, 2))
        return feed_back(0, second0, gate(up_low0), up0, hidden0, []), seconds0[2]

    def do_intra_back0(gate):
        ups0.append(flip(gate(up0), "batch", 3))
        return (
            intra_back(gate(fq0), fk0, v0, scores0, gnum0, gden0, entered0, eq0),
            packed_grad(gate(first1), att_low1, gp1, cot, (1, 2)),
            ups0[1:3],
        )

    (mine, theirs), made = exchange(
        keep, send, flag, core, chip, True, [do_feed_back, do_intra_back0]
    )
    ((base0, sgain0, sshift0, gib0), seconds0[2]), ((gq0, gfk0, gval0), parts1, ups0[1:3]) = made
    keep1a, send1a, keep1b, send1b = parts1
    got1a, got1b = flip(send1a.array, "seq", 1), flip(send1b.array, "seq", 1)
    mine, theirs, got1a, got1b = tie(mine, theirs, got1a, got1b)
    gp0, gqb0, ggain0, gshift0, ginputs = call(
        last_kernel,
        "last",
        [masks, mine, theirs, gfk0, gval0, fk0, v0, ek0, tables, dct, gq0]
        + [Layer(qkv_weight, 0), hidden0, Layer(norm_gain, 0), base0],
        [packed, *vector_outs, far],
    )
    vectors = (ggain0, sgain0, gshift0, sshift0, gqb0, gib0)
    vectors += (ggain1, sgain1, gshift1, sshift1, gqb1, gib1, cot)
    made = packed_grad(first0, att_low0, gp0, up_low0, (1, 2), vectors)
    first1a = flip(keep1a[2:] + got1a[2:], "batch", 1)
    made, grads1, ups0[3], first1a = together(
        made,
        feed_grad([wide1, *seconds1], [cot_wide, *cots], 1),
        ups0[3],
        first1a,
    )
    keep0a, send0a, keep0b, send0b = made
    feed_keep1, feed_send1 = grads1
    got0a, got0b = flip(send0a.array, "seq", 1), flip(send0b.array, "seq", 1)
    feed_got1 = flip(feed_send1.array, "seq", 1)
    grads0, got0a, got0b, feed_got1 = together(
        feed_grad([wide0, *seconds0], ups0, 0), got0a, got0b, feed_got1
    )
    feed_keep0, feed_send0 = grads0
    feed_got0 = flip(feed_send0.array, "seq", 1)
    feed1_sum = Halving(feed_keep1 + feed_got1)
    got_feed1 = feed1_sum.send()
    first1b = flip(keep1b[2:] + got1b[2:], "batch", 2)
    first0a = flip(keep0a[2:] + got0a[2:], "batch", 1)
    first0b = flip(keep0b[2:] + got0b[2:], "batch", 2)
    (result,) = call(
        result_kernel,
        "result",
        [hidden1, feed1, att_low1, Layer(out_weight, 1), out_bias],
        [far_low],
    )
    feed_got0, got_feed1, first0a, first0b, first1b, result = together(
        feed_got0, got_feed1, first0a, first0b, first1b, result
    )
    feed1_sum.add(got_feed1)
    got_feed1 = feed1_sum.send()
    feed0 = Halving(feed_keep0 + feed_got0)
    got_feed0 = feed0.send()
    second0a = flip(keep0a[1] + got0a[1] + first0a[1], "batch", 2)
    second0b = flip(keep0b[1] + got0b[1] + first0b[1], "batch", 1)
    second1a = flip(keep1a[1] + got1a[1] + first1a[1], "batch", 2)
    second1b = flip(keep1b[1] + got1b[1] + first1b[1], "batch", 1)
    got_feed1, got_feed0, second0a, second0b, second1a, second1b = tie(
        got_feed1, got_feed0, second0a, second0b, second1a, second1b
    )

    def total_of(keeps, gots, firsts, seconds):
        parts = [k[0] + g[0] + a[0] + b for k, g, a, b in zip(keeps, gots, firsts, seconds)]
        return Halving(jnp.concatenate(parts, axis=1))

    feed1_sum.add(got_feed1)
    feed1_all = spread(feed1_sum.finish())
    feed0.add(got_feed0)
    got_feed0 = feed0.send()
    packed0 = total_of((keep0a, keep0b), (got0a, got0b), (first0a, first0b), (second0a, second0b))
    packed1 = total_of((keep1a, keep1b), (got1a, got1b), (first1a, first1b), (second1a, second1b))
    got_packed0, got_packed1 = packed0.send(), packed1.send()
    feed1_all[1:], got_feed0, got_packed0, got_packed1 = together(
        feed1_all[1:], got_feed0, got_packed0, got_packed1
    )
    feed0.add(got_feed0)
    feed0_all = spread(feed0.finish())
    packed0.add(got_packed0)
    packed1.add(got_packed1)
    got_packed0, got_packed1 = packed0.send(), packed1.send()
    feed0_all[1:], got_packed0, got_packed1 = together(feed0_all[1:], got_packed0, got_packed1)
    packed0.add(got_packed0)
    packed1.add(got_packed1)
    pieces = feed0_all + spread(packed0.finish()) + feed1_all + spread(packed1.finish())
    slot = D // size
    outs = [
        Far((2, slot, FF)),
        Far((2, FF // size, D)),
        Far((2, slot, 3 * D)),
        Far((2, slot, D)),
        Far((2, 2, slot)),
        Far((2, 2, slot)),
        Far((3, 2, slot)),
        Far((2, slot)),
        Far((2, slot)),
        Far((2, FF // size)),
    ]
    if quarter_wide == HEAD:
        joined = [x.array for x in call(join_kernel, "join", pieces, outs)]
    else:
        joined = join(pieces, size)
    grad_in, grad_down, grad_qkv, grad_out, gain, shift, grad_qkv_b, out_b, down_b, in_b = joined
    return (
        result.array.reshape(rows, length, D),
        ginputs.array.reshape(rows, length, D),
        gain,
        shift,
        grad_qkv,
        grad_qkv_b.swapaxes(0, 1),
        grad_out,
        out_b,
        grad_in,
        in_b,
        grad_down,
        down_b,
    )


def solution(mesh):
    placed = (
        P("batch", "seq", None),
        P("batch", None),
        P("batch", "seq", None),
        P(),
        P(),
        P(),
        P(),
        P(),
        P(),
        P(),
        P(),
        P(),
        P(),
    )
    return jax.shard_map(
        per_device,
        mesh=mesh,
        in_specs=placed,
        out_specs=(
            P("batch", "seq", None),
            P("batch", "seq", None),
            P(None, None, "seq"),
            P(None, None, "seq"),
            P(None, "seq", None),
            P(None, None, "seq"),
            P(None, "seq", None),
            P(None, "seq"),
            P(None, "seq", None),
            P(None, "seq"),
            P(None, "seq", None),
            P(None, "seq"),
        ),
        check_vma=False,
    )
```

```python
import functools
import math

import jax
import jax.numpy as jnp
import numpy as np
from jax import lax
from jax.experimental import pallas as pl
from jax.experimental.pallas import tpu as pltpu
from jax.sharding import PartitionSpec as P

D = 512
HEADS = 8
HEAD = 64
FF = 2048
ROT = 16
LAYERS = 2
NDOC = 4
LEN = 128
PAIRS = HEADS // 2
PACK = 2 * HEAD + 8
WIDE = 512

epsilon = 1e-05
f32, bf16 = jnp.float32, jnp.bfloat16
NN = (((1,), (0,)), ((), ()))
NT = (((1,), (1,)), ((), ()))
TN = (((0,), (0,)), ((), ()))


def dot(a, b, dims=NN):
    return lax.dot_general(a, b, dims, preferred_element_type=f32)


def split(x):
    high = x.astype(bf16)
    return high, (x - high.astype(f32)).astype(bf16)


def sds(shape, dtype=f32):
    return jax.ShapeDtypeStruct(shape, dtype)


def norm_parts(hidden):
    centred = hidden - jnp.mean(hidden, axis=-1, keepdims=True)
    variance = jnp.mean(centred * centred, axis=-1, keepdims=True)
    inverse = lax.rsqrt(variance + epsilon)
    return centred * inverse, inverse


def segment_of(position, starts, row):
    found = jnp.zeros_like(position)
    for k in range(NDOC):
        entry = starts[row, k]
        found = jnp.maximum(found, jnp.where(entry <= position, entry, 0))
    return found


def prepare(starts, masks, tables):
    begin = lax.axis_index("seq") * LEN
    for row in range(masks.shape[1]):
        at_i = begin + lax.broadcasted_iota(jnp.int32, (LEN, 128), 0)
        at_j = begin + lax.broadcasted_iota(jnp.int32, (LEN, 128), 1)
        seg_i, seg_j = segment_of(at_i, starts, row), segment_of(at_j, starts, row)
        last = jnp.int32(0)
        for k in range(NDOC):
            entry = starts[row, k]
            last = jnp.maximum(last, jnp.where(entry <= begin + (LEN - 1), entry, 0))
        masks[0, row] = jnp.where((at_j <= at_i) & (seg_i == seg_j), 1.0, 0.0).astype(f32)
        masks[1, row] = jnp.where(seg_i < begin, 1.0, 0.0).astype(f32)
        masks[2, row] = jnp.where(seg_i == last, 1.0, 0.0).astype(f32)
        lane = lax.broadcasted_iota(jnp.int32, (LEN, 128), 1) % HEAD
        inverse = jnp.exp((lane % (ROT // 2)).astype(f32) * (-2.0 / ROT * math.log(10000.0)))
        angles = (at_i - seg_i).astype(f32) * jnp.where(lane < ROT, inverse, 0.0)
        at = slice(row * LEN, (row + 1) * LEN)
        tables[0, at] = jnp.cos(angles)
        tables[1, at] = jnp.sin(angles)


def masks_of(row, masks):
    return masks[0, row], masks[1, row], masks[2, row]


def low_lanes(rows):
    return lax.broadcasted_iota(jnp.int32, (rows, 128), 1) < HEAD


def read_tables(tables):
    sine = tables[1]
    lane = lax.broadcasted_iota(jnp.int32, sine.shape, 1) % HEAD
    ahead = jnp.where(lane < ROT // 2, -sine, 0.0)
    behind = jnp.where((lane >= ROT // 2) & (lane < ROT), sine, 0.0)
    return tables[0], ahead, behind


def rotate(x, tables):
    base, ahead, behind = tables
    return x * base + pltpu.roll(x, 120, 1) * ahead + pltpu.roll(x, 8, 1) * behind


def rotate_back(g, tables):
    base, ahead, behind = tables
    return g * base + pltpu.roll(g * ahead, 8, 1) + pltpu.roll(g * behind, 120, 1)


def featurize(x, tables, high, low):
    pieces = [rotate(x[:, g * 128 : (g + 1) * 128], tables) for g in range(4)]
    found = []
    for g in range(2):
        a, b = split(jnp.concatenate(pieces[2 * g : 2 * g + 2], axis=1))
        found.append(jnp.exp(dot(a, high) + dot(b, high) + dot(a, low)))
    return jnp.concatenate(found, axis=1)


def unfeaturize(g, tables, high, low):
    found = []
    for k in range(2):
        a, b = split(g[:, k * 256 : (k + 1) * 256])
        back = dot(a, high, NT) + dot(b, high, NT) + dot(a, low, NT)
        found += [rotate_back(back[:, :128], tables), rotate_back(back[:, 128:], tables)]
    return jnp.concatenate(found, axis=1)


def head_ones():
    across = lax.broadcasted_iota(jnp.int32, (256, 256), 0) // HEAD
    along = lax.broadcasted_iota(jnp.int32, (256, 256), 1) // HEAD
    return jnp.where(across == along, 1.0, 0.0).astype(bf16)


def head_sum(x, ones):
    found = []
    for g in range(2):
        a, b = split(x[:, g * 256 : (g + 1) * 256])
        found.append(dot(a, ones) + dot(b, ones))
    return jnp.concatenate(found, axis=1)


def store_halves(keep_ref, send_ref, halves):
    def put(ref, half):
        for row, at, value in halves[half]:
            ref[row, at[0] : at[1], :] = value

    core = lax.axis_index("seq") % 2
    for mine in range(2):

        @pl.when(core == mine)
        def _():
            put(keep_ref, mine)
            put(send_ref, 1 - mine)


def pack_states(rows, left_of, right, norm_of):
    low = low_lanes(HEAD)
    halves = [[], []]
    for row in range(rows):
        at = slice(row * LEN, (row + 1) * LEN)
        left, norm = left_of(row), norm_of(row)
        for pair in range(PAIRS):
            lanes = slice(pair * 128, (pair + 1) * 128)
            both = dot(left[:, lanes], right[at, lanes], TN)
            half, place = pair // 2, pair % 2
            halves[half].append(
                (row, (place * HEAD, (place + 1) * HEAD), jnp.where(low, both[:HEAD], both[HEAD:]))
            )
        for half in range(2):
            pieces = [norm[:, (2 * half + k) * 128 : (2 * half + k + 1) * 128] for k in range(2)]
            block = jnp.concatenate(pieces + [jnp.zeros((6, 128), f32)], axis=0)
            halves[half].append((row, (2 * HEAD, PACK), block))
    return halves


def unpack_state(mine_ref, theirs_ref, row):
    low = low_lanes(HEAD)
    blocks, norms = [], []
    for half in range(2):
        here = lax.axis_index("seq") % 2 == half
        packed = jnp.where(here, mine_ref[row], theirs_ref[row])
        for place in range(2):
            state = packed[place * HEAD : (place + 1) * HEAD]
            both = jnp.concatenate(
                [jnp.where(low, state, 0.0), jnp.where(low, 0.0, state)], axis=0
            )
            blocks.append(split(both))
            norms.append(packed[2 * HEAD + place : 2 * HEAD + place + 1])
    return blocks, jnp.concatenate(norms, axis=1)


def cross_dot(x, block, dims=NN):
    return dot(x, block[0], dims) + dot(x, block[1], dims)


def gelu_parts(lifted):
    phi = 0.5 + 0.5 * lax.erf(lifted * math.sqrt(0.5))
    slope = phi + lifted * (jnp.exp(-0.5 * lifted * lifted) * (1.0 / math.sqrt(2.0 * math.pi)))
    return lifted * phi, slope


def norm_back(grad, xhat, inverse, gain):
    u = grad * gain
    mean_u = jnp.mean(u, axis=-1, keepdims=True)
    mean_ux = jnp.mean(u * xhat, axis=-1, keepdims=True)
    down = (u - mean_u - xhat * mean_ux) * inverse
    return down, jnp.sum(grad * xhat, axis=0, keepdims=True), jnp.sum(grad, axis=0, keepdims=True)


def front_body(layer, masks, hidden, gain, shift, w, b, tables, dct, outs):
    first_ref, second_ref, fq_ref, fk_ref, v_ref, eq_ref, ek_ref, keep_ref, send_ref, *_ = outs
    xhat, _ = norm_parts(hidden)
    gains, shifts = gain[...].astype(f32), shift[...].astype(f32)
    first = (xhat * gains[0:1] + shifts[0:1]).astype(bf16)
    first_ref[...] = first
    second_ref[...] = (xhat * gains[1:2] + shifts[1:2]).astype(bf16)
    bias = [b[k][layer : layer + 1].astype(f32) for k in range(3)]
    tabs = read_tables(tables)
    high, low = dct[0], dct[1]
    keys = dot(first, w[:, D : 2 * D]) + bias[1]
    values = (dot(first, w[:, 2 * D :]) + bias[2]).astype(bf16)
    v_ref[...] = values
    exp_k = featurize(keys, tabs, high, low)
    ek_ref[...] = exp_k
    feat_k = exp_k.astype(bf16)
    fk_ref[...] = feat_k
    rows = hidden.shape[0] // LEN
    wide = feat_k.astype(f32)

    def tailed(row):
        tail = masks_of(row, masks)[2]
        return wide[row * LEN : (row + 1) * LEN] * jnp.concatenate([tail] * 4, axis=1)

    kept = [tailed(row) for row in range(rows)]
    halves = pack_states(
        rows,
        lambda row: kept[row].astype(bf16),
        values,
        lambda row: jnp.sum(kept[row], axis=0, keepdims=True),
    )
    store_halves(keep_ref, send_ref, halves)
    queries = dot(first, w[:, :D]) + bias[0]
    exp_q = featurize(queries, tabs, high, low)
    eq_ref[...] = exp_q
    fq_ref[...] = exp_q.astype(bf16)


def front_kernel(starts, h, cot, gain, shift, w, b, dct, *outs):
    *outs, masks, tables = outs
    prepare(starts, masks, tables)
    hidden = h[...].astype(f32)
    front_body(0, masks, hidden, gain, shift, w, b, tables, dct, outs[:9])
    outs[9][...] = outs[1][...].astype(f32)
    outs[10][...] = cot[...].astype(f32)


def attend(masks, num_ref, kt_ref, fq_ref, mine_ref, theirs_ref, den_ref, att_ref, low_ref):
    rows = num_ref.shape[0] // LEN
    ones = head_ones()
    for row in range(rows):
        at = slice(row * LEN, (row + 1) * LEN)
        cross = masks_of(row, masks)[1]
        cross4 = jnp.concatenate([cross] * 4, axis=1)
        blocks, norm = unpack_state(mine_ref, theirs_ref, row)
        fq = fq_ref[at]
        far = jnp.concatenate(
            [cross_dot(fq[:, p * 128 : (p + 1) * 128], blocks[p]) for p in range(PAIRS)], axis=1
        )
        num = num_ref[at] + cross4 * far
        den = head_sum(fq.astype(f32) * (kt_ref[at] + cross4 * norm), ones)
        att = num / den
        den_ref[at] = den
        att_ref[at] = att
        low_ref[at] = att.astype(bf16)
    begin_writing(den_ref, att_ref, low_ref)


def middle_kernel(
    masks, num, kt, fq0, mine, theirs, ow, ob, h, feed, gain, shift, w, b, tables, dct,
    den, att, att_low, h2, *outs,
):
    attend(masks, num, kt, fq0, mine, theirs, den, att, att_low)
    hidden = h[...].astype(f32) + (dot(att_low[...], ow[...]) + ob[0:1].astype(f32)) + feed[...]
    h2[...] = hidden
    front_body(1, masks, hidden, gain, shift, w, b, tables, dct, outs)
    outs[9][...] = outs[1][...].astype(f32)


def attend_back(masks, up, ow, den, att, fq, gnum, gden, keep_ref, send_ref):
    ga = dot(up, ow[...], NT)
    den_v = den[...]
    gn = (ga / den_v).astype(bf16)
    gnum[...] = gn
    gd = -head_sum(ga * att[...], head_ones()) / den_v
    gden[...] = gd
    rows = up.shape[0] // LEN
    wide = fq[...].astype(f32)

    def crossed(row):
        cross = masks_of(row, masks)[1]
        return wide[row * LEN : (row + 1) * LEN] * jnp.concatenate([cross] * 4, axis=1)

    kept = [crossed(row) for row in range(rows)]
    halves = pack_states(
        rows,
        lambda row: kept[row].astype(bf16),
        gn,
        lambda row: jnp.sum(kept[row] * gd[row * LEN : (row + 1) * LEN], axis=0, keepdims=True),
    )
    store_halves(keep_ref, send_ref, halves)


def turn_kernel(
    masks, num, kt, fq, mine, theirs, ow, cot, att_low, gnum, gden, keep, send, den, att,
):
    attend(masks, num, kt, fq, mine, theirs, den, att, att_low)
    attend_back(masks, cot[...], ow, den, att, fq, gnum, gden, keep, send)


def feed_kernel(second, iw, ib, dw, db, feed):
    total = jnp.broadcast_to(db[0:1].astype(f32), feed.shape)
    for g in range(FF // WIDE):
        lanes = slice(g * WIDE, (g + 1) * WIDE)
        lifted = dot(second[...], iw[:, lanes]) + ib[0:1, lanes].astype(f32)
        total = total + dot(gelu_parts(lifted)[0].astype(bf16), dw[lanes, :])
    feed[...] = total


def feed_back_kernel(layer, second, iw, ib, dw, db, up_low, up, h, gain, *outs):
    base, gain_out, shift_out, gib, *feed = outs
    total = jnp.broadcast_to(db[layer : layer + 1].astype(f32), base.shape)
    back = jnp.zeros(base.shape, f32)
    low_up = up_low[...]
    for g in range(FF // WIDE):
        lanes = slice(g * WIDE, (g + 1) * WIDE)
        lifted = dot(second[...], iw[:, lanes]) + ib[layer : layer + 1, lanes].astype(f32)
        value, slope = gelu_parts(lifted)
        rows = dw[lanes, :]
        if feed:
            total = total + dot(value.astype(bf16), rows)
        low = (dot(low_up, rows, NT) * slope).astype(bf16)
        gib[:, lanes] = jnp.sum(low.astype(f32), axis=0, keepdims=True)
        back = back + dot(low, iw[:, lanes], NT)
    if feed:
        feed[0][...] = total
    xhat, inverse = norm_parts(h[...].astype(f32))
    gains = gain[...].astype(f32)
    part, gain_out[...], shift_out[...] = norm_back(back, xhat, inverse, gains[1:2])
    base[...] = up[...].astype(f32) + part


def intra_kernel(masks, fq, fk, v, scores, num, kt):
    low = low_lanes(LEN)
    even = jnp.where(low, 1.0, 0.0).astype(bf16)
    odd = jnp.where(low, 0.0, 1.0).astype(bf16)
    for row in range(fq.shape[0] // LEN):
        at = slice(row * LEN, (row + 1) * LEN)
        intra = masks_of(row, masks)[0]
        kt[at] = dot(intra.astype(bf16), fk[at])
        twice = jnp.concatenate([intra, intra], axis=0)
        for pair in range(PAIRS):
            lanes = slice(pair * 128, (pair + 1) * 128)
            q = fq[at, lanes]
            both = jnp.concatenate([q * even, q * odd], axis=0)
            rounded = (dot(both, fk[at, lanes], NT) * twice).astype(bf16)
            scores[row, pair] = rounded
            out = dot(rounded, v[at, lanes])
            num[at, lanes] = jnp.where(low, out[:LEN], out[LEN:])


def intra_back_kernel(
    masks, fq, fk, v, scores, gnum, gden, mine, theirs, eq, tables, dct, gq, gfk, gval
):
    low = low_lanes(LEN)
    even = jnp.where(low, 1.0, 0.0).astype(bf16)
    odd = jnp.where(low, 0.0, 1.0).astype(bf16)
    grad = []
    for row in range(fq.shape[0] // LEN):
        at = slice(row * LEN, (row + 1) * LEN)
        intra, cross, _ = masks_of(row, masks)
        twice = jnp.concatenate([intra, intra], axis=0)
        blocks, norm = unpack_state(mine, theirs, row)
        queries = []
        for pair in range(PAIRS):
            lanes = slice(pair * 128, (pair + 1) * 128)
            gn, gd, q, k = gnum[at, lanes], gden[at, lanes], fq[at, lanes], fk[at, lanes]
            both = jnp.concatenate([gn * even, gn * odd], axis=0)
            turned = pltpu.roll(gd, HEAD, 1)
            dens = jnp.concatenate(
                [jnp.where(low, gd, turned), jnp.where(low, turned, gd)], axis=0
            )
            gs = ((dot(both, v[at, lanes], NT) + dens) * twice).astype(bf16)
            near = dot(gs, k)
            far = cross_dot(gn, blocks[pair], NT) + gd * norm[:, lanes]
            queries.append(jnp.where(low, near[:LEN], near[LEN:]) + cross * far)
            gfk[at, lanes] = jnp.where(low, dot(gs[:LEN], q, TN), dot(gs[LEN:], q, TN))
            sl = scores[row, pair]
            gval[at, lanes] = jnp.where(low, dot(sl[:LEN], gn, TN), dot(sl[LEN:], gn, TN))
        grad.append(jnp.concatenate(queries, axis=1))
    begin_writing(gfk, gval)
    turned = unfeaturize(
        jnp.concatenate(grad, axis=0) * eq[...], read_tables(tables), dct[0], dct[1]
    )
    gq[...] = turned.astype(bf16)


def packed_back(masks, mine, theirs, gq, gfk, gval, fk, v, ek, tables, dct, gp, gqb):
    keys, values = [], []
    for row in range(fk.shape[0] // LEN):
        at = slice(row * LEN, (row + 1) * LEN)
        tail = masks_of(row, masks)[2]
        blocks, norm = unpack_state(mine, theirs, row)
        key_row, value_row = [], []
        for pair in range(PAIRS):
            lanes = slice(pair * 128, (pair + 1) * 128)
            far = cross_dot(v[at, lanes], blocks[pair], NT) + norm[:, lanes]
            key_row.append(gfk[at, lanes] + tail * far)
            value_row.append(gval[at, lanes] + tail * cross_dot(fk[at, lanes], blocks[pair]))
        keys.append(jnp.concatenate(key_row, axis=1))
        values.append(jnp.concatenate(value_row, axis=1))
    gp[:, 2 * D :] = jnp.concatenate(values, axis=0).astype(bf16)
    gp[:, :D] = gq[...]
    keys = unfeaturize(
        jnp.concatenate(keys, axis=0) * ek[...], read_tables(tables), dct[0], dct[1]
    )
    gp[:, D : 2 * D] = keys.astype(bf16)
    gqb[...] = jnp.sum(gp[...].astype(f32), axis=0, keepdims=True)


def upstream_back(base, hidden, gp, w, gain, gain_out, shift_out):
    gfirst = dot(gp[...], w[...], NT)
    xhat, inverse = norm_parts(hidden)
    part, gain_out[...], shift_out[...] = norm_back(
        gfirst, xhat, inverse, gain[...].astype(f32)[0:1]
    )
    return base[...] + part


def turn_back_kernel(
    masks, mine, theirs, gfk, gval, fk, v, ek, tables, dct, gq, w, h, gain, base, ow, den, att, fq,
    gp, gqb, ggain, gshift, up_ref, up_low, gnum, gden, keep, send,
):
    packed_back(masks, mine, theirs, gq, gfk, gval, fk, v, ek, tables, dct, gp, gqb)
    up = upstream_back(base, h[...], gp, w, gain, ggain, gshift)
    up_ref[...] = up
    low = up.astype(bf16)
    up_low[...] = low
    attend_back(masks, low, ow, den, att, fq, gnum, gden, keep, send)


def result_kernel(h, feed, att_low, ow, ob, result):
    hidden = h[...] + (dot(att_low[...], ow[...]) + ob[1:2].astype(f32)) + feed[...]
    result[...] = hidden.astype(bf16)


def last_kernel(
    masks, mine, theirs, gfk, gval, fk, v, ek, tables, dct, gq, w, h, gain, base,
    gp, gqb, ggain, gshift, ginputs,
):
    packed_back(masks, mine, theirs, gq, gfk, gval, fk, v, ek, tables, dct, gp, gqb)
    ginputs[...] = upstream_back(base, h[...].astype(f32), gp, w, gain, ggain, gshift)


def gathered(size, x, flat, held):
    block = flat.shape[0] // size
    flat[...] = x.astype(f32).T
    for place in range(size):
        source = block_at(size, place)
        held[place * block : (place + 1) * block, :] = flat[
            pl.ds(pl.multiple_of(source * block, block), block), :
        ]
    return held[...].astype(bf16)


def reversed_bits(value, count):
    return sum(((value >> k) & 1) << (count - 1 - k) for k in range(count))


def block_at(size, place):
    return reversed_bits(place, size.bit_length() - 1) ^ lax.axis_index("seq")


def pick_quarter(size, layer, q, iw, ib, dw, iw_q, ib_q, dw_q):
    wide = FF // size
    rows = lax.broadcasted_iota(jnp.int32, (128, 128), 0) - HEAD * (q % 2)
    lanes = lax.broadcasted_iota(jnp.int32, (128, 128), 1)
    left = jnp.where((rows == lanes) & (lanes < HEAD), 1.0, 0.0).astype(bf16)
    right = jnp.where((rows == lanes - HEAD) & (lanes >= HEAD), 1.0, 0.0).astype(bf16)
    for pair in range(size // 2):
        at = [
            pl.ds(pl.multiple_of((2 * pair + k) * wide + (q // 2) * 128, 128), 128)
            for k in range(2)
        ]
        here = slice(pair * 128, (pair + 1) * 128)
        iw_q[:, here] = (dot(iw[:, at[0]], left) + dot(iw[:, at[1]], right)).astype(bf16)
        bias = [ib[:, at[k]] for k in range(2)]
        ib_q[:, here] = (dot(bias[0], left) + dot(bias[1], right))[layer : layer + 1]
    quarter = wide // 4
    for s in range(size):
        rows = pl.ds(pl.multiple_of(s * wide + q * quarter, quarter), quarter)
        dw_q[s * quarter : (s + 1) * quarter, :] = dw[rows, :]


def feed_grad_kernel(size, layer, groups, quarters, *refs):
    count = len(quarters)
    seconds, ups, refs = refs[:groups], refs[groups : 2 * groups], refs[2 * groups :]
    own = FF // size // 4 == HEAD
    weights = refs[: 3 if own else 3 * count]
    keep, send, s_all, u_all, act, lift, out, *picked = refs[len(weights) :]
    tokens = s_all.shape[0] // groups
    block = D // size
    for n, quarter in enumerate(quarters):
        if own:
            pick_quarter(size, layer, lax.axis_index("batch") ^ quarter, *weights, *picked)
            iw, ib, dw = picked
        else:
            iw, ib, dw = weights[3 * n : 3 * n + 3]
        for k in range(groups):
            at = slice(k * tokens, (k + 1) * tokens)
            if n == 0:
                s_all[at], u_all[at] = seconds[k][...].astype(bf16), ups[k][...].astype(bf16)
            lifted = dot(s_all[at], iw[...]) + ib[...].astype(f32)
            value, slope = gelu_parts(lifted)
            act[at] = value.astype(bf16)
            lift[at] = (dot(u_all[at], dw[...], NT) * slope).astype(bf16)
        for part, grads in enumerate(
            (dot(s_all[...], lift[...], TN), dot(act[...], u_all[...], TN))
        ):
            for s in range(size):
                place = reversed_bits(s ^ lax.axis_index("seq"), size.bit_length() - 1)
                at = pl.multiple_of((2 * place + part) * block, block)
                out[pl.ds(at, block), :] = grads[s * block : (s + 1) * block]
        keep[n], send[n] = out[:D], out[D:]


def chosen(refs, index):
    value = refs[0][...]
    for k in range(1, len(refs)):
        value = jnp.where(index == k, refs[k][...], value)
    return value


def join_kernel(*refs):
    feed0, x0, y0, feed1, x1, *pieces = refs[:9]
    outs = refs[9:]
    me = lax.axis_index("batch")
    in_out, down_out, qkv_out, out_out, gain_out, shift_out, qkvb_out = outs[:7]
    outb_out, downb_out, inb_out = outs[7:]
    block = in_out.shape[1]
    low = low_lanes(block)
    for layer in range(2):
        two = 2 * block
        if layer == 0:
            held = (feed0, x0, y0.at[:two], y0.at[two:])
        else:
            held = (feed1.at[:two], x1.at[:two], feed1.at[two:], x1.at[two:])
        begin = layer * (block + 8)
        for q in range(4):
            packed = chosen(pieces, q ^ me)[begin : begin + block + 8 * (1 - layer)]
            qkv_out[layer, :, q * 384 : (q + 1) * 384] = packed[:block, :384]
            out_out[layer, :, q * 128 : (q + 1) * 128] = packed[:block, 384:]
            if layer == 0 and q < 2:
                lines = packed[block:]
                gain_out[q] = lines[0:2, :block]
                shift_out[q] = lines[2:4, :block]
                for k in range(3):
                    qkvb_out[k, q : q + 1, :] = lines[4 + k : 5 + k, :block]
                outb_out[q : q + 1, :] = lines[7:8, :block]
                downb_out[q : q + 1, :] = lines[7:8, :block]
                inb_out[q : q + 1, :] = lines[0:1, 256 : 256 + inb_out.shape[1]]
        for pair in range(2):
            left, right = (chosen(held, (2 * pair + k) ^ me) for k in range(2))
            down_out[layer, 2 * pair * block : (2 * pair + 1) * block, :] = left[block:]
            down_out[layer, (2 * pair + 1) * block : (2 * pair + 2) * block, :] = right[block:]
            for tile in range(D // 128):
                lanes = slice(tile * 128, (tile + 1) * 128)
                a, b = left[:block, lanes], right[:block, lanes]
                at = 2 * tile * 256 + pair * 128
                in_out[layer, :, at : at + 128] = jnp.where(low, a, pltpu.roll(b, 64, 1))
                in_out[layer, :, at + 256 : at + 384] = jnp.where(low, pltpu.roll(a, 64, 1), b)


PARTS = ((0, 256), (256, 512))


def standing(quarter, bit):
    return jnp.where(bit == 1, (quarter % 2) * 2 + quarter // 2, quarter)


def packed_grad_kernel(size, bits, first, att_low, gp, up, *refs):
    *vectors, keep_a, send_a, keep_b, send_b, f1, h1 = refs
    block, under = D // size, 8 if vectors else 0
    half, me = size // 2, lax.axis_index("batch")
    for source, right, wide, begin in ((first, gp, 384, 0), (att_low, up, 128, 384)):
        left = gathered(size, source[...], f1, h1)
        for q in range(4):
            out = dot(left, right[:, q * wide : (q + 1) * wide])
            for (low, high), bit, refs in zip(PARTS, bits, ((keep_a, send_a), (keep_b, send_b))):
                lanes = max(low, begin), min(high, begin + wide)
                if lanes[0] >= lanes[1]:
                    continue
                at = standing(q ^ me, bit)
                for place in range(size):
                    here = (place % half) * (block + under)
                    refs[place // half][
                        at, here : here + block, lanes[0] - low : lanes[1] - low
                    ] = out[
                        place * block : (place + 1) * block, lanes[0] - begin : lanes[1] - begin
                    ]
    if vectors:
        put_lines(size, bits, vectors, up, ((keep_a, send_a), (keep_b, send_b)))


def put_lines(size, bits, vectors, up, parts):
    block, wide, me = D // size, FF // size, lax.axis_index("batch")
    held = []
    for *norms, gqb, gib, ups in ((*vectors[:6], up), vectors[6:]):
        gob = jnp.sum(ups[...].astype(f32), axis=0, keepdims=True)
        rows = [part[...] for part in norms]
        rows += [gqb[:, k * D : (k + 1) * D] for k in range(3)] + [gob]
        held.append((jnp.concatenate(rows, axis=0), jnp.broadcast_to(gib[...], (8, FF))))
    for place in range(size):
        source = block_at(size, place)
        here = (place % (size // 2)) * (block + 8) + block
        a_ref, b_ref = (refs[place // (size // 2)] for refs in parts)
        for layer, (rows, line) in enumerate(held):
            a_ref[standing(layer ^ me, bits[0]), here : here + 8, :128] = pltpu.roll(
                rows, (D - source * block) % D, 1
            )[:, :128]
            b_ref[standing(layer ^ me, bits[1]), here : here + 8, :] = pltpu.roll(
                line, (FF - source * wide) % FF, 1
            )[:, :256]
            a_ref[standing(layer ^ me, bits[0]), here : here + 8, 128:] = jnp.zeros((8, 128), f32)
        for k in (2, 3):
            for ref, bit in ((a_ref, bits[0]), (b_ref, bits[1])):
                ref[standing(k ^ me, bit), here : here + 8, :] = jnp.zeros((8, 256), f32)


class Layer:
    def __init__(self, array, index=None):
        self.array, self.index = array, index
        self.shape = array.shape if index is None else jax.eval_shape(lambda x: x[index], array).shape


class Far:
    def __init__(self, shape, dtype=f32):
        self.shape, self.dtype = shape, dtype


class Scalars:
    def __init__(self, array):
        self.array = array


class Source:
    def __init__(self, here, there, semaphore):
        self.here, self.copy = here, pltpu.make_async_copy(there, here, semaphore)
        self.shape, self.copying = here.shape, True
        self.copy.start()

    def __getitem__(self, at):
        if self.copying:
            self.copy.wait()
            self.copying = False
        return self.here[at]


class Target:
    def __init__(self, here, there, semaphore):
        self.here, self.copy = here, pltpu.make_async_copy(here, there, semaphore)
        self.shape, self.started = here.shape, False

    def __getitem__(self, at):
        return self.here[at]

    def __setitem__(self, at, value):
        assert not self.started
        self.here[at] = value
        if at is Ellipsis:
            self.start()

    def start(self):
        if not self.started:
            self.copy.start()
            self.started = True


def begin_writing(*results):
    for result in results:
        if isinstance(result, Target):
            result.start()


def call(kernel, name, operands, outs, scratch=()):
    arrays = [getattr(operand, "array", operand) for operand in operands]
    copied = [k for k, operand in enumerate(operands) if isinstance(operand, Layer)]
    written = [k for k, out in enumerate(outs) if isinstance(out, Far)]
    arrays = [
        a
        if isinstance(o, Scalars)
        else pltpu.with_memory_space_constraint(a, pltpu.HBM if isinstance(o, Layer) else pltpu.VMEM)
        for o, a in zip(operands, arrays)
    ]
    vmem, smem = pl.BlockSpec(memory_space=pltpu.VMEM), pl.BlockSpec(memory_space=pltpu.SMEM)
    hbm = pl.BlockSpec(memory_space=pltpu.HBM)
    own = 1 + len(copied) + len(written)

    def body(*refs):
        ins, results = list(refs[: len(operands)]), list(refs[len(operands) :][: len(outs)])
        semaphores, *buffers = refs[len(operands) + len(outs) :]
        for n, k in enumerate(copied):
            index = operands[k].index
            there = ins[k] if index is None else ins[k].at[index]
            ins[k] = Source(buffers[n], there, semaphores.at[n])
        for n, k in enumerate(written):
            n += len(copied)
            results[k] = Target(buffers[n], results[k], semaphores.at[n])
        kernel(*ins, *results, *buffers[own - 1 :])
        assert not any(ins[k].copying for k in copied), name
        for k in written:
            results[k].start()
        for k in written:
            results[k].copy.wait()

    found = pl.pallas_call(
        body,
        name=name,
        in_specs=[
            smem if isinstance(o, Scalars) else hbm if isinstance(o, Layer) else vmem
            for o in operands
        ],
        out_specs=[hbm if isinstance(o, Far) else vmem for o in outs],
        out_shape=[(pltpu.HBM if isinstance(o, Far) else pltpu.VMEM)(o.shape, o.dtype) for o in outs],
        scratch_shapes=[
            pltpu.SemaphoreType.DMA((max(own - 1, 1),)),
            *[pltpu.VMEM(operands[k].shape, arrays[k].dtype) for k in copied],
            *[pltpu.VMEM(outs[k].shape, outs[k].dtype) for k in written],
            *scratch,
        ],
        cost_estimate=pl.CostEstimate(flops=1024, bytes_accessed=1024, transcendentals=0),
        compiler_params=pltpu.CompilerParams(vmem_limit_bytes=26 * 1024 * 1024),
    )(*arrays)
    return [Layer(x) if isinstance(o, Far) else x for x, o in zip(found, outs)]


def cosine_table():
    frequency = np.arange(HEAD, dtype=np.float64)[:, None]
    columns = np.arange(HEAD, dtype=np.float64)[None, :]
    entries = np.cos(math.pi * (2.0 * columns + 1.0) * frequency / (2.0 * HEAD))
    entries = entries * math.sqrt(2.0 / HEAD)
    entries[0] *= math.sqrt(0.5)
    wide = np.kron(np.eye(4), entries.T)
    high = wide.astype(np.float32).astype(bf16)
    low = (wide.astype(np.float32) - high.astype(np.float32)).astype(bf16)
    return jnp.asarray(np.stack([high, low]))


def rotary_tables(places):
    lane = jnp.arange(128) % HEAD
    half = ROT // 2
    inverse = 10000.0 ** (-((lane % half).astype(f32) * 2.0 / ROT))
    inverse = jnp.where(lane < ROT, inverse, 0.0)
    angles = places.astype(f32)[:, None] * inverse[None, :]
    return jnp.stack([jnp.cos(angles), jnp.sin(angles)])


def flip(value, axis, bit):
    size = lax.axis_size(axis)
    return lax.ppermute(value, axis, [(i, i ^ bit) for i in range(size)])


def tie(*values):
    return lax.optimization_barrier(values)


def after(first, x):
    if isinstance(x, Layer):
        return Layer(tie(first, x.array)[1], x.index)
    return tie(first, x)[1]


jax.tree_util.register_pytree_node(
    Layer, lambda x: ((x.array,), x.index), lambda index, leaves: Layer(*leaves, index)
)


def together(*values):
    leaves, tree = jax.tree.flatten(values)
    return jax.tree.unflatten(tree, tie(*leaves))


def exchange(keep, send, flag, core, chip, backward, works=(), beside_core=()):
    chips = lax.axis_size("seq") // 2
    begin, span = chip * 2 * LEN, 2 * LEN
    got = flip(send, "seq", 1)
    if beside_core:
        got, *came = tie(got, *beside_core)
    even, odd = jnp.where(core == 0, keep, got), jnp.where(core == 0, got, keep)
    if backward:
        total = even + flag(begin + LEN - 1, begin) * odd
    else:
        total = odd + flag(begin + span - 1, begin + LEN) * even
    entered, made, step = None, [], 1
    while step < chips:
        other = flip(total, "seq", 2 * step)
        if len(made) < len(works):
            found = works[len(made)](lambda x, total=total: after(total, x))
            leaves, tree = jax.tree.flatten(found)
            other, *leaves = tie(other, *leaves)
            made.append(jax.tree.unflatten(tree, leaves))
        upper = (chip // step) % 2 == 1
        first = chip - chip % (2 * step)
        middle = first + step
        later, earlier = jnp.where(upper, total, other), jnp.where(upper, other, total)
        if backward:
            passed = jnp.where(upper, 0.0, flag(middle * span - 1, (chip + 1) * span))
            total = earlier + flag(middle * span - 1, first * span) * later
        else:
            passed = jnp.where(upper, flag(chip * span - 1, middle * span), 0.0)
            total = later + flag((middle + step) * span - 1, middle * span) * earlier
        entered = passed * other if entered is None else entered + passed * other
        step *= 2
    if backward:
        for_even, for_odd = odd + flag(begin + span - 1, begin + LEN) * entered, entered
    else:
        for_even, for_odd = entered, even + flag(begin + LEN - 1, begin) * entered
    mine = jnp.where(core == 0, for_even, for_odd)
    theirs = flip(jnp.where(core == 0, for_odd, for_even), "seq", 1)
    return (mine, theirs), made + ([came] if beside_core else [])


def spread(x):
    return [x] + [flip(x, "batch", bit) for bit in (1, 2, 3)]


class Halving:
    def __init__(self, total):
        self.total, self.step = total, 2

    def send(self):
        return flip(self.total[self.total.shape[0] // 2 :], "seq", self.step)

    def tail(self):
        return self.total[self.total.shape[0] // 2 :]

    def add(self, got):
        self.total = self.total[: self.total.shape[0] // 2] + got
        self.step *= 2

    def finish(self):
        while self.step < lax.axis_size("seq"):
            self.add(self.send())
        return self.total


def join(pieces, size):
    order = np.arange(4) ^ lax.axis_index("batch")
    slot = D // size
    feed0, x0, y0, feed1, x1, *packed = pieces
    feed0 = [feed0, x0, y0[: 2 * slot], y0[2 * slot :]]
    feed1 = [feed1[: 2 * slot], x1[: 2 * slot], feed1[2 * slot :], x1[2 * slot :]]
    pieces = [jnp.take(jnp.stack(part), order, axis=0) for part in (feed0, feed1, packed)]
    pieces = [pieces[0], pieces[2][:, : slot + 8], pieces[1], pieces[2][:, slot + 8 :]]
    slot = D // size
    made = [[], [], [], []]
    for feed, packed in (pieces[:2], pieces[2:]):
        made[0].append(
            feed[:, :slot].reshape(4, slot, size, slot).transpose(1, 2, 0, 3).reshape(slot, FF)
        )
        made[1].append(feed[:, slot:].reshape(4 * slot, D))
        packed = packed[:, :slot]
        made[2].append(packed[:, :, :384].swapaxes(0, 1).reshape(slot, 3 * D))
        made[3].append(packed[:, :, 384:].swapaxes(0, 1).reshape(slot, D))
    made = [jnp.stack(part) for part in made]
    lines = pieces[1][:2, slot:]
    vectors = lines[:, :, :slot]
    made += [vectors[:, 0:2], vectors[:, 2:4], vectors[:, 4:7].swapaxes(0, 1)]
    return made + [vectors[:, 7], vectors[:, 7], lines[:, 0, 256 : 256 + FF // size]]


def per_device(
    inputs,
    doc_starts,
    cotangent,
    norm_gain,
    norm_bias,
    qkv_weight,
    qkv_bias,
    out_weight,
    out_bias,
    in_weight,
    in_bias,
    down_weight,
    down_bias,
):
    rows, length = inputs.shape[0], inputs.shape[1]
    tokens = rows * length
    size = lax.axis_size("seq")
    me, column = lax.axis_index("seq"), lax.axis_index("batch")
    core, chip = me % 2, me // 2
    def segment_at(position):
        return jnp.max(jnp.where(doc_starts <= position, doc_starts, 0), axis=1)

    def flag(position, limit):
        return (segment_at(position) < limit).astype(f32)[:, None, None]

    dct = Layer(cosine_table())
    hidden0 = Layer(inputs.reshape(tokens, D))
    cot = Layer(cotangent.reshape(tokens, D))
    qkv_bias_t, out_bias = Layer(qkv_bias.swapaxes(0, 1)), Layer(out_bias)
    in_bias, down_bias = Layer(in_bias), Layer(down_bias)

    tall, fat = sds((tokens, D)), sds((tokens, D), bf16)
    far, far_low = Far((tokens, D)), Far((tokens, D), bf16)
    packed_state = sds((rows, PACK, 128))
    front_outs = [far_low] * 5 + [far, far, packed_state, packed_state]

    def front_of(layer, *given):
        return [
            Layer(norm_gain, layer),
            Layer(norm_bias, layer),
            Layer(qkv_weight, layer),
            qkv_bias_t,
            *given,
            dct,
        ]

    quarter_wide = FF // size // 4
    feed_weights = [
        [Layer(in_weight, layer), in_bias, Layer(down_weight, layer), down_bias]
        for layer in range(2)
    ]

    def quarter_weights(layer, quarter):
        shape = (size, 4, quarter_wide)
        pick = functools.partial(lax.dynamic_index_in_dim, index=column ^ quarter, keepdims=False)
        return [
            pick(in_weight[layer].reshape((D,) + shape), axis=2).reshape(D, D),
            pick(in_bias.array[layer].reshape(shape), axis=1).reshape(1, D),
            pick(down_weight[layer].reshape(shape + (D,)), axis=1).reshape(D, D),
        ]

    def feed_grad(seconds, ups, layer, quarters):
        groups = len(seconds)
        scratch = [pltpu.VMEM((groups * tokens, D), bf16)] * 4 + [pltpu.VMEM((2 * D, D), f32)]
        if quarter_wide == HEAD:
            weights = [Layer(in_weight, layer), in_bias, Layer(down_weight, layer)]
            scratch += [pltpu.VMEM((D, D), bf16), pltpu.VMEM((1, D), f32), pltpu.VMEM((D, D), bf16)]
        else:
            weights = [w for quarter in quarters for w in quarter_weights(layer, quarter)]
        return call(
            functools.partial(feed_grad_kernel, size, layer, groups, quarters),
            "feed_grad",
            [*seconds, *ups, *weights],
            [sds((len(quarters), D, D)), Far((len(quarters), D, D))],
            scratch,
        )

    def packed_grad(first, att_low, gp, up, bits, vectors=()):
        rows_of = D // 2 + (size // 2 * 8 if vectors else 0)
        return call(
            functools.partial(packed_grad_kernel, size, bits),
            "packed_grad",
            [first, att_low, gp, up, *vectors],
            [sds((4, rows_of, D // 2)), Far((4, rows_of, D // 2))] * 2,
            [pltpu.VMEM((D, tokens), f32)] * 2,
        )

    first0, second0, fq0, fk0, v0, eq0, ek0, keep, send, wide0, cot_wide, *prepared = call(
        front_kernel,
        "front",
        [Scalars(doc_starts), hidden0, cot, *front_of(0)],
        front_outs + [far, far, sds((3, rows, LEN, 128)), sds((2, tokens, 128))],
    )
    masks, tables = prepared
    intra_outs = [Far((rows, PAIRS, 2 * LEN, LEN), bf16), tall, tall]

    def near_two(x):
        return [flip(x, "batch", bit) for bit in (1, 2)]

    def last_one(x):
        return flip(x, "batch", 3)

    def do_feed(gate):
        (feed,) = call(feed_kernel, "feed", [gate(second0), *feed_weights[0]], [tall])
        return feed

    def do_intra0(gate):
        return intra(gate(fq0), fk0, v0), cots

    cots = [flip(cot_wide.array, "batch", 1), flip(wide0.array, "batch", 2)]

    def intra(fq, fk, v):
        return call(intra_kernel, "intra", [masks, fq, fk, v], intra_outs)

    entered0, made = exchange(
        keep, send, flag, core, chip, False, [do_feed, do_intra0]
    )
    feed0, ((scores0, num0, kt0), (cot_next, second_y)) = made
    (
        den0, att0, att_low0, hidden1, first1, second1, fq1, fk1, v1, eq1, ek1, keep, send, wide1,
    ) = call(
        middle_kernel,
        "middle",
        [masks, num0, kt0, fq0, *entered0, Layer(out_weight, 0), out_bias]
        + [hidden0, feed0, *front_of(1, tables)],
        [far, far, far_low, far] + front_outs + [far],
    )
    row, wide_row = Far((1, D)), Far((1, FF))

    def feed_back(layer, second, up_low, up, hidden, more):
        return call(
            functools.partial(feed_back_kernel, layer),
            "feed_back",
            [second, *feed_weights[layer], up_low, up, hidden, Layer(norm_gain, layer)],
            [tall, row, row, wide_row] + more,
        )

    def do_intra1(gate):
        seconds1.append(flip(gate(wide1.array), "batch", 1))
        return intra(gate(fq1), fk1, v1)

    def do_feed_back1(gate):
        made = feed_back(1, gate(second1), cot, cot, hidden1, [far])
        return made, seconds1[0]

    seconds1 = []
    entered1, made = exchange(
        keep, send, flag, core, chip, False, [do_intra1, do_feed_back1]
    )
    scores1, num1, kt1 = made[0]
    ((base1, sgain1, sshift1, gib1, feed1), second_next) = made[1]
    att_low1, gnum1, gden1, keep, send = call(
        turn_kernel,
        "turn",
        [masks, num1, kt1, fq1, *entered1, Layer(out_weight, 1), cot],
        [far_low, fat, tall, packed_state, packed_state],
        [pltpu.VMEM((tokens, D), f32)] * 2,
    )

    def intra_back(fq, fk, v, scores, gnum, gden, entered, eq, place):
        return call(
            intra_back_kernel,
            "intra_back",
            [masks, fq, fk, v, scores, gnum, gden, *entered, eq, tables, dct],
            [fat, place, place],
        )

    def do_intra_back1(gate):
        second_x.append(flip(gate(wide0.array), "batch", 1))
        return intra_back(gate(fq1), fk1, v1, scores1, gnum1, gden1, entered1, eq1, far)

    def do_feed_grad1(gate):
        made = feed_grad([after(gate(gnum1), wide1), second_next], [cot_wide, cot_next], 1, (0, 2))
        return made, second_x[0]

    second_x = []
    (mine, theirs), made = exchange(
        keep, send, flag, core, chip, True, [do_intra_back1, do_feed_grad1]
    )
    (gq1, gfk1, gval1), ((feed_keep1, feed_send1), second_x) = made
    second_xy = flip(tie(second_x, wide0.array)[1], "batch", 3)
    feed_got1 = flip(feed_send1.array, "seq", 1)
    mine, theirs, feed_got1 = tie(mine, theirs, feed_got1)
    sums1 = [Halving(feed_keep1[k] + feed_got1[k]) for k in range(2)]
    vector_outs = [Far((1, 3 * D)), row, row]
    packed = sds((tokens, 3 * D), bf16)
    gp1, gqb1, ggain1, gshift1, up0, up_low0, gnum0, gden0, keep, send = call(
        turn_back_kernel,
        "turn_back",
        [masks, mine, theirs, gfk1, gval1, fk1, v1, ek1, tables, dct, gq1]
        + [Layer(qkv_weight, 1), hidden1, Layer(norm_gain, 1), base1]
        + [Layer(out_weight, 0), den0, att0, fq0],
        [packed, *vector_outs, tall, fat, fat, tall, packed_state, packed_state],
    )
    ups0 = [up0]

    def do_feed_back(gate):
        ups0.extend(flip(gate(up0), "batch", bit) for bit in (1, 2))
        return feed_back(0, second0, gate(up_low0), up0, hidden0, []), second_xy

    def do_intra_back0(gate):
        ups0.append(flip(gate(up0), "batch", 3))
        return (
            intra_back(gate(fq0), fk0, v0, scores0, gnum0, gden0, entered0, eq0, tall),
            packed_grad(gate(first1), att_low1, gp1, cot, (1, 2)),
            ups0[1:3],
        )

    (mine, theirs), made = exchange(
        keep, send, flag, core, chip, True, [do_feed_back, do_intra_back0]
    )
    ((base0, sgain0, sshift0, gib0), second_xy), ((gq0, gfk0, gval0), parts1, ups0[1:3]) = made
    keep1a, send1a, keep1b, send1b = parts1
    got1a, got1b = flip(send1a.array, "seq", 1), flip(send1b.array, "seq", 1)
    mine, theirs, got1a, got1b = tie(mine, theirs, got1a, got1b)
    gp0, gqb0, ggain0, gshift0, ginputs = call(
        last_kernel,
        "last",
        [masks, mine, theirs, gfk0, gval0, fk0, v0, ek0, tables, dct, gq0]
        + [Layer(qkv_weight, 0), hidden0, Layer(norm_gain, 0), base0],
        [packed, *vector_outs, far],
    )
    vectors = (ggain0, sgain0, gshift0, sshift0, gqb0, gib0)
    vectors += (ggain1, sgain1, gshift1, sshift1, gqb1, gib1, cot)
    made = packed_grad(first0, att_low0, gp0, up_low0, (1, 2), vectors)
    made, ups0[3], got = together(made, ups0[3], sums1[0].send())
    sums1[0].add(got)
    keep0a, send0a, keep0b, send0b = made
    got0a, got0b = flip(send0a.array, "seq", 1), flip(send0b.array, "seq", 1)
    first1a = flip(keep1a[2:] + got1a[2:], "batch", 1)
    first1b = flip(keep1b[2:] + got1b[2:], "batch", 2)
    grads0, got0a, got0b, got, first1a, first1b = together(
        feed_grad([wide0, second_x, second_y, second_xy], ups0, 0, (0,)),
        got0a, got0b, sums1[1].send(), first1a, first1b,
    )
    feed_keep0, feed_send0 = grads0
    sums1[1].add(got)
    feed_got0 = flip(feed_send0.array, "seq", 1)
    first0a = flip(keep0a[2:] + got0a[2:], "batch", 1)
    first0b = flip(keep0b[2:] + got0b[2:], "batch", 2)
    (result,) = call(
        result_kernel,
        "result",
        [hidden1, feed1, att_low1, Layer(out_weight, 1), out_bias],
        [far_low],
    )
    feed_got0, first0a, first0b, result, got = together(
        feed_got0, first0a, first0b, result, sums1[0].send()
    )
    sums1[0].add(got)
    feed0 = Halving(feed_keep0[0] + feed_got0[0])
    got_feed0 = feed0.send()

    def second(part0, part1, at, bit):
        parts = [sum(x[at] for x in part).reshape(size // 2, -1, D // 2) for part in (part0, part1)]
        both = jnp.concatenate(parts, axis=1).reshape(-1, D // 2)
        return both if bit is None else flip(both, "batch", bit)

    a0, a1 = (keep0a, got0a, first0a), (keep1a, got1a, first1a)
    b0, b1 = (keep0b, got0b, first0b), (keep1b, got1b, first1b)
    second_a, second_b = second(a0, a1, 1, 2), second(b0, b1, 1, 1)
    got_feed0, second_a, second_b, got = tie(got_feed0, second_a, second_b, sums1[1].send())
    sums1[1].add(got)
    sums1 = [part.finish() for part in sums1]

    feed0.add(got_feed0)
    feed0 = feed0.finish()
    packed = Halving(
        jnp.concatenate(
            [second(a0, a1, 0, None) + second_a, second(b0, b1, 0, None) + second_b], axis=1
        )
    )
    other1 = flip(jnp.concatenate([sums1[1], sums1[0]], axis=0), "batch", 2)
    other0, got, other1 = tie(flip(feed0, "batch", 1), packed.send(), other1)
    packed.add(got)
    mine1 = jnp.concatenate(sums1, axis=0) + other1
    other1 = flip(mine1, "batch", 1)
    other0_y = flip(jnp.concatenate([feed0, other0], axis=0), "batch", 2)
    got, other1, other0_y = tie(packed.send(), other1, other0_y)
    packed.add(got)
    pieces = [feed0, other0, other0_y, mine1, other1] + spread(packed.finish())
    slot = D // size
    outs = [
        Far((2, slot, FF)),
        Far((2, FF // size, D)),
        Far((2, slot, 3 * D)),
        Far((2, slot, D)),
        Far((2, 2, slot)),
        Far((2, 2, slot)),
        Far((3, 2, slot)),
        Far((2, slot)),
        Far((2, slot)),
        Far((2, FF // size)),
    ]
    if quarter_wide == HEAD:
        joined = [x.array for x in call(join_kernel, "join", pieces, outs)]
    else:
        joined = join(pieces, size)
    grad_in, grad_down, grad_qkv, grad_out, gain, shift, grad_qkv_b, out_b, down_b, in_b = joined
    return (
        result.array.reshape(rows, length, D),
        ginputs.array.reshape(rows, length, D),
        gain,
        shift,
        grad_qkv,
        grad_qkv_b.swapaxes(0, 1),
        grad_out,
        out_b,
        grad_in,
        in_b,
        grad_down,
        down_b,
    )


def solution(mesh):
    placed = (
        P("batch", "seq", None),
        P("batch", None),
        P("batch", "seq", None),
        P(),
        P(),
        P(),
        P(),
        P(),
        P(),
        P(),
        P(),
        P(),
        P(),
    )
    return jax.shard_map(
        per_device,
        mesh=mesh,
        in_specs=placed,
        out_specs=(
            P("batch", "seq", None),
            P("batch", "seq", None),
            P(None, None, "seq"),
            P(None, None, "seq"),
            P(None, "seq", None),
            P(None, None, "seq"),
            P(None, "seq", None),
            P(None, "seq"),
            P(None, "seq", None),
            P(None, "seq"),
            P(None, "seq", None),
            P(None, "seq"),
        ),
        check_vma=False,
    )
```

```python
import functools
import math

import jax
import jax.numpy as jnp
import numpy as np
from jax import lax
from jax.experimental import pallas as pl
from jax.experimental.pallas import tpu as pltpu
from jax.sharding import PartitionSpec as P

D = 512
HEADS = 8
HEAD = 64
FF = 2048
ROT = 16
LAYERS = 2
NDOC = 4
LEN = 128
PAIRS = HEADS // 2
PACK = 2 * HEAD + 8
WIDE = 512

epsilon = 1e-05
f32, bf16 = jnp.float32, jnp.bfloat16
NN = (((1,), (0,)), ((), ()))
NT = (((1,), (1,)), ((), ()))
TN = (((0,), (0,)), ((), ()))


def dot(a, b, dims=NN):
    return lax.dot_general(a, b, dims, preferred_element_type=f32)


def split(x):
    high = x.astype(bf16)
    return high, (x - high.astype(f32)).astype(bf16)


def sds(shape, dtype=f32):
    return jax.ShapeDtypeStruct(shape, dtype)


def norm_parts(hidden):
    centred = hidden - jnp.mean(hidden, axis=-1, keepdims=True)
    variance = jnp.mean(centred * centred, axis=-1, keepdims=True)
    inverse = lax.rsqrt(variance + epsilon)
    return centred * inverse, inverse


def segment_of(position, starts, row):
    found = jnp.zeros_like(position)
    for k in range(NDOC):
        entry = starts[row, k]
        found = jnp.maximum(found, jnp.where(entry <= position, entry, 0))
    return found


def prepare(starts, masks, tables):
    begin = lax.axis_index("seq") * LEN
    for row in range(masks.shape[1]):
        at_i = begin + lax.broadcasted_iota(jnp.int32, (LEN, 128), 0)
        at_j = begin + lax.broadcasted_iota(jnp.int32, (LEN, 128), 1)
        seg_i, seg_j = segment_of(at_i, starts, row), segment_of(at_j, starts, row)
        last = jnp.int32(0)
        for k in range(NDOC):
            entry = starts[row, k]
            last = jnp.maximum(last, jnp.where(entry <= begin + (LEN - 1), entry, 0))
        masks[0, row] = jnp.where((at_j <= at_i) & (seg_i == seg_j), 1.0, 0.0).astype(f32)
        masks[1, row] = jnp.where(seg_i < begin, 1.0, 0.0).astype(f32)
        masks[2, row] = jnp.where(seg_i == last, 1.0, 0.0).astype(f32)
        lane = lax.broadcasted_iota(jnp.int32, (LEN, 128), 1) % HEAD
        inverse = jnp.exp((lane % (ROT // 2)).astype(f32) * (-2.0 / ROT * math.log(10000.0)))
        angles = (at_i - seg_i).astype(f32) * jnp.where(lane < ROT, inverse, 0.0)
        at = slice(row * LEN, (row + 1) * LEN)
        tables[0, at] = jnp.cos(angles)
        tables[1, at] = jnp.sin(angles)


def masks_of(row, masks):
    return masks[0, row], masks[1, row], masks[2, row]


def low_lanes(rows):
    return lax.broadcasted_iota(jnp.int32, (rows, 128), 1) < HEAD


def read_tables(tables):
    sine = tables[1]
    lane = lax.broadcasted_iota(jnp.int32, sine.shape, 1) % HEAD
    ahead = jnp.where(lane < ROT // 2, -sine, 0.0)
    behind = jnp.where((lane >= ROT // 2) & (lane < ROT), sine, 0.0)
    return tables[0], ahead, behind


def rotate(x, tables):
    base, ahead, behind = tables
    return x * base + pltpu.roll(x, 120, 1) * ahead + pltpu.roll(x, 8, 1) * behind


def rotate_back(g, tables):
    base, ahead, behind = tables
    return g * base + pltpu.roll(g * ahead, 8, 1) + pltpu.roll(g * behind, 120, 1)


def featurize(x, tables, high, low):
    pieces = [rotate(x[:, g * 128 : (g + 1) * 128], tables) for g in range(4)]
    found = []
    for g in range(2):
        a, b = split(jnp.concatenate(pieces[2 * g : 2 * g + 2], axis=1))
        found.append(jnp.exp(dot(a, high) + dot(b, high) + dot(a, low)))
    return jnp.concatenate(found, axis=1)


def unfeaturize(g, tables, high, low):
    found = []
    for k in range(2):
        a, b = split(g[:, k * 256 : (k + 1) * 256])
        back = dot(a, high, NT) + dot(b, high, NT) + dot(a, low, NT)
        found += [rotate_back(back[:, :128], tables), rotate_back(back[:, 128:], tables)]
    return jnp.concatenate(found, axis=1)


def head_ones():
    across = lax.broadcasted_iota(jnp.int32, (256, 256), 0) // HEAD
    along = lax.broadcasted_iota(jnp.int32, (256, 256), 1) // HEAD
    return jnp.where(across == along, 1.0, 0.0).astype(bf16)


def head_sum(x, ones):
    found = []
    for g in range(2):
        a, b = split(x[:, g * 256 : (g + 1) * 256])
        found.append(dot(a, ones) + dot(b, ones))
    return jnp.concatenate(found, axis=1)


def store_halves(keep_ref, send_ref, halves):
    def put(ref, half):
        for row, at, value in halves[half]:
            ref[row, at[0] : at[1], :] = value

    core = lax.axis_index("seq") % 2
    for mine in range(2):

        @pl.when(core == mine)
        def _():
            put(keep_ref, mine)
            put(send_ref, 1 - mine)


def pack_states(rows, left_of, right, norm_of):
    low = low_lanes(HEAD)
    halves = [[], []]
    for row in range(rows):
        at = slice(row * LEN, (row + 1) * LEN)
        left, norm = left_of(row), norm_of(row)
        for pair in range(PAIRS):
            lanes = slice(pair * 128, (pair + 1) * 128)
            both = dot(left[:, lanes], right[at, lanes], TN)
            half, place = pair // 2, pair % 2
            halves[half].append(
                (row, (place * HEAD, (place + 1) * HEAD), jnp.where(low, both[:HEAD], both[HEAD:]))
            )
        for half in range(2):
            pieces = [norm[:, (2 * half + k) * 128 : (2 * half + k + 1) * 128] for k in range(2)]
            block = jnp.concatenate(pieces + [jnp.zeros((6, 128), f32)], axis=0)
            halves[half].append((row, (2 * HEAD, PACK), block))
    return halves


def unpack_state(mine_ref, theirs_ref, row):
    low = low_lanes(HEAD)
    blocks, norms = [], []
    for half in range(2):
        here = lax.axis_index("seq") % 2 == half
        packed = jnp.where(here, mine_ref[row], theirs_ref[row])
        for place in range(2):
            state = packed[place * HEAD : (place + 1) * HEAD]
            both = jnp.concatenate(
                [jnp.where(low, state, 0.0), jnp.where(low, 0.0, state)], axis=0
            )
            blocks.append(split(both))
            norms.append(packed[2 * HEAD + place : 2 * HEAD + place + 1])
    return blocks, jnp.concatenate(norms, axis=1)


def cross_dot(x, block, dims=NN):
    return dot(x, block[0], dims) + dot(x, block[1], dims)


def gelu_parts(lifted):
    phi = 0.5 + 0.5 * lax.erf(lifted * math.sqrt(0.5))
    slope = phi + lifted * (jnp.exp(-0.5 * lifted * lifted) * (1.0 / math.sqrt(2.0 * math.pi)))
    return lifted * phi, slope


def norm_back(grad, xhat, inverse, gain):
    u = grad * gain
    mean_u = jnp.mean(u, axis=-1, keepdims=True)
    mean_ux = jnp.mean(u * xhat, axis=-1, keepdims=True)
    down = (u - mean_u - xhat * mean_ux) * inverse
    return down, jnp.sum(grad * xhat, axis=0, keepdims=True), jnp.sum(grad, axis=0, keepdims=True)


def front_body(layer, masks, hidden, gain, shift, b, tables, dct, wk, wv, outs):
    first_ref, again_ref, second_ref, fk_ref, v_ref, ek_ref, keep_ref, send_ref, wide_ref = outs
    xhat, _ = norm_parts(hidden)
    gains, shifts = gain[...].astype(f32), shift[...].astype(f32)
    first = (xhat * gains[0:1] + shifts[0:1]).astype(bf16)
    first_ref[...] = first
    again_ref[...] = first
    second = (xhat * gains[1:2] + shifts[1:2]).astype(bf16)
    second_ref[...] = second
    wide_ref[...] = second.astype(f32)
    bias = [b[k][layer : layer + 1].astype(f32) for k in range(3)]
    tabs = read_tables(tables)
    high, low = dct[0], dct[1]
    keys = dot(first, wk[...]) + bias[1]
    values = (dot(first, wv[...]) + bias[2]).astype(bf16)
    v_ref[...] = values
    exp_k = featurize(keys, tabs, high, low)
    ek_ref[...] = exp_k
    feat_k = exp_k.astype(bf16)
    fk_ref[...] = feat_k
    rows = hidden.shape[0] // LEN
    wide = feat_k.astype(f32)

    def tailed(row):
        tail = masks_of(row, masks)[2]
        return wide[row * LEN : (row + 1) * LEN] * jnp.concatenate([tail] * 4, axis=1)

    kept = [tailed(row) for row in range(rows)]
    halves = pack_states(
        rows,
        lambda row: kept[row].astype(bf16),
        values,
        lambda row: jnp.sum(kept[row], axis=0, keepdims=True),
    )
    store_halves(keep_ref, send_ref, halves)


def front_kernel(starts, cot, h, gain, shift, b, dct, wk, wv, *outs):
    *outs, masks, tables = outs
    outs[9][...] = cot[...].astype(f32)
    prepare(starts, masks, tables)
    hidden = h[...].astype(f32)
    front_body(0, masks, hidden, gain, shift, b, tables, dct, wk, wv, outs[:9])


def attend(masks, num_ref, kt_ref, fq_ref, mine_ref, theirs_ref, den_ref, att_ref, low_ref):
    rows = num_ref.shape[0] // LEN
    ones = head_ones()
    for row in range(rows):
        at = slice(row * LEN, (row + 1) * LEN)
        cross = masks_of(row, masks)[1]
        cross4 = jnp.concatenate([cross] * 4, axis=1)
        blocks, norm = unpack_state(mine_ref, theirs_ref, row)
        fq = fq_ref[at]
        far = jnp.concatenate(
            [cross_dot(fq[:, p * 128 : (p + 1) * 128], blocks[p]) for p in range(PAIRS)], axis=1
        )
        num = num_ref[at] + cross4 * far
        den = head_sum(fq.astype(f32) * (kt_ref[at] + cross4 * norm), ones)
        att = num / den
        den_ref[at] = den
        att_ref[at] = att
        low_ref[at] = att.astype(bf16)
    begin_writing(den_ref, att_ref, low_ref)


def middle_kernel(
    masks, num, kt, fq0, mine, theirs, ow, ob, h, feed, gain, shift, b, tables, dct, wk, wv,
    den, att, att_low, h2, *outs,
):
    attend(masks, num, kt, fq0, mine, theirs, den, att, att_low)
    hidden = h[...].astype(f32) + (dot(att_low[...], ow[...]) + ob[0:1].astype(f32)) + feed[...]
    h2[...] = hidden
    front_body(1, masks, hidden, gain, shift, b, tables, dct, wk, wv, outs)


def attend_back(masks, up, ow, den, att, fq, gnum, gden, keep_ref, send_ref):
    ga = dot(up, ow[...], NT)
    den_v = den[...]
    gn = (ga / den_v).astype(bf16)
    gnum[...] = gn
    gd = -head_sum(ga * att[...], head_ones()) / den_v
    gden[...] = gd
    rows = up.shape[0] // LEN
    wide = fq[...].astype(f32)

    def crossed(row):
        cross = masks_of(row, masks)[1]
        return wide[row * LEN : (row + 1) * LEN] * jnp.concatenate([cross] * 4, axis=1)

    kept = [crossed(row) for row in range(rows)]
    halves = pack_states(
        rows,
        lambda row: kept[row].astype(bf16),
        gn,
        lambda row: jnp.sum(kept[row] * gd[row * LEN : (row + 1) * LEN], axis=0, keepdims=True),
    )
    store_halves(keep_ref, send_ref, halves)


def turn_kernel(
    masks, num, kt, fq, mine, theirs, ow, cot, att_low, gnum, gden, keep, send, den, att,
):
    attend(masks, num, kt, fq, mine, theirs, den, att, att_low)
    attend_back(masks, cot[...], ow, den, att, fq, gnum, gden, keep, send)


CHUNKS = FF // WIDE


def feed_kernel(second, ib, db, *refs):
    chunks, feed = refs[:-1], refs[-1]
    total = jnp.broadcast_to(db[0:1].astype(f32), feed.shape)
    for g in range(CHUNKS):
        iw, dw = chunks[2 * g : 2 * g + 2]
        bias = ib[0:1, g * WIDE : (g + 1) * WIDE].astype(f32)
        lifted = dot(second[...], iw[...]) + bias
        total = total + dot(gelu_parts(lifted)[0].astype(bf16), dw[...])
    feed[...] = total


def feed_back_kernel(layer, second, ib, db, up_low, *refs):
    chunks, (up, h, gain, base, gain_out, shift_out, gib, *feed) = (
        refs[: 2 * CHUNKS],
        refs[2 * CHUNKS :],
    )
    total = jnp.broadcast_to(db[layer : layer + 1].astype(f32), base.shape)
    back = jnp.zeros(base.shape, f32)
    low_up = up_low[...]
    for g in range(CHUNKS):
        lanes = slice(g * WIDE, (g + 1) * WIDE)
        iw, dw = (part[...] for part in chunks[2 * g : 2 * g + 2])
        lifted = dot(second[...], iw) + ib[layer : layer + 1, lanes].astype(f32)
        value, slope = gelu_parts(lifted)
        if feed:
            total = total + dot(value.astype(bf16), dw)
        low = (dot(low_up, dw, NT) * slope).astype(bf16)
        gib[:, lanes] = jnp.sum(low.astype(f32), axis=0, keepdims=True)
        back = back + dot(low, iw, NT)
    if feed:
        feed[0][...] = total
    xhat, inverse = norm_parts(h[...].astype(f32))
    gains = gain[...].astype(f32)
    part, gain_out[...], shift_out[...] = norm_back(back, xhat, inverse, gains[1:2])
    base[...] = up[...].astype(f32) + part


def intra_kernel(layer, masks, first, wq, b, tables, dct, fk, v, fq, eq, scores, num, kt):
    queries = dot(first[...], wq[...]) + b[0][layer : layer + 1].astype(f32)
    exp_q = featurize(queries, read_tables(tables), dct[0], dct[1])
    eq[...] = exp_q
    fq[...] = exp_q.astype(bf16)
    low = low_lanes(LEN)
    even = jnp.where(low, 1.0, 0.0).astype(bf16)
    odd = jnp.where(low, 0.0, 1.0).astype(bf16)
    for row in range(fq.shape[0] // LEN):
        at = slice(row * LEN, (row + 1) * LEN)
        intra = masks_of(row, masks)[0]
        kt[at] = dot(intra.astype(bf16), fk[at])
        twice = jnp.concatenate([intra, intra], axis=0)
        for pair in range(PAIRS):
            lanes = slice(pair * 128, (pair + 1) * 128)
            q = fq[at, lanes]
            both = jnp.concatenate([q * even, q * odd], axis=0)
            rounded = (dot(both, fk[at, lanes], NT) * twice).astype(bf16)
            scores[row, pair] = rounded
            out = dot(rounded, v[at, lanes])
            num[at, lanes] = jnp.where(low, out[:LEN], out[LEN:])


def intra_back_kernel(
    masks, fq, fk, v, scores, gnum, gden, mine, theirs, eq, tables, dct, gq, gfk, gval
):
    low = low_lanes(LEN)
    even = jnp.where(low, 1.0, 0.0).astype(bf16)
    odd = jnp.where(low, 0.0, 1.0).astype(bf16)
    grad = []
    for row in range(fq.shape[0] // LEN):
        at = slice(row * LEN, (row + 1) * LEN)
        intra, cross, _ = masks_of(row, masks)
        twice = jnp.concatenate([intra, intra], axis=0)
        blocks, norm = unpack_state(mine, theirs, row)
        queries = []
        for pair in range(PAIRS):
            lanes = slice(pair * 128, (pair + 1) * 128)
            gn, gd, q, k = gnum[at, lanes], gden[at, lanes], fq[at, lanes], fk[at, lanes]
            both = jnp.concatenate([gn * even, gn * odd], axis=0)
            turned = pltpu.roll(gd, HEAD, 1)
            dens = jnp.concatenate(
                [jnp.where(low, gd, turned), jnp.where(low, turned, gd)], axis=0
            )
            gs = ((dot(both, v[at, lanes], NT) + dens) * twice).astype(bf16)
            near = dot(gs, k)
            far = cross_dot(gn, blocks[pair], NT) + gd * norm[:, lanes]
            queries.append(jnp.where(low, near[:LEN], near[LEN:]) + cross * far)
            gfk[at, lanes] = jnp.where(low, dot(gs[:LEN], q, TN), dot(gs[LEN:], q, TN))
            sl = scores[row, pair]
            gval[at, lanes] = jnp.where(low, dot(sl[:LEN], gn, TN), dot(sl[LEN:], gn, TN))
        grad.append(jnp.concatenate(queries, axis=1))
    begin_writing(gfk, gval)
    turned = unfeaturize(
        jnp.concatenate(grad, axis=0) * eq[...], read_tables(tables), dct[0], dct[1]
    )
    gq[...] = turned.astype(bf16)


def packed_back(masks, mine, theirs, gq, gfk, gval, fk, v, ek, tables, dct, gp, gqb):
    keys, values = [], []
    for row in range(fk.shape[0] // LEN):
        at = slice(row * LEN, (row + 1) * LEN)
        tail = masks_of(row, masks)[2]
        blocks, norm = unpack_state(mine, theirs, row)
        key_row, value_row = [], []
        for pair in range(PAIRS):
            lanes = slice(pair * 128, (pair + 1) * 128)
            far = cross_dot(v[at, lanes], blocks[pair], NT) + norm[:, lanes]
            key_row.append(gfk[at, lanes] + tail * far)
            value_row.append(gval[at, lanes] + tail * cross_dot(fk[at, lanes], blocks[pair]))
        keys.append(jnp.concatenate(key_row, axis=1))
        values.append(jnp.concatenate(value_row, axis=1))
    gp[:, 2 * D :] = jnp.concatenate(values, axis=0).astype(bf16)
    gp[:, :D] = gq[...]
    keys = unfeaturize(
        jnp.concatenate(keys, axis=0) * ek[...], read_tables(tables), dct[0], dct[1]
    )
    gp[:, D : 2 * D] = keys.astype(bf16)
    gqb[...] = jnp.sum(gp[...].astype(f32), axis=0, keepdims=True)


def upstream_back(base, hidden, gp, weights, gain, gain_out, shift_out):
    gfirst = sum(
        dot(gp[:, k * D : (k + 1) * D], part[...], NT) for k, part in zip((0, 2, 1), weights)
    )
    xhat, inverse = norm_parts(hidden)
    part, gain_out[...], shift_out[...] = norm_back(
        gfirst, xhat, inverse, gain[...].astype(f32)[0:1]
    )
    return base[...] + part


def turn_back_kernel(
    masks, mine, theirs, gfk, gval, fk, v, ek, tables, dct, gq, wq, wv, wk, h, gain, base, ow, den, att, fq,
    gp, gqb, ggain, gshift, up_ref, up_low, gnum, gden, keep, send,
):
    packed_back(masks, mine, theirs, gq, gfk, gval, fk, v, ek, tables, dct, gp, gqb)
    up = upstream_back(base, h[...], gp, (wq, wv, wk), gain, ggain, gshift)
    up_ref[...] = up
    low = up.astype(bf16)
    up_low[...] = low
    attend_back(masks, low, ow, den, att, fq, gnum, gden, keep, send)


def result_kernel(h, feed, att_low, ow, ob, result):
    hidden = h[...] + (dot(att_low[...], ow[...]) + ob[1:2].astype(f32)) + feed[...]
    result[...] = hidden.astype(bf16)


def last_kernel(
    masks, mine, theirs, gfk, gval, fk, v, ek, tables, dct, gq, wq, wv, wk, h, gain, base,
    gp, gqb, ggain, gshift, ginputs,
):
    packed_back(masks, mine, theirs, gq, gfk, gval, fk, v, ek, tables, dct, gp, gqb)
    weights = (wq, wv, wk)
    ginputs[...] = upstream_back(base, h[...].astype(f32), gp, weights, gain, ggain, gshift)


def gathered(size, x, flat, held):
    block = flat.shape[0] // size
    flat[...] = x.astype(f32).T
    for place in range(size):
        source = block_at(size, place)
        held[place * block : (place + 1) * block, :] = flat[
            pl.ds(pl.multiple_of(source * block, block), block), :
        ]
    return held[...].astype(bf16)


def reversed_bits(value, count):
    return sum(((value >> k) & 1) << (count - 1 - k) for k in range(count))


def block_at(size, place):
    return reversed_bits(place, size.bit_length() - 1) ^ lax.axis_index("seq")


def pick_quarter(size, layer, q, ib, chunks, iw_q, ib_q, dw_q):
    wide = FF // size
    rows = lax.broadcasted_iota(jnp.int32, (128, 128), 0) - HEAD * (q % 2)
    lanes = lax.broadcasted_iota(jnp.int32, (128, 128), 1)
    left = jnp.where((rows == lanes) & (lanes < HEAD), 1.0, 0.0).astype(bf16)
    right = jnp.where((rows == lanes - HEAD) & (lanes >= HEAD), 1.0, 0.0).astype(bf16)
    quarter = wide // 4
    for pair in range(size // 2):
        iw, dw = chunks[2 * pair : 2 * pair + 2]
        here = slice(pair * 128, (pair + 1) * 128)
        at = [k * wide + (q // 2) * 128 for k in range(2)]
        cut = [pl.ds(pl.multiple_of(begin, 128), 128) for begin in at]
        iw_q[:, here] = (dot(iw[:, cut[0]], left) + dot(iw[:, cut[1]], right)).astype(bf16)
        cut = [pl.ds(pl.multiple_of(pair * 2 * wide + begin, 128), 128) for begin in at]
        bias = [ib[:, part] for part in cut]
        ib_q[:, here] = (dot(bias[0], left) + dot(bias[1], right))[layer : layer + 1]
        for k in range(2):
            s = 2 * pair + k
            picked = pl.ds(pl.multiple_of(k * wide + q * quarter, quarter), quarter)
            dw_q[s * quarter : (s + 1) * quarter, :] = dw[picked, :]


def feed_grad_kernel(size, layer, groups, quarters, *refs):
    count = len(quarters)
    own = FF // size // 4 == HEAD
    weights, refs = refs[: 1 + 2 * CHUNKS if own else 3 * count], refs[1 + 2 * CHUNKS if own else 3 * count :]
    seconds, ups, refs = refs[:groups], refs[groups : 2 * groups], refs[2 * groups :]
    keep, send, s_all, u_all, act, lift, out, *picked = refs
    tokens = s_all.shape[0] // groups
    block = D // size
    for n, quarter in enumerate(quarters):
        if own:
            q = lax.axis_index("batch") ^ quarter
            pick_quarter(size, layer, q, weights[0], weights[1:], *picked)
            iw, ib, dw = picked
        else:
            iw, ib, dw = weights[3 * n : 3 * n + 3]
        for k in range(groups):
            at = slice(k * tokens, (k + 1) * tokens)
            if n == 0:
                s_all[at], u_all[at] = seconds[k][...].astype(bf16), ups[k][...].astype(bf16)
            lifted = dot(s_all[at], iw[...]) + ib[...].astype(f32)
            value, slope = gelu_parts(lifted)
            act[at] = value.astype(bf16)
            lift[at] = (dot(u_all[at], dw[...], NT) * slope).astype(bf16)
        for part, grads in enumerate(
            (dot(s_all[...], lift[...], TN), dot(act[...], u_all[...], TN))
        ):
            for s in range(size):
                place = reversed_bits(s ^ lax.axis_index("seq"), size.bit_length() - 1)
                at = pl.multiple_of((2 * place + part) * block, block)
                out[pl.ds(at, block), :] = grads[s * block : (s + 1) * block]
        keep[n], send[n] = out[:D], out[D:]


def chosen(refs, index):
    value = refs[0][...]
    for k in range(1, len(refs)):
        value = jnp.where(index == k, refs[k][...], value)
    return value


def join_kernel(*refs):
    feed0, x0, y0, feed1, x1, *pieces = refs[:9]
    outs = refs[9:]
    me = lax.axis_index("batch")
    in_out, down_out, qkv_out, out_out, gain_out, shift_out, qkvb_out = outs[:7]
    outb_out, downb_out, inb_out = outs[7:]
    block = in_out.shape[1]
    low = low_lanes(block)
    for layer in range(2):
        two = 2 * block
        if layer == 0:
            held = (feed0, x0, y0.at[:two], y0.at[two:])
        else:
            held = (feed1.at[:two], x1.at[:two], feed1.at[two:], x1.at[two:])
        begin = layer * (block + 8)
        for q in range(4):
            packed = chosen(pieces, q ^ me)[begin : begin + block + 8 * (1 - layer)]
            qkv_out[layer, :, q * 384 : (q + 1) * 384] = packed[:block, :384]
            out_out[layer, :, q * 128 : (q + 1) * 128] = packed[:block, 384:]
            if layer == 0 and q < 2:
                lines = packed[block:]
                gain_out[q] = lines[0:2, :block]
                shift_out[q] = lines[2:4, :block]
                for k in range(3):
                    qkvb_out[k, q : q + 1, :] = lines[4 + k : 5 + k, :block]
                outb_out[q : q + 1, :] = lines[7:8, :block]
                downb_out[q : q + 1, :] = lines[7:8, :block]
                inb_out[q : q + 1, :] = lines[0:1, 256 : 256 + inb_out.shape[1]]
        for pair in range(2):
            left, right = (chosen(held, (2 * pair + k) ^ me) for k in range(2))
            down_out[layer, 2 * pair * block : (2 * pair + 1) * block, :] = left[block:]
            down_out[layer, (2 * pair + 1) * block : (2 * pair + 2) * block, :] = right[block:]
            for tile in range(D // 128):
                lanes = slice(tile * 128, (tile + 1) * 128)
                a, b = left[:block, lanes], right[:block, lanes]
                at = 2 * tile * 256 + pair * 128
                in_out[layer, :, at : at + 128] = jnp.where(low, a, pltpu.roll(b, 64, 1))
                in_out[layer, :, at + 256 : at + 384] = jnp.where(low, pltpu.roll(a, 64, 1), b)


PARTS = ((0, 256), (256, 512))


def standing(quarter, bit):
    return jnp.where(bit == 1, (quarter % 2) * 2 + quarter // 2, quarter)


def packed_grad_kernel(size, bits, more, *refs):
    first, att_low, gp, up, *refs = refs[more:]
    *vectors, keep_a, send_a, keep_b, send_b, f1, h1 = refs
    block, under = D // size, 8 if vectors else 0
    half, me = size // 2, lax.axis_index("batch")
    for source, right, wide, begin in ((first, gp, 384, 0), (att_low, up, 128, 384)):
        left = gathered(size, source[...], f1, h1)
        for q in range(4):
            out = dot(left, right[:, q * wide : (q + 1) * wide])
            for (low, high), bit, refs in zip(PARTS, bits, ((keep_a, send_a), (keep_b, send_b))):
                lanes = max(low, begin), min(high, begin + wide)
                if lanes[0] >= lanes[1]:
                    continue
                at = standing(q ^ me, bit)
                for place in range(size):
                    here = (place % half) * (block + under)
                    refs[place // half][
                        at, here : here + block, lanes[0] - low : lanes[1] - low
                    ] = out[
                        place * block : (place + 1) * block, lanes[0] - begin : lanes[1] - begin
                    ]
    if vectors:
        put_lines(size, bits, vectors, up, ((keep_a, send_a), (keep_b, send_b)))


def put_lines(size, bits, vectors, up, parts):
    block, wide, me = D // size, FF // size, lax.axis_index("batch")
    held = []
    for *norms, gqb, gib, ups in ((*vectors[:6], up), vectors[6:]):
        gob = jnp.sum(ups[...].astype(f32), axis=0, keepdims=True)
        rows = [part[...] for part in norms]
        rows += [gqb[:, k * D : (k + 1) * D] for k in range(3)] + [gob]
        held.append((jnp.concatenate(rows, axis=0), jnp.broadcast_to(gib[...], (8, FF))))
    for place in range(size):
        source = block_at(size, place)
        here = (place % (size // 2)) * (block + 8) + block
        a_ref, b_ref = (refs[place // (size // 2)] for refs in parts)
        for layer, (rows, line) in enumerate(held):
            a_ref[standing(layer ^ me, bits[0]), here : here + 8, :128] = pltpu.roll(
                rows, (D - source * block) % D, 1
            )[:, :128]
            b_ref[standing(layer ^ me, bits[1]), here : here + 8, :] = pltpu.roll(
                line, (FF - source * wide) % FF, 1
            )[:, :256]
            a_ref[standing(layer ^ me, bits[0]), here : here + 8, 128:] = jnp.zeros((8, 128), f32)
        for k in (2, 3):
            for ref, bit in ((a_ref, bits[0]), (b_ref, bits[1])):
                ref[standing(k ^ me, bit), here : here + 8, :] = jnp.zeros((8, 256), f32)


class Layer:
    def __init__(self, array, index=None):
        self.array, self.index = array, index
        self.shape = array.shape if index is None else jax.eval_shape(lambda x: x[index], array).shape


class Far:
    def __init__(self, shape, dtype=f32):
        self.shape, self.dtype = shape, dtype


class Parked:
    def __init__(self, array):
        self.array = array


class Scalars:
    def __init__(self, array):
        self.array = array


class Source:
    def __init__(self, here, there, semaphore):
        self.here, self.copy = here, pltpu.make_async_copy(there, here, semaphore)
        self.shape, self.copying = here.shape, True
        self.copy.start()

    def __getitem__(self, at):
        if self.copying:
            self.copy.wait()
            self.copying = False
        return self.here[at]


class Target:
    def __init__(self, here, there, semaphore):
        self.here, self.copy = here, pltpu.make_async_copy(here, there, semaphore)
        self.shape, self.started = here.shape, False

    def __getitem__(self, at):
        return self.here[at]

    def __setitem__(self, at, value):
        assert not self.started
        self.here[at] = value
        if at is Ellipsis:
            self.start()

    def start(self):
        if not self.started:
            self.copy.start()
            self.started = True


def begin_writing(*results):
    for result in results:
        if isinstance(result, Target):
            result.start()


def call(kernel, name, operands, outs, scratch=()):
    arrays = [getattr(operand, "array", operand) for operand in operands]
    copied = [k for k, operand in enumerate(operands) if isinstance(operand, Layer)]
    written = [k for k, out in enumerate(outs) if isinstance(out, Far)]
    parked = [k for k, operand in enumerate(operands) if isinstance(operand, Parked)]
    arrays = [
        a
        if isinstance(o, Scalars)
        else pltpu.with_memory_space_constraint(a, pltpu.HBM if isinstance(o, Layer) else pltpu.VMEM)
        for o, a in zip(operands, arrays)
    ]
    vmem, smem = pl.BlockSpec(memory_space=pltpu.VMEM), pl.BlockSpec(memory_space=pltpu.SMEM)
    hbm = pl.BlockSpec(memory_space=pltpu.HBM)
    own = 1 + len(copied) + len(written)
    shown = len(outs)
    outs = list(outs) + [Far(arrays[k].shape, arrays[k].dtype) for k in parked]

    def body(*refs):
        ins, results = list(refs[: len(operands)]), list(refs[len(operands) :][: len(outs)])
        semaphores, *buffers = refs[len(operands) + len(outs) :]
        results, places = results[:shown], results[shown:]
        copies = [
            pltpu.make_async_copy(ins[k], place, semaphores.at[own - 1 + n])
            for n, (k, place) in enumerate(zip(parked, places))
        ]
        for copy in copies:
            copy.start()
        for n, k in enumerate(copied):
            index = operands[k].index
            there = ins[k] if index is None else ins[k].at[index]
            ins[k] = Source(buffers[n], there, semaphores.at[n])
        for n, k in enumerate(written):
            n += len(copied)
            results[k] = Target(buffers[n], results[k], semaphores.at[n])
        kernel(*ins, *results, *buffers[own - 1 :])
        assert not any(ins[k].copying for k in copied), name
        for k in written:
            results[k].start()
        for k in written:
            results[k].copy.wait()
        for copy in copies:
            copy.wait()

    found = pl.pallas_call(
        body,
        name=name,
        in_specs=[
            smem if isinstance(o, Scalars) else hbm if isinstance(o, Layer) else vmem
            for o in operands
        ],
        out_specs=[hbm if isinstance(o, Far) else vmem for o in outs],
        out_shape=[(pltpu.HBM if isinstance(o, Far) else pltpu.VMEM)(o.shape, o.dtype) for o in outs],
        scratch_shapes=[
            pltpu.SemaphoreType.DMA((max(own - 1 + len(parked), 1),)),
            *[pltpu.VMEM(operands[k].shape, arrays[k].dtype) for k in copied],
            *[pltpu.VMEM(outs[k].shape, outs[k].dtype) for k in written],
            *scratch,
        ],
        cost_estimate=pl.CostEstimate(flops=1024, bytes_accessed=1024, transcendentals=0),
        compiler_params=pltpu.CompilerParams(vmem_limit_bytes=26 * 1024 * 1024),
    )(*arrays)
    return [Layer(x) if isinstance(o, Far) else x for x, o in zip(found, outs)]


def cosine_table():
    frequency = np.arange(HEAD, dtype=np.float64)[:, None]
    columns = np.arange(HEAD, dtype=np.float64)[None, :]
    entries = np.cos(math.pi * (2.0 * columns + 1.0) * frequency / (2.0 * HEAD))
    entries = entries * math.sqrt(2.0 / HEAD)
    entries[0] *= math.sqrt(0.5)
    wide = np.kron(np.eye(4), entries.T)
    high = wide.astype(np.float32).astype(bf16)
    low = (wide.astype(np.float32) - high.astype(np.float32)).astype(bf16)
    return jnp.asarray(np.stack([high, low]))


def rotary_tables(places):
    lane = jnp.arange(128) % HEAD
    half = ROT // 2
    inverse = 10000.0 ** (-((lane % half).astype(f32) * 2.0 / ROT))
    inverse = jnp.where(lane < ROT, inverse, 0.0)
    angles = places.astype(f32)[:, None] * inverse[None, :]
    return jnp.stack([jnp.cos(angles), jnp.sin(angles)])


def flip(value, axis, bit):
    size = lax.axis_size(axis)
    return lax.ppermute(value, axis, [(i, i ^ bit) for i in range(size)])


def tie(*values):
    return lax.optimization_barrier(values)


def after(first, x):
    if isinstance(x, Layer):
        return Layer(tie(first, x.array)[1], x.index)
    return tie(first, x)[1]


jax.tree_util.register_pytree_node(
    Layer, lambda x: ((x.array,), x.index), lambda index, leaves: Layer(*leaves, index)
)


def together(*values):
    leaves, tree = jax.tree.flatten(values)
    return jax.tree.unflatten(tree, tie(*leaves))


def exchange(keep, send, flag, core, chip, backward, works=(), beside_core=()):
    chips = lax.axis_size("seq") // 2
    begin, span = chip * 2 * LEN, 2 * LEN
    got = flip(send, "seq", 1)
    if beside_core:
        got, *came = tie(got, *beside_core)
    even, odd = jnp.where(core == 0, keep, got), jnp.where(core == 0, got, keep)
    if backward:
        total = even + flag(begin + LEN - 1, begin) * odd
    else:
        total = odd + flag(begin + span - 1, begin + LEN) * even
    entered, made, step = None, [], 1
    while step < chips:
        other = flip(total, "seq", 2 * step)
        if len(made) < len(works):
            found = works[len(made)](lambda x, total=total: after(total, x))
            leaves, tree = jax.tree.flatten(found)
            other, *leaves = tie(other, *leaves)
            made.append(jax.tree.unflatten(tree, leaves))
        upper = (chip // step) % 2 == 1
        first = chip - chip % (2 * step)
        middle = first + step
        later, earlier = jnp.where(upper, total, other), jnp.where(upper, other, total)
        if backward:
            passed = jnp.where(upper, 0.0, flag(middle * span - 1, (chip + 1) * span))
            total = earlier + flag(middle * span - 1, first * span) * later
        else:
            passed = jnp.where(upper, flag(chip * span - 1, middle * span), 0.0)
            total = later + flag((middle + step) * span - 1, middle * span) * earlier
        entered = passed * other if entered is None else entered + passed * other
        step *= 2
    if backward:
        for_even, for_odd = odd + flag(begin + span - 1, begin + LEN) * entered, entered
    else:
        for_even, for_odd = entered, even + flag(begin + LEN - 1, begin) * entered
    mine = jnp.where(core == 0, for_even, for_odd)
    theirs = flip(jnp.where(core == 0, for_odd, for_even), "seq", 1)
    return (mine, theirs), made + ([came] if beside_core else [])


def spread(x):
    return [x] + [flip(x, "batch", bit) for bit in (1, 2, 3)]


class Halving:
    def __init__(self, total):
        self.total, self.step = total, 2

    def send(self):
        return flip(self.total[self.total.shape[0] // 2 :], "seq", self.step)

    def tail(self):
        return self.total[self.total.shape[0] // 2 :]

    def add(self, got):
        self.total = self.total[: self.total.shape[0] // 2] + got
        self.step *= 2

    def finish(self):
        while self.step < lax.axis_size("seq"):
            self.add(self.send())
        return self.total


def join(pieces, size):
    order = np.arange(4) ^ lax.axis_index("batch")
    slot = D // size
    feed0, x0, y0, feed1, x1, *packed = pieces
    feed0 = [feed0, x0, y0[: 2 * slot], y0[2 * slot :]]
    feed1 = [feed1[: 2 * slot], x1[: 2 * slot], feed1[2 * slot :], x1[2 * slot :]]
    pieces = [jnp.take(jnp.stack(part), order, axis=0) for part in (feed0, feed1, packed)]
    pieces = [pieces[0], pieces[2][:, : slot + 8], pieces[1], pieces[2][:, slot + 8 :]]
    slot = D // size
    made = [[], [], [], []]
    for feed, packed in (pieces[:2], pieces[2:]):
        made[0].append(
            feed[:, :slot].reshape(4, slot, size, slot).transpose(1, 2, 0, 3).reshape(slot, FF)
        )
        made[1].append(feed[:, slot:].reshape(4 * slot, D))
        packed = packed[:, :slot]
        made[2].append(packed[:, :, :384].swapaxes(0, 1).reshape(slot, 3 * D))
        made[3].append(packed[:, :, 384:].swapaxes(0, 1).reshape(slot, D))
    made = [jnp.stack(part) for part in made]
    lines = pieces[1][:2, slot:]
    vectors = lines[:, :, :slot]
    made += [vectors[:, 0:2], vectors[:, 2:4], vectors[:, 4:7].swapaxes(0, 1)]
    return made + [vectors[:, 7], vectors[:, 7], lines[:, 0, 256 : 256 + FF // size]]


def per_device(
    inputs,
    doc_starts,
    cotangent,
    norm_gain,
    norm_bias,
    qkv_weight,
    qkv_bias,
    out_weight,
    out_bias,
    in_weight,
    in_bias,
    down_weight,
    down_bias,
):
    rows, length = inputs.shape[0], inputs.shape[1]
    tokens = rows * length
    size = lax.axis_size("seq")
    me, column = lax.axis_index("seq"), lax.axis_index("batch")
    core, chip = me % 2, me // 2
    def segment_at(position):
        return jnp.max(jnp.where(doc_starts <= position, doc_starts, 0), axis=1)

    def flag(position, limit):
        return (segment_at(position) < limit).astype(f32)[:, None, None]

    dct = Layer(cosine_table())
    hidden0 = Layer(inputs.reshape(tokens, D))
    cot = Layer(cotangent.reshape(tokens, D))
    qkv_bias_t, out_bias = Layer(qkv_bias.swapaxes(0, 1)), Layer(out_bias)
    in_bias, down_bias = Layer(in_bias), Layer(down_bias)

    tall, fat = sds((tokens, D)), sds((tokens, D), bf16)
    far, far_low = Far((tokens, D)), Far((tokens, D), bf16)
    packed_state = sds((rows, PACK, 128))
    front_outs = [far_low, fat, far_low, far_low, far_low, far, packed_state, packed_state]

    def qkv_parts(layer, order):
        return [
            Layer(qkv_weight, (layer, slice(None), slice(k * D, (k + 1) * D))) for k in order
        ]

    def front_of(layer, *given):
        norms = [Layer(norm_gain, layer), Layer(norm_bias, layer), qkv_bias_t]
        return [*norms, *given, dct, *qkv_parts(layer, (1, 2))]

    quarter_wide = FF // size // 4
    def feed_chunks(layer):
        parts = []
        for g in range(CHUNKS):
            here = slice(g * WIDE, (g + 1) * WIDE)
            parts.append(Layer(in_weight, (layer, slice(None), here)))
            parts.append(Layer(down_weight, (layer, here, slice(None))))
        return parts

    def quarter_weights(layer, quarter):
        shape = (size, 4, quarter_wide)
        pick = functools.partial(lax.dynamic_index_in_dim, index=column ^ quarter, keepdims=False)
        return [
            pick(in_weight[layer].reshape((D,) + shape), axis=2).reshape(D, D),
            pick(in_bias.array[layer].reshape(shape), axis=1).reshape(1, D),
            pick(down_weight[layer].reshape(shape + (D,)), axis=1).reshape(D, D),
        ]

    def feed_grad(seconds, ups, layer, quarters):
        groups = len(seconds)
        scratch = [pltpu.VMEM((groups * tokens, D), bf16)] * 4 + [pltpu.VMEM((2 * D, D), f32)]
        if quarter_wide == HEAD:
            weights = [in_bias, *feed_chunks(layer)]
            scratch += [pltpu.VMEM((D, D), bf16), pltpu.VMEM((1, D), f32), pltpu.VMEM((D, D), bf16)]
        else:
            weights = [w for quarter in quarters for w in quarter_weights(layer, quarter)]
        return call(
            functools.partial(feed_grad_kernel, size, layer, groups, quarters),
            "feed_grad",
            [*weights, *seconds, *ups],
            [sds((len(quarters), D, D))] * 2,
            scratch,
        )

    def packed_grad(first, att_low, gp, up, bits, vectors=(), more=()):
        rows_of = D // 2 + (size // 2 * 8 if vectors else 0)
        return call(
            functools.partial(packed_grad_kernel, size, bits, len(more)),
            "packed_grad",
            [*more, first, att_low, gp, up, *vectors],
            [sds((4, rows_of, D // 2)), (sds if vectors else Far)((4, rows_of, D // 2))] * 2,
            [pltpu.VMEM((D, tokens), f32)] * 2,
        )

    first0, again, second0, fk0, v0, ek0, keep, send, wide0, cot_wide, *prepared = call(
        front_kernel,
        "front",
        [Scalars(doc_starts), cot, hidden0, *front_of(0)],
        front_outs + [far, far, sds((3, rows, LEN, 128)), sds((2, tokens, 128))],
    )
    masks, tables = prepared
    intra_outs = [far_low, far, Far((rows, PAIRS, 2 * LEN, LEN), bf16), tall, tall]

    def near_two(x):
        return [flip(x, "batch", bit) for bit in (1, 2)]

    def last_one(x):
        return flip(x, "batch", 3)

    def do_feed(gate):
        (feed,) = call(feed_kernel, "feed", [gate(second0), in_bias, down_bias, *feed_chunks(0)], [tall])
        return feed

    def do_intra0(gate):
        return intra(0, gate(again), fk0, v0), cots

    cots = [flip(cot_wide.array, "batch", 1), flip(wide0.array, "batch", 2)]

    def intra(layer, first, fk, v):
        operands = [masks, first, *qkv_parts(layer, (0,)), qkv_bias_t, tables, dct, fk, v]
        return call(functools.partial(intra_kernel, layer), "intra", operands, intra_outs)

    entered0, made = exchange(
        keep, send, flag, core, chip, False, [do_feed, do_intra0]
    )
    feed0, ((fq0, eq0, scores0, num0, kt0), (cot_next, second_y)) = made
    (
        den0, att0, att_low0, hidden1, first1, again, second1, fk1, v1, ek1, keep, send, wide1,
    ) = call(
        middle_kernel,
        "middle",
        [masks, num0, kt0, fq0, *entered0, Layer(out_weight, 0), out_bias]
        + [hidden0, feed0, *front_of(1, tables)],
        [far, far, far_low, far] + front_outs + [far],
    )
    row, wide_row = Far((1, D)), Far((1, FF))

    def feed_back(layer, second, up_low, up, hidden, more):
        return call(
            functools.partial(feed_back_kernel, layer),
            "feed_back",
            [second, in_bias, down_bias, up_low, *feed_chunks(layer)]
            + [up, hidden, Layer(norm_gain, layer)],
            [far if more else tall, row, row, wide_row] + more,
        )

    def do_intra1(gate):
        seconds1.append(flip(gate(wide1.array), "batch", 1))
        return intra(1, gate(again), fk1, v1)

    def do_feed_back1(gate):
        made = feed_back(1, gate(second1), cot, cot, hidden1, [far])
        return made, seconds1[0]

    seconds1 = []
    entered1, made = exchange(
        keep, send, flag, core, chip, False, [do_intra1, do_feed_back1]
    )
    fq1, eq1, scores1, num1, kt1 = made[0]
    ((base1, sgain1, sshift1, gib1, feed1), second_next) = made[1]
    att_low1, gnum1, gden1, keep, send = call(
        turn_kernel,
        "turn",
        [masks, num1, kt1, fq1, *entered1, Layer(out_weight, 1), cot],
        [far_low, fat, tall, packed_state, packed_state],
        [pltpu.VMEM((tokens, D), f32)] * 2,
    )

    def intra_back(fq, fk, v, scores, gnum, gden, entered, eq, place):
        return call(
            intra_back_kernel,
            "intra_back",
            [masks, fq, fk, v, scores, gnum, gden, *entered, eq, tables, dct],
            [fat, place, place],
        )

    def do_intra_back1(gate):
        second_x.append(flip(gate(wide0.array), "batch", 1))
        return intra_back(gate(fq1), fk1, v1, scores1, gnum1, gden1, entered1, eq1, far)

    def do_feed_grad1(gate):
        made = feed_grad([after(gate(gnum1), wide1), second_next], [cot_wide, Layer(cot_next)], 1, (0, 2))
        return made, second_x[0]

    second_x = []
    (mine, theirs), made = exchange(
        keep, send, flag, core, chip, True, [do_intra_back1, do_feed_grad1]
    )
    (gq1, gfk1, gval1), ((feed_keep1, feed_send1), second_x) = made
    second_xy = flip(tie(second_x, wide0.array)[1], "batch", 3)
    feed_got1 = flip(feed_send1, "seq", 1)
    mine, theirs, feed_got1 = tie(mine, theirs, feed_got1)
    sums1 = [Halving(feed_keep1[k] + feed_got1[k]) for k in range(2)]
    got = sums1[0].send()
    vector_outs = [Far((1, 3 * D)), row, row]
    packed = sds((tokens, 3 * D), bf16)
    gp1, gqb1, ggain1, gshift1, up0, up_low0, gnum0, gden0, keep, send = call(
        turn_back_kernel,
        "turn_back",
        [masks, mine, theirs, gfk1, gval1, fk1, v1, ek1, tables, dct, gq1]
        + [*qkv_parts(1, (0, 2, 1)), hidden1, Layer(norm_gain, 1), base1]
        + [Layer(out_weight, 0), den0, att0, fq0],
        [packed, *vector_outs, tall, fat, fat, tall, packed_state, packed_state],
    )
    ups0 = [up0]

    def do_feed_back(gate):
        ups0.extend(flip(gate(up0), "batch", bit) for bit in (1, 2))
        return feed_back(0, second0, gate(up_low0), up0, hidden0, []), second_xy, got

    def do_intra_back0(gate):
        ups0.append(flip(gate(up0), "batch", 3))
        return (
            intra_back(gate(fq0), fk0, v0, scores0, gnum0, gden0, entered0, eq0, tall),
            packed_grad(gate(first1), att_low1, gp1, cot, (1, 2)),
            ups0[1:3],
        )

    (mine, theirs), made = exchange(
        keep, send, flag, core, chip, True, [do_feed_back, do_intra_back0]
    )
    ((base0, sgain0, sshift0, gib0), second_xy, got), made = made[0], made[1]
    (gq0, gfk0, gval0), parts1, ups0[1:3] = made
    sums1[0].add(got)
    keep1a, send1a, keep1b, send1b = parts1
    got1a, got1b = flip(send1a.array, "seq", 1), flip(send1b.array, "seq", 1)
    mine, theirs, got1a, got1b = tie(mine, theirs, got1a, got1b)
    gp0, gqb0, ggain0, gshift0, ginputs = call(
        last_kernel,
        "last",
        [masks, mine, theirs, gfk0, gval0, fk0, v0, ek0, tables, dct, gq0]
        + [*qkv_parts(0, (0, 2, 1)), hidden0, Layer(norm_gain, 0), base0],
        [packed, sds((1, 3 * D)), sds((1, D)), sds((1, D)), tall],
    )
    vectors = (ggain0, sgain0, gshift0, sshift0, gqb0, gib0)
    vectors += (ggain1, sgain1, gshift1, sshift1, gqb1, gib1, cot)
    *made, ginputs = packed_grad(
        first0, att_low0, gp0, up_low0, (1, 2), vectors, [Parked(ginputs)]
    )
    made, ups0[3], got = together(made, ups0[3], sums1[1].send())
    sums1[1].add(got)
    keep0a, send0a, keep0b, send0b = made
    got0a, got0b = flip(send0a, "seq", 1), flip(send0b, "seq", 1)
    first1a = flip(keep1a[2:] + got1a[2:], "batch", 1)
    first1b = flip(keep1b[2:] + got1b[2:], "batch", 2)
    grads0, got0a, got0b, got, first1a, first1b = together(
        feed_grad([wide0, *map(Layer, (second_x, second_y, second_xy))], ups0, 0, (0,)),
        got0a, got0b, sums1[0].send(), first1a, first1b,
    )
    feed_keep0, feed_send0 = grads0
    sums1[0].add(got)
    feed_got0 = flip(feed_send0, "seq", 1)
    first0a = flip(keep0a[2:] + got0a[2:], "batch", 1)
    first0b = flip(keep0b[2:] + got0b[2:], "batch", 2)
    (result,) = call(
        result_kernel,
        "result",
        [hidden1, feed1, att_low1, Layer(out_weight, 1), out_bias],
        [far_low],
    )
    feed_got0, first0a, first0b, result, got = together(
        feed_got0, first0a, first0b, result, sums1[1].send()
    )
    sums1[1].add(got)
    sums1 = [part.finish() for part in sums1]
    feed0 = Halving(feed_keep0[0] + feed_got0[0])
    got_feed0 = feed0.send()

    def second(part0, part1, at, bit):
        parts = [sum(x[at] for x in part).reshape(size // 2, -1, D // 2) for part in (part0, part1)]
        both = jnp.concatenate(parts, axis=1).reshape(-1, D // 2)
        return both if bit is None else flip(both, "batch", bit)

    a0, a1 = (keep0a, got0a, first0a), (keep1a, got1a, first1a)
    b0, b1 = (keep0b, got0b, first0b), (keep1b, got1b, first1b)
    second_a, second_b = second(a0, a1, 1, 2), second(b0, b1, 1, 1)
    got_feed0, second_a, second_b = tie(got_feed0, second_a, second_b)

    feed0.add(got_feed0)
    feed0 = feed0.finish()
    packed = Halving(
        jnp.concatenate(
            [second(a0, a1, 0, None) + second_a, second(b0, b1, 0, None) + second_b], axis=1
        )
    )
    other1 = flip(jnp.concatenate([sums1[1], sums1[0]], axis=0), "batch", 2)
    other0, got, other1 = tie(flip(feed0, "batch", 1), packed.send(), other1)
    packed.add(got)
    mine1 = jnp.concatenate(sums1, axis=0) + other1
    other1 = flip(mine1, "batch", 1)
    other0_y = flip(jnp.concatenate([feed0, other0], axis=0), "batch", 2)
    got, other1, other0_y = tie(packed.send(), other1, other0_y)
    packed.add(got)
    pieces = [feed0, other0, other0_y, mine1, other1] + spread(packed.finish())
    slot = D // size
    outs = [
        Far((2, slot, FF)),
        Far((2, FF // size, D)),
        Far((2, slot, 3 * D)),
        Far((2, slot, D)),
        Far((2, 2, slot)),
        Far((2, 2, slot)),
        Far((3, 2, slot)),
        Far((2, slot)),
        Far((2, slot)),
        Far((2, FF // size)),
    ]
    if quarter_wide == HEAD:
        joined = [x.array for x in call(join_kernel, "join", pieces, outs)]
    else:
        joined = join(pieces, size)
    grad_in, grad_down, grad_qkv, grad_out, gain, shift, grad_qkv_b, out_b, down_b, in_b = joined
    return (
        result.array.reshape(rows, length, D),
        ginputs.array.reshape(rows, length, D),
        gain,
        shift,
        grad_qkv,
        grad_qkv_b.swapaxes(0, 1),
        grad_out,
        out_b,
        grad_in,
        in_b,
        grad_down,
        down_b,
    )


def solution(mesh):
    placed = (
        P("batch", "seq", None),
        P("batch", None),
        P("batch", "seq", None),
        P(),
        P(),
        P(),
        P(),
        P(),
        P(),
        P(),
        P(),
        P(),
        P(),
    )
    return jax.shard_map(
        per_device,
        mesh=mesh,
        in_specs=placed,
        out_specs=(
            P("batch", "seq", None),
            P("batch", "seq", None),
            P(None, None, "seq"),
            P(None, None, "seq"),
            P(None, "seq", None),
            P(None, None, "seq"),
            P(None, "seq", None),
            P(None, "seq"),
            P(None, "seq", None),
            P(None, "seq"),
            P(None, "seq", None),
            P(None, "seq"),
        ),
        check_vma=False,
    )
```

```python
import functools
import math

import jax
import jax.numpy as jnp
import numpy as np
from jax import lax
from jax.experimental import pallas as pl
from jax.experimental.pallas import tpu as pltpu
from jax.sharding import PartitionSpec as P

D = 512
HEADS = 8
HEAD = 64
FF = 2048
ROT = 16
LAYERS = 2
NDOC = 4
LEN = 128
PAIRS = HEADS // 2
PACK = 2 * HEAD + 8
WIDE = 512

epsilon = 1e-05
f32, bf16 = jnp.float32, jnp.bfloat16
NN = (((1,), (0,)), ((), ()))
NT = (((1,), (1,)), ((), ()))
TN = (((0,), (0,)), ((), ()))


def dot(a, b, dims=NN):
    return lax.dot_general(a, b, dims, preferred_element_type=f32)


def split(x):
    high = x.astype(bf16)
    return high, (x - high.astype(f32)).astype(bf16)


def sds(shape, dtype=f32):
    return jax.ShapeDtypeStruct(shape, dtype)


def norm_parts(hidden):
    centred = hidden - jnp.mean(hidden, axis=-1, keepdims=True)
    variance = jnp.mean(centred * centred, axis=-1, keepdims=True)
    inverse = lax.rsqrt(variance + epsilon)
    return centred * inverse, inverse


def segment_of(position, starts, row):
    found = jnp.zeros_like(position)
    for k in range(NDOC):
        entry = starts[row, k]
        found = jnp.maximum(found, jnp.where(entry <= position, entry, 0))
    return found


def prepare(starts, masks, tables):
    begin = lax.axis_index("seq") * LEN
    for row in range(masks.shape[1]):
        at_i = begin + lax.broadcasted_iota(jnp.int32, (LEN, 128), 0)
        at_j = begin + lax.broadcasted_iota(jnp.int32, (LEN, 128), 1)
        seg_i, seg_j = segment_of(at_i, starts, row), segment_of(at_j, starts, row)
        last = jnp.int32(0)
        for k in range(NDOC):
            entry = starts[row, k]
            last = jnp.maximum(last, jnp.where(entry <= begin + (LEN - 1), entry, 0))
        masks[0, row] = jnp.where((at_j <= at_i) & (seg_i == seg_j), 1.0, 0.0).astype(f32)
        masks[1, row] = jnp.where(seg_i < begin, 1.0, 0.0).astype(f32)
        masks[2, row] = jnp.where(seg_i == last, 1.0, 0.0).astype(f32)
        lane = lax.broadcasted_iota(jnp.int32, (LEN, 128), 1) % HEAD
        inverse = jnp.zeros((LEN, 128), f32)
        for k in range(ROT // 2):
            here = (lane < ROT) & (lane % (ROT // 2) == k)
            inverse = jnp.where(here, 10000.0 ** (-2.0 * k / ROT), inverse)
        angles = (at_i - seg_i).astype(f32) * inverse
        at = slice(row * LEN, (row + 1) * LEN)
        tables[0, at] = jnp.cos(angles)
        tables[1, at] = jnp.sin(angles)


def masks_of(row, masks):
    return masks[0, row], masks[1, row], masks[2, row]


def low_lanes(rows):
    return lax.broadcasted_iota(jnp.int32, (rows, 128), 1) < HEAD


def read_tables(tables):
    sine = tables[1]
    lane = lax.broadcasted_iota(jnp.int32, sine.shape, 1) % HEAD
    ahead = jnp.where(lane < ROT // 2, -sine, 0.0)
    behind = jnp.where((lane >= ROT // 2) & (lane < ROT), sine, 0.0)
    return tables[0], ahead, behind


def rotate(x, tables):
    base, ahead, behind = tables
    return x * base + pltpu.roll(x, 120, 1) * ahead + pltpu.roll(x, 8, 1) * behind


def rotate_back(g, tables):
    base, ahead, behind = tables
    return g * base + pltpu.roll(g * ahead, 8, 1) + pltpu.roll(g * behind, 120, 1)


def featurize(x, tables, high, low):
    pieces = [rotate(x[:, g * 128 : (g + 1) * 128], tables) for g in range(4)]
    found = []
    for g in range(2):
        a, b = split(jnp.concatenate(pieces[2 * g : 2 * g + 2], axis=1))
        found.append(jnp.exp(dot(a, high) + dot(b, high) + dot(a, low)))
    return jnp.concatenate(found, axis=1)


def unfeaturize(g, tables, high, low):
    found = []
    for k in range(2):
        a, b = split(g[:, k * 256 : (k + 1) * 256])
        back = dot(a, high, NT) + dot(b, high, NT) + dot(a, low, NT)
        found += [rotate_back(back[:, :128], tables), rotate_back(back[:, 128:], tables)]
    return jnp.concatenate(found, axis=1)


def head_ones():
    across = lax.broadcasted_iota(jnp.int32, (256, 256), 0) // HEAD
    along = lax.broadcasted_iota(jnp.int32, (256, 256), 1) // HEAD
    return jnp.where(across == along, 1.0, 0.0).astype(bf16)


def head_sum(x, ones):
    found = []
    for g in range(2):
        a, b = split(x[:, g * 256 : (g + 1) * 256])
        found.append(dot(a, ones) + dot(b, ones))
    return jnp.concatenate(found, axis=1)


def store_halves(keep_ref, send_ref, halves):
    def put(ref, half):
        for row, at, value in halves[half]:
            ref[row, at[0] : at[1], :] = value

    core = lax.axis_index("seq") % 2
    for mine in range(2):

        @pl.when(core == mine)
        def _():
            put(keep_ref, mine)
            put(send_ref, 1 - mine)


def pack_states(rows, left_of, right, norm_of):
    low = low_lanes(HEAD)
    halves = [[], []]
    for row in range(rows):
        at = slice(row * LEN, (row + 1) * LEN)
        left, norm = left_of(row), norm_of(row)
        for pair in range(PAIRS):
            lanes = slice(pair * 128, (pair + 1) * 128)
            both = dot(left[:, lanes], right[at, lanes], TN)
            half, place = pair // 2, pair % 2
            halves[half].append(
                (row, (place * HEAD, (place + 1) * HEAD), jnp.where(low, both[:HEAD], both[HEAD:]))
            )
        for half in range(2):
            pieces = [norm[:, (2 * half + k) * 128 : (2 * half + k + 1) * 128] for k in range(2)]
            block = jnp.concatenate(pieces + [jnp.zeros((6, 128), f32)], axis=0)
            halves[half].append((row, (2 * HEAD, PACK), block))
    return halves


def unpack_state(mine_ref, theirs_ref, row):
    low = low_lanes(HEAD)
    blocks, norms = [], []
    for half in range(2):
        here = lax.axis_index("seq") % 2 == half
        packed = jnp.where(here, mine_ref[row], theirs_ref[row])
        for place in range(2):
            state = packed[place * HEAD : (place + 1) * HEAD]
            both = jnp.concatenate(
                [jnp.where(low, state, 0.0), jnp.where(low, 0.0, state)], axis=0
            )
            blocks.append(split(both))
            norms.append(packed[2 * HEAD + place : 2 * HEAD + place + 1])
    return blocks, jnp.concatenate(norms, axis=1)


def cross_dot(x, block, dims=NN):
    return dot(x, block[0], dims) + dot(x, block[1], dims)


def gelu_parts(lifted):
    phi = 0.5 + 0.5 * lax.erf(lifted * math.sqrt(0.5))
    slope = phi + lifted * (jnp.exp(-0.5 * lifted * lifted) * (1.0 / math.sqrt(2.0 * math.pi)))
    return lifted * phi, slope


def norm_back(grad, xhat, inverse, gain):
    u = grad * gain
    mean_u = jnp.mean(u, axis=-1, keepdims=True)
    mean_ux = jnp.mean(u * xhat, axis=-1, keepdims=True)
    down = (u - mean_u - xhat * mean_ux) * inverse
    return down, jnp.sum(grad * xhat, axis=0, keepdims=True), jnp.sum(grad, axis=0, keepdims=True)


def front_body(layer, masks, hidden, gain, shift, b, tables, dct, wk, wv, outs):
    first_ref, again_ref, second_ref, fk_ref, v_ref, ek_ref, keep_ref, send_ref, wide_ref = outs
    xhat, _ = norm_parts(hidden)
    gains, shifts = gain[...].astype(f32), shift[...].astype(f32)
    first = (xhat * gains[0:1] + shifts[0:1]).astype(bf16)
    first_ref[...] = first
    again_ref[...] = first
    second = (xhat * gains[1:2] + shifts[1:2]).astype(bf16)
    second_ref[...] = second
    wide_ref[...] = second.astype(f32)
    bias = [b[k][layer : layer + 1].astype(f32) for k in range(3)]
    tabs = read_tables(tables)
    high, low = dct[0], dct[1]
    keys = dot(first, wk[...]) + bias[1]
    values = (dot(first, wv[...]) + bias[2]).astype(bf16)
    v_ref[...] = values
    exp_k = featurize(keys, tabs, high, low)
    ek_ref[...] = exp_k
    feat_k = exp_k.astype(bf16)
    fk_ref[...] = feat_k
    rows = hidden.shape[0] // LEN
    wide = feat_k.astype(f32)

    def tailed(row):
        tail = masks_of(row, masks)[2]
        return wide[row * LEN : (row + 1) * LEN] * jnp.concatenate([tail] * 4, axis=1)

    kept = [tailed(row) for row in range(rows)]
    halves = pack_states(
        rows,
        lambda row: kept[row].astype(bf16),
        values,
        lambda row: jnp.sum(kept[row], axis=0, keepdims=True),
    )
    store_halves(keep_ref, send_ref, halves)


def front_kernel(starts, cot, h, gain, shift, b, dct, wk, wv, *outs):
    *outs, masks, tables = outs
    outs[9][...] = cot[...].astype(f32)
    prepare(starts, masks, tables)
    hidden = h[...].astype(f32)
    front_body(0, masks, hidden, gain, shift, b, tables, dct, wk, wv, outs[:9])


def attend(masks, num_ref, kt_ref, fq_ref, mine_ref, theirs_ref, den_ref, att_ref, low_ref):
    rows = num_ref.shape[0] // LEN
    ones = head_ones()
    for row in range(rows):
        at = slice(row * LEN, (row + 1) * LEN)
        cross = masks_of(row, masks)[1]
        cross4 = jnp.concatenate([cross] * 4, axis=1)
        blocks, norm = unpack_state(mine_ref, theirs_ref, row)
        fq = fq_ref[at]
        far = jnp.concatenate(
            [cross_dot(fq[:, p * 128 : (p + 1) * 128], blocks[p]) for p in range(PAIRS)], axis=1
        )
        num = num_ref[at] + cross4 * far
        den = head_sum(fq.astype(f32) * (kt_ref[at] + cross4 * norm), ones)
        att = num / den
        den_ref[at] = den
        att_ref[at] = att
        low_ref[at] = att.astype(bf16)
    begin_writing(den_ref, att_ref, low_ref)


def middle_kernel(
    masks, num, kt, fq0, mine, theirs, ow, ob, h, feed, gain, shift, b, tables, dct, wk, wv,
    den, att, att_low, h2, *outs,
):
    attend(masks, num, kt, fq0, mine, theirs, den, att, att_low)
    hidden = h[...].astype(f32) + (dot(att_low[...], ow[...]) + ob[0:1].astype(f32)) + feed[...]
    h2[...] = hidden
    front_body(1, masks, hidden, gain, shift, b, tables, dct, wk, wv, outs)


def attend_back(masks, up, ow, den, att, fq, gnum, gden, keep_ref, send_ref):
    ga = dot(up, ow[...], NT)
    den_v = den[...]
    gn = (ga / den_v).astype(bf16)
    gnum[...] = gn
    gd = -head_sum(ga * att[...], head_ones()) / den_v
    gden[...] = gd
    rows = up.shape[0] // LEN
    wide = fq[...].astype(f32)

    def crossed(row):
        cross = masks_of(row, masks)[1]
        return wide[row * LEN : (row + 1) * LEN] * jnp.concatenate([cross] * 4, axis=1)

    kept = [crossed(row) for row in range(rows)]
    halves = pack_states(
        rows,
        lambda row: kept[row].astype(bf16),
        gn,
        lambda row: jnp.sum(kept[row] * gd[row * LEN : (row + 1) * LEN], axis=0, keepdims=True),
    )
    store_halves(keep_ref, send_ref, halves)


def turn_kernel(
    masks, num, kt, fq, mine, theirs, ow, cot, att_low, gnum, gden, keep, send, den, att,
):
    attend(masks, num, kt, fq, mine, theirs, den, att, att_low)
    attend_back(masks, cot[...], ow, den, att, fq, gnum, gden, keep, send)


CHUNKS = FF // WIDE


def feed_kernel(second, ib, db, *refs):
    chunks, feed = refs[:-1], refs[-1]
    total = jnp.broadcast_to(db[0:1].astype(f32), feed.shape)
    for g in range(CHUNKS):
        iw, dw = chunks[2 * g : 2 * g + 2]
        bias = ib[0:1, g * WIDE : (g + 1) * WIDE].astype(f32)
        lifted = dot(second[...], iw[...]) + bias
        total = total + dot(gelu_parts(lifted)[0].astype(bf16), dw[...])
    feed[...] = total


def feed_back_kernel(layer, second, ib, db, up_low, *refs):
    chunks, (up, h, gain, base, gain_out, shift_out, gib, *feed) = (
        refs[: 2 * CHUNKS],
        refs[2 * CHUNKS :],
    )
    total = jnp.broadcast_to(db[layer : layer + 1].astype(f32), base.shape)
    back = jnp.zeros(base.shape, f32)
    low_up = up_low[...]
    for g in range(CHUNKS):
        lanes = slice(g * WIDE, (g + 1) * WIDE)
        iw, dw = (part[...] for part in chunks[2 * g : 2 * g + 2])
        lifted = dot(second[...], iw) + ib[layer : layer + 1, lanes].astype(f32)
        value, slope = gelu_parts(lifted)
        if feed:
            total = total + dot(value.astype(bf16), dw)
        low = (dot(low_up, dw, NT) * slope).astype(bf16)
        gib[:, lanes] = jnp.sum(low.astype(f32), axis=0, keepdims=True)
        back = back + dot(low, iw, NT)
    if feed:
        feed[0][...] = total
    xhat, inverse = norm_parts(h[...].astype(f32))
    gains = gain[...].astype(f32)
    part, gain_out[...], shift_out[...] = norm_back(back, xhat, inverse, gains[1:2])
    base[...] = up[...].astype(f32) + part


def intra_kernel(layer, masks, first, wq, b, tables, dct, fk, v, fq, eq, scores, num, kt):
    queries = dot(first[...], wq[...]) + b[0][layer : layer + 1].astype(f32)
    exp_q = featurize(queries, read_tables(tables), dct[0], dct[1])
    eq[...] = exp_q
    fq[...] = exp_q.astype(bf16)
    low = low_lanes(LEN)
    even = jnp.where(low, 1.0, 0.0).astype(bf16)
    odd = jnp.where(low, 0.0, 1.0).astype(bf16)
    for row in range(fq.shape[0] // LEN):
        at = slice(row * LEN, (row + 1) * LEN)
        intra = masks_of(row, masks)[0]
        kt[at] = dot(intra.astype(bf16), fk[at])
        twice = jnp.concatenate([intra, intra], axis=0)
        for pair in range(PAIRS):
            lanes = slice(pair * 128, (pair + 1) * 128)
            q = fq[at, lanes]
            both = jnp.concatenate([q * even, q * odd], axis=0)
            rounded = (dot(both, fk[at, lanes], NT) * twice).astype(bf16)
            scores[row, pair] = rounded
            out = dot(rounded, v[at, lanes])
            num[at, lanes] = jnp.where(low, out[:LEN], out[LEN:])


def intra_back_kernel(
    masks, fq, fk, v, scores, gnum, gden, mine, theirs, eq, tables, dct, gq, gfk, gval
):
    low = low_lanes(LEN)
    even = jnp.where(low, 1.0, 0.0).astype(bf16)
    odd = jnp.where(low, 0.0, 1.0).astype(bf16)
    grad = []
    for row in range(fq.shape[0] // LEN):
        at = slice(row * LEN, (row + 1) * LEN)
        intra, cross, _ = masks_of(row, masks)
        twice = jnp.concatenate([intra, intra], axis=0)
        blocks, norm = unpack_state(mine, theirs, row)
        queries = []
        for pair in range(PAIRS):
            lanes = slice(pair * 128, (pair + 1) * 128)
            gn, gd, q, k = gnum[at, lanes], gden[at, lanes], fq[at, lanes], fk[at, lanes]
            both = jnp.concatenate([gn * even, gn * odd], axis=0)
            turned = pltpu.roll(gd, HEAD, 1)
            dens = jnp.concatenate(
                [jnp.where(low, gd, turned), jnp.where(low, turned, gd)], axis=0
            )
            gs = ((dot(both, v[at, lanes], NT) + dens) * twice).astype(bf16)
            near = dot(gs, k)
            far = cross_dot(gn, blocks[pair], NT) + gd * norm[:, lanes]
            queries.append(jnp.where(low, near[:LEN], near[LEN:]) + cross * far)
            gfk[at, lanes] = jnp.where(low, dot(gs[:LEN], q, TN), dot(gs[LEN:], q, TN))
            sl = scores[row, pair]
            gval[at, lanes] = jnp.where(low, dot(sl[:LEN], gn, TN), dot(sl[LEN:], gn, TN))
        grad.append(jnp.concatenate(queries, axis=1))
    begin_writing(gfk, gval)
    turned = unfeaturize(
        jnp.concatenate(grad, axis=0) * eq[...], read_tables(tables), dct[0], dct[1]
    )
    gq[...] = turned.astype(bf16)


def packed_back(masks, mine, theirs, gq, gfk, gval, fk, v, ek, tables, dct, gp, gqb):
    keys, values = [], []
    for row in range(fk.shape[0] // LEN):
        at = slice(row * LEN, (row + 1) * LEN)
        tail = masks_of(row, masks)[2]
        blocks, norm = unpack_state(mine, theirs, row)
        key_row, value_row = [], []
        for pair in range(PAIRS):
            lanes = slice(pair * 128, (pair + 1) * 128)
            far = cross_dot(v[at, lanes], blocks[pair], NT) + norm[:, lanes]
            key_row.append(gfk[at, lanes] + tail * far)
            value_row.append(gval[at, lanes] + tail * cross_dot(fk[at, lanes], blocks[pair]))
        keys.append(jnp.concatenate(key_row, axis=1))
        values.append(jnp.concatenate(value_row, axis=1))
    gp[:, 2 * D :] = jnp.concatenate(values, axis=0).astype(bf16)
    gp[:, :D] = gq[...]
    keys = unfeaturize(
        jnp.concatenate(keys, axis=0) * ek[...], read_tables(tables), dct[0], dct[1]
    )
    gp[:, D : 2 * D] = keys.astype(bf16)
    gqb[...] = jnp.sum(gp[...].astype(f32), axis=0, keepdims=True)


def upstream_back(base, hidden, gp, weights, gain, gain_out, shift_out):
    gfirst = sum(
        dot(gp[:, k * D : (k + 1) * D], part[...], NT) for k, part in zip((0, 2, 1), weights)
    )
    xhat, inverse = norm_parts(hidden)
    part, gain_out[...], shift_out[...] = norm_back(
        gfirst, xhat, inverse, gain[...].astype(f32)[0:1]
    )
    return base[...] + part


def turn_back_kernel(
    masks, mine, theirs, gfk, gval, fk, v, ek, tables, dct, gq, wq, wv, wk, h, gain, base, ow, den, att, fq,
    gp, gqb, ggain, gshift, up_ref, up_low, gnum, gden, keep, send,
):
    packed_back(masks, mine, theirs, gq, gfk, gval, fk, v, ek, tables, dct, gp, gqb)
    up = upstream_back(base, h[...], gp, (wq, wv, wk), gain, ggain, gshift)
    up_ref[...] = up
    low = up.astype(bf16)
    up_low[...] = low
    attend_back(masks, low, ow, den, att, fq, gnum, gden, keep, send)


def result_kernel(h, feed, att_low, ow, ob, result):
    hidden = h[...] + (dot(att_low[...], ow[...]) + ob[1:2].astype(f32)) + feed[...]
    result[...] = hidden.astype(bf16)


def last_kernel(
    masks, mine, theirs, gfk, gval, fk, v, ek, tables, dct, gq, wq, wv, wk, h, gain, base,
    gp, gqb, ggain, gshift, ginputs,
):
    packed_back(masks, mine, theirs, gq, gfk, gval, fk, v, ek, tables, dct, gp, gqb)
    weights = (wq, wv, wk)
    ginputs[...] = upstream_back(base, h[...].astype(f32), gp, weights, gain, ggain, gshift)


def gathered(size, x, flat, held):
    block = flat.shape[0] // size
    flat[...] = x.astype(f32).T
    for place in range(size):
        source = block_at(size, place)
        held[place * block : (place + 1) * block, :] = flat[
            pl.ds(pl.multiple_of(source * block, block), block), :
        ]
    return held[...].astype(bf16)


def reversed_bits(value, count):
    return sum(((value >> k) & 1) << (count - 1 - k) for k in range(count))


def block_at(size, place):
    return reversed_bits(place, size.bit_length() - 1) ^ lax.axis_index("seq")


def pick_quarter(size, layer, q, ib, chunks, iw_q, ib_q, dw_q):
    wide = FF // size
    rows = lax.broadcasted_iota(jnp.int32, (128, 128), 0) - HEAD * (q % 2)
    lanes = lax.broadcasted_iota(jnp.int32, (128, 128), 1)
    left = jnp.where((rows == lanes) & (lanes < HEAD), 1.0, 0.0).astype(bf16)
    right = jnp.where((rows == lanes - HEAD) & (lanes >= HEAD), 1.0, 0.0).astype(bf16)
    quarter = wide // 4
    for pair in range(size // 2):
        iw, dw = chunks[2 * pair : 2 * pair + 2]
        here = slice(pair * 128, (pair + 1) * 128)
        at = [k * wide + (q // 2) * 128 for k in range(2)]
        cut = [pl.ds(pl.multiple_of(begin, 128), 128) for begin in at]
        iw_q[:, here] = (dot(iw[:, cut[0]], left) + dot(iw[:, cut[1]], right)).astype(bf16)
        cut = [pl.ds(pl.multiple_of(pair * 2 * wide + begin, 128), 128) for begin in at]
        bias = [ib[:, part] for part in cut]
        ib_q[:, here] = (dot(bias[0], left) + dot(bias[1], right))[layer : layer + 1]
        for k in range(2):
            s = 2 * pair + k
            picked = pl.ds(pl.multiple_of(k * wide + q * quarter, quarter), quarter)
            dw_q[s * quarter : (s + 1) * quarter, :] = dw[picked, :]


def feed_grad_kernel(size, layer, groups, quarters, *refs):
    count = len(quarters)
    own = FF // size // 4 == HEAD
    weights, refs = refs[: 1 + 2 * CHUNKS if own else 3 * count], refs[1 + 2 * CHUNKS if own else 3 * count :]
    seconds, ups, refs = refs[:groups], refs[groups : 2 * groups], refs[2 * groups :]
    keep, send, s_all, u_all, act, lift, out, *picked = refs
    tokens = s_all.shape[0] // groups
    block = D // size
    for n, quarter in enumerate(quarters):
        if own:
            q = lax.axis_index("batch") ^ quarter
            pick_quarter(size, layer, q, weights[0], weights[1:], *picked)
            iw, ib, dw = picked
        else:
            iw, ib, dw = weights[3 * n : 3 * n + 3]
        for k in range(groups):
            at = slice(k * tokens, (k + 1) * tokens)
            if n == 0:
                s_all[at], u_all[at] = seconds[k][...].astype(bf16), ups[k][...].astype(bf16)
            lifted = dot(s_all[at], iw[...]) + ib[...].astype(f32)
            value, slope = gelu_parts(lifted)
            act[at] = value.astype(bf16)
            lift[at] = (dot(u_all[at], dw[...], NT) * slope).astype(bf16)
        for part, grads in enumerate(
            (dot(s_all[...], lift[...], TN), dot(act[...], u_all[...], TN))
        ):
            for s in range(size):
                place = reversed_bits(s ^ lax.axis_index("seq"), size.bit_length() - 1)
                at = pl.multiple_of((2 * place + part) * block, block)
                out[pl.ds(at, block), :] = grads[s * block : (s + 1) * block]
        keep[n], send[n] = out[:D], out[D:]


def chosen(refs, index):
    value = refs[0][...]
    for k in range(1, len(refs)):
        value = jnp.where(index == k, refs[k][...], value)
    return value


def join_feed_kernel(feed0, x0, y0, feed1, x1, in_out, down_out):
    me = lax.axis_index("batch")
    block = in_out.shape[1]
    low, two = low_lanes(block), 2 * block
    for layer in range(2):
        if layer == 0:
            held = (feed0, x0, y0.at[:two], y0.at[two:])
        else:
            held = (feed1.at[:two], x1.at[:two], feed1.at[two:], x1.at[two:])
        for pair in range(2):
            left, right = (chosen(held, (2 * pair + k) ^ me) for k in range(2))
            down_out[layer, 2 * pair * block : (2 * pair + 1) * block, :] = left[block:]
            down_out[layer, (2 * pair + 1) * block : (2 * pair + 2) * block, :] = right[block:]
            for tile in range(D // 128):
                lanes = slice(tile * 128, (tile + 1) * 128)
                a, b = left[:block, lanes], right[:block, lanes]
                at = 2 * tile * 256 + pair * 128
                in_out[layer, :, at : at + 128] = jnp.where(low, a, pltpu.roll(b, 64, 1))
                in_out[layer, :, at + 256 : at + 384] = jnp.where(low, pltpu.roll(a, 64, 1), b)


def join_packed_kernel(*refs):
    pieces, outs = refs[:4], refs[4:]
    qkv_out, out_out, gain_out, shift_out, qkvb_out, outb_out, downb_out, inb_out = outs
    me = lax.axis_index("batch")
    block = qkv_out.shape[1]
    for layer in range(2):
        begin = layer * (block + 8)
        for q in range(4):
            packed = chosen(pieces, q ^ me)[begin : begin + block + 8 * (1 - layer)]
            qkv_out[layer, :, q * 384 : (q + 1) * 384] = packed[:block, :384]
            out_out[layer, :, q * 128 : (q + 1) * 128] = packed[:block, 384:]
            if layer == 0 and q < 2:
                lines = packed[block:]
                gain_out[q] = lines[0:2, :block]
                shift_out[q] = lines[2:4, :block]
                for k in range(3):
                    qkvb_out[k, q : q + 1, :] = lines[4 + k : 5 + k, :block]
                outb_out[q : q + 1, :] = lines[7:8, :block]
                downb_out[q : q + 1, :] = lines[7:8, :block]
                inb_out[q : q + 1, :] = lines[0:1, 256 : 256 + inb_out.shape[1]]


PARTS = ((0, 256), (256, 512))


def standing(quarter, bit):
    return jnp.where(bit == 1, (quarter % 2) * 2 + quarter // 2, quarter)


def packed_grad_kernel(size, bits, more, *refs):
    first, att_low, gp, up, *refs = refs[more:]
    *vectors, keep_a, send_a, keep_b, send_b, f1, h1 = refs
    block, under = D // size, 8 if vectors else 0
    half, me = size // 2, lax.axis_index("batch")
    for source, right, wide, begin in ((first, gp, 384, 0), (att_low, up, 128, 384)):
        left = gathered(size, source[...], f1, h1)
        for q in range(4):
            out = dot(left, right[:, q * wide : (q + 1) * wide])
            for (low, high), bit, refs in zip(PARTS, bits, ((keep_a, send_a), (keep_b, send_b))):
                lanes = max(low, begin), min(high, begin + wide)
                if lanes[0] >= lanes[1]:
                    continue
                at = standing(q ^ me, bit)
                for place in range(size):
                    here = (place % half) * (block + under)
                    refs[place // half][
                        at, here : here + block, lanes[0] - low : lanes[1] - low
                    ] = out[
                        place * block : (place + 1) * block, lanes[0] - begin : lanes[1] - begin
                    ]
    if vectors:
        put_lines(size, bits, vectors, up, ((keep_a, send_a), (keep_b, send_b)))


def put_lines(size, bits, vectors, up, parts):
    block, wide, me = D // size, FF // size, lax.axis_index("batch")
    held = []
    for *norms, gqb, gib, ups in ((*vectors[:6], up), vectors[6:]):
        gob = jnp.sum(ups[...].astype(f32), axis=0, keepdims=True)
        rows = [part[...] for part in norms]
        rows += [gqb[:, k * D : (k + 1) * D] for k in range(3)] + [gob]
        held.append((jnp.concatenate(rows, axis=0), jnp.broadcast_to(gib[...], (8, FF))))
    for place in range(size):
        source = block_at(size, place)
        here = (place % (size // 2)) * (block + 8) + block
        a_ref, b_ref = (refs[place // (size // 2)] for refs in parts)
        for layer, (rows, line) in enumerate(held):
            a_ref[standing(layer ^ me, bits[0]), here : here + 8, :128] = pltpu.roll(
                rows, (D - source * block) % D, 1
            )[:, :128]
            b_ref[standing(layer ^ me, bits[1]), here : here + 8, :] = pltpu.roll(
                line, (FF - source * wide) % FF, 1
            )[:, :256]
            a_ref[standing(layer ^ me, bits[0]), here : here + 8, 128:] = jnp.zeros((8, 128), f32)
        for k in (2, 3):
            for ref, bit in ((a_ref, bits[0]), (b_ref, bits[1])):
                ref[standing(k ^ me, bit), here : here + 8, :] = jnp.zeros((8, 256), f32)


class Layer:
    def __init__(self, array, index=None):
        self.array, self.index = array, index
        self.shape = array.shape if index is None else jax.eval_shape(lambda x: x[index], array).shape


class Far:
    def __init__(self, shape, dtype=f32):
        self.shape, self.dtype = shape, dtype


class Parked:
    def __init__(self, array):
        self.array = array


class Scalars:
    def __init__(self, array):
        self.array = array


class Source:
    def __init__(self, here, there, semaphore):
        self.here, self.copy = here, pltpu.make_async_copy(there, here, semaphore)
        self.shape, self.copying = here.shape, True
        self.copy.start()

    def __getitem__(self, at):
        if self.copying:
            self.copy.wait()
            self.copying = False
        return self.here[at]


class Target:
    def __init__(self, here, there, semaphore):
        self.here, self.copy = here, pltpu.make_async_copy(here, there, semaphore)
        self.shape, self.started = here.shape, False

    def __getitem__(self, at):
        return self.here[at]

    def __setitem__(self, at, value):
        assert not self.started
        self.here[at] = value
        if at is Ellipsis:
            self.start()

    def start(self):
        if not self.started:
            self.copy.start()
            self.started = True


def begin_writing(*results):
    for result in results:
        if isinstance(result, Target):
            result.start()


def call(kernel, name, operands, outs, scratch=()):
    arrays = [getattr(operand, "array", operand) for operand in operands]
    copied = [k for k, operand in enumerate(operands) if isinstance(operand, Layer)]
    written = [k for k, out in enumerate(outs) if isinstance(out, Far)]
    parked = [k for k, operand in enumerate(operands) if isinstance(operand, Parked)]
    arrays = [
        a
        if isinstance(o, Scalars)
        else pltpu.with_memory_space_constraint(a, pltpu.HBM if isinstance(o, Layer) else pltpu.VMEM)
        for o, a in zip(operands, arrays)
    ]
    vmem, smem = pl.BlockSpec(memory_space=pltpu.VMEM), pl.BlockSpec(memory_space=pltpu.SMEM)
    hbm = pl.BlockSpec(memory_space=pltpu.HBM)
    own = 1 + len(copied) + len(written)
    shown = len(outs)
    outs = list(outs) + [Far(arrays[k].shape, arrays[k].dtype) for k in parked]

    def body(*refs):
        ins, results = list(refs[: len(operands)]), list(refs[len(operands) :][: len(outs)])
        semaphores, *buffers = refs[len(operands) + len(outs) :]
        results, places = results[:shown], results[shown:]
        copies = [
            pltpu.make_async_copy(ins[k], place, semaphores.at[own - 1 + n])
            for n, (k, place) in enumerate(zip(parked, places))
        ]
        for copy in copies:
            copy.start()
        for n, k in enumerate(copied):
            index = operands[k].index
            there = ins[k] if index is None else ins[k].at[index]
            ins[k] = Source(buffers[n], there, semaphores.at[n])
        for n, k in enumerate(written):
            n += len(copied)
            results[k] = Target(buffers[n], results[k], semaphores.at[n])
        kernel(*ins, *results, *buffers[own - 1 :])
        assert not any(ins[k].copying for k in copied), name
        for k in written:
            results[k].start()
        for k in written:
            results[k].copy.wait()
        for copy in copies:
            copy.wait()

    found = pl.pallas_call(
        body,
        name=name,
        in_specs=[
            smem if isinstance(o, Scalars) else hbm if isinstance(o, Layer) else vmem
            for o in operands
        ],
        out_specs=[hbm if isinstance(o, Far) else vmem for o in outs],
        out_shape=[(pltpu.HBM if isinstance(o, Far) else pltpu.VMEM)(o.shape, o.dtype) for o in outs],
        scratch_shapes=[
            pltpu.SemaphoreType.DMA((max(own - 1 + len(parked), 1),)),
            *[pltpu.VMEM(operands[k].shape, arrays[k].dtype) for k in copied],
            *[pltpu.VMEM(outs[k].shape, outs[k].dtype) for k in written],
            *scratch,
        ],
        cost_estimate=pl.CostEstimate(flops=1024, bytes_accessed=1024, transcendentals=0),
        compiler_params=pltpu.CompilerParams(vmem_limit_bytes=26 * 1024 * 1024),
    )(*arrays)
    return [Layer(x) if isinstance(o, Far) else x for x, o in zip(found, outs)]


def cosine_table():
    frequency = np.arange(HEAD, dtype=np.float64)[:, None]
    columns = np.arange(HEAD, dtype=np.float64)[None, :]
    entries = np.cos(math.pi * (2.0 * columns + 1.0) * frequency / (2.0 * HEAD))
    entries = entries * math.sqrt(2.0 / HEAD)
    entries[0] *= math.sqrt(0.5)
    wide = np.kron(np.eye(4), entries.T)
    high = wide.astype(np.float32).astype(bf16)
    low = (wide.astype(np.float32) - high.astype(np.float32)).astype(bf16)
    return jnp.asarray(np.stack([high, low]))


def rotary_tables(places):
    lane = jnp.arange(128) % HEAD
    half = ROT // 2
    inverse = 10000.0 ** (-((lane % half).astype(f32) * 2.0 / ROT))
    inverse = jnp.where(lane < ROT, inverse, 0.0)
    angles = places.astype(f32)[:, None] * inverse[None, :]
    return jnp.stack([jnp.cos(angles), jnp.sin(angles)])


def flip(value, axis, bit):
    size = lax.axis_size(axis)
    return lax.ppermute(value, axis, [(i, i ^ bit) for i in range(size)])


def tie(*values):
    return lax.optimization_barrier(values)


def after(first, x):
    if isinstance(x, Layer):
        return Layer(tie(first, x.array)[1], x.index)
    return tie(first, x)[1]


jax.tree_util.register_pytree_node(
    Layer, lambda x: ((x.array,), x.index), lambda index, leaves: Layer(*leaves, index)
)


def together(*values):
    leaves, tree = jax.tree.flatten(values)
    return jax.tree.unflatten(tree, tie(*leaves))


def exchange(keep, send, flag, core, chip, backward, works=(), beside_core=()):
    chips = lax.axis_size("seq") // 2
    begin, span = chip * 2 * LEN, 2 * LEN
    got = flip(send, "seq", 1)
    if beside_core:
        got, *came = tie(got, *beside_core)
    even, odd = jnp.where(core == 0, keep, got), jnp.where(core == 0, got, keep)
    if backward:
        total = even + flag(begin + LEN - 1, begin) * odd
    else:
        total = odd + flag(begin + span - 1, begin + LEN) * even
    entered, made, step = None, [], 1
    while step < chips:
        other = flip(total, "seq", 2 * step)
        if len(made) < len(works):
            found = works[len(made)](lambda x, total=total: after(total, x))
            leaves, tree = jax.tree.flatten(found)
            other, *leaves = tie(other, *leaves)
            made.append(jax.tree.unflatten(tree, leaves))
        upper = (chip // step) % 2 == 1
        first = chip - chip % (2 * step)
        middle = first + step
        later, earlier = jnp.where(upper, total, other), jnp.where(upper, other, total)
        if backward:
            passed = jnp.where(upper, 0.0, flag(middle * span - 1, (chip + 1) * span))
            total = earlier + flag(middle * span - 1, first * span) * later
        else:
            passed = jnp.where(upper, flag(chip * span - 1, middle * span), 0.0)
            total = later + flag((middle + step) * span - 1, middle * span) * earlier
        entered = passed * other if entered is None else entered + passed * other
        step *= 2
    if backward:
        for_even, for_odd = odd + flag(begin + span - 1, begin + LEN) * entered, entered
    else:
        for_even, for_odd = entered, even + flag(begin + LEN - 1, begin) * entered
    mine = jnp.where(core == 0, for_even, for_odd)
    theirs = flip(jnp.where(core == 0, for_odd, for_even), "seq", 1)
    return (mine, theirs), made + ([came] if beside_core else [])


def spread(x):
    return [x] + [flip(x, "batch", bit) for bit in (1, 2, 3)]


class Halving:
    def __init__(self, total):
        self.total, self.step = total, 2

    def send(self):
        return flip(self.total[self.total.shape[0] // 2 :], "seq", self.step)

    def tail(self):
        return self.total[self.total.shape[0] // 2 :]

    def add(self, got):
        self.total = self.total[: self.total.shape[0] // 2] + got
        self.step *= 2

    def finish(self):
        while self.step < lax.axis_size("seq"):
            self.add(self.send())
        return self.total


def join(pieces, size):
    order = np.arange(4) ^ lax.axis_index("batch")
    slot = D // size
    feed0, x0, y0, feed1, x1, *packed = pieces
    feed0 = [feed0, x0, y0[: 2 * slot], y0[2 * slot :]]
    feed1 = [feed1[: 2 * slot], x1[: 2 * slot], feed1[2 * slot :], x1[2 * slot :]]
    pieces = [jnp.take(jnp.stack(part), order, axis=0) for part in (feed0, feed1, packed)]
    pieces = [pieces[0], pieces[2][:, : slot + 8], pieces[1], pieces[2][:, slot + 8 :]]
    slot = D // size
    made = [[], [], [], []]
    for feed, packed in (pieces[:2], pieces[2:]):
        made[0].append(
            feed[:, :slot].reshape(4, slot, size, slot).transpose(1, 2, 0, 3).reshape(slot, FF)
        )
        made[1].append(feed[:, slot:].reshape(4 * slot, D))
        packed = packed[:, :slot]
        made[2].append(packed[:, :, :384].swapaxes(0, 1).reshape(slot, 3 * D))
        made[3].append(packed[:, :, 384:].swapaxes(0, 1).reshape(slot, D))
    made = [jnp.stack(part) for part in made]
    lines = pieces[1][:2, slot:]
    vectors = lines[:, :, :slot]
    made += [vectors[:, 0:2], vectors[:, 2:4], vectors[:, 4:7].swapaxes(0, 1)]
    return made + [vectors[:, 7], vectors[:, 7], lines[:, 0, 256 : 256 + FF // size]]


def per_device(
    inputs,
    doc_starts,
    cotangent,
    norm_gain,
    norm_bias,
    qkv_weight,
    qkv_bias,
    out_weight,
    out_bias,
    in_weight,
    in_bias,
    down_weight,
    down_bias,
):
    rows, length = inputs.shape[0], inputs.shape[1]
    tokens = rows * length
    size = lax.axis_size("seq")
    me, column = lax.axis_index("seq"), lax.axis_index("batch")
    core, chip = me % 2, me // 2
    def segment_at(position):
        return jnp.max(jnp.where(doc_starts <= position, doc_starts, 0), axis=1)

    def flag(position, limit):
        return (segment_at(position) < limit).astype(f32)[:, None, None]

    dct = Layer(cosine_table())
    hidden0 = Layer(inputs.reshape(tokens, D))
    cot = Layer(cotangent.reshape(tokens, D))
    qkv_bias_t, out_bias = Layer(qkv_bias.swapaxes(0, 1)), Layer(out_bias)
    in_bias, down_bias = Layer(in_bias), Layer(down_bias)

    tall, fat = sds((tokens, D)), sds((tokens, D), bf16)
    far, far_low = Far((tokens, D)), Far((tokens, D), bf16)
    packed_state = sds((rows, PACK, 128))
    front_outs = [far_low, fat, far_low, far_low, far_low, far, packed_state, packed_state]

    def qkv_parts(layer, order):
        return [
            Layer(qkv_weight, (layer, slice(None), slice(k * D, (k + 1) * D))) for k in order
        ]

    def front_of(layer, *given):
        norms = [Layer(norm_gain, layer), Layer(norm_bias, layer), qkv_bias_t]
        return [*norms, *given, dct, *qkv_parts(layer, (1, 2))]

    quarter_wide = FF // size // 4
    def feed_chunks(layer):
        parts = []
        for g in range(CHUNKS):
            here = slice(g * WIDE, (g + 1) * WIDE)
            parts.append(Layer(in_weight, (layer, slice(None), here)))
            parts.append(Layer(down_weight, (layer, here, slice(None))))
        return parts

    def quarter_weights(layer, quarter):
        shape = (size, 4, quarter_wide)
        pick = functools.partial(lax.dynamic_index_in_dim, index=column ^ quarter, keepdims=False)
        return [
            pick(in_weight[layer].reshape((D,) + shape), axis=2).reshape(D, D),
            pick(in_bias.array[layer].reshape(shape), axis=1).reshape(1, D),
            pick(down_weight[layer].reshape(shape + (D,)), axis=1).reshape(D, D),
        ]

    def feed_grad(seconds, ups, layer, quarters):
        groups = len(seconds)
        scratch = [pltpu.VMEM((groups * tokens, D), bf16)] * 4 + [pltpu.VMEM((2 * D, D), f32)]
        if quarter_wide == HEAD:
            weights = [in_bias, *feed_chunks(layer)]
            scratch += [pltpu.VMEM((D, D), bf16), pltpu.VMEM((1, D), f32), pltpu.VMEM((D, D), bf16)]
        else:
            weights = [w for quarter in quarters for w in quarter_weights(layer, quarter)]
        return call(
            functools.partial(feed_grad_kernel, size, layer, groups, quarters),
            "feed_grad",
            [*weights, *seconds, *ups],
            [sds((len(quarters), D, D))] * 2,
            scratch,
        )

    def packed_grad(first, att_low, gp, up, bits, vectors=(), more=()):
        rows_of = D // 2 + (size // 2 * 8 if vectors else 0)
        return call(
            functools.partial(packed_grad_kernel, size, bits, len(more)),
            "packed_grad",
            [*more, first, att_low, gp, up, *vectors],
            [sds((4, rows_of, D // 2)), (sds if vectors else Far)((4, rows_of, D // 2))] * 2,
            [pltpu.VMEM((D, tokens), f32)] * 2,
        )

    first0, again, second0, fk0, v0, ek0, keep, send, wide0, cot_wide, *prepared = call(
        front_kernel,
        "front",
        [Scalars(doc_starts), cot, hidden0, *front_of(0)],
        front_outs + [far, far, sds((3, rows, LEN, 128)), sds((2, tokens, 128))],
    )
    masks, tables = prepared
    intra_outs = [far_low, far, Far((rows, PAIRS, 2 * LEN, LEN), bf16), tall, tall]

    def near_two(x):
        return [flip(x, "batch", bit) for bit in (1, 2)]

    def last_one(x):
        return flip(x, "batch", 3)

    def do_feed(gate):
        (feed,) = call(feed_kernel, "feed", [gate(second0), in_bias, down_bias, *feed_chunks(0)], [tall])
        return feed

    def do_intra0(gate):
        return intra(0, gate(again), fk0, v0), cots

    cots = [flip(cot_wide.array, "batch", 1), flip(wide0.array, "batch", 2)]

    def intra(layer, first, fk, v):
        operands = [masks, first, *qkv_parts(layer, (0,)), qkv_bias_t, tables, dct, fk, v]
        return call(functools.partial(intra_kernel, layer), "intra", operands, intra_outs)

    entered0, made = exchange(
        keep, send, flag, core, chip, False, [do_feed, do_intra0]
    )
    feed0, ((fq0, eq0, scores0, num0, kt0), (cot_next, second_y)) = made
    (
        den0, att0, att_low0, hidden1, first1, again, second1, fk1, v1, ek1, keep, send, wide1,
    ) = call(
        middle_kernel,
        "middle",
        [masks, num0, kt0, fq0, *entered0, Layer(out_weight, 0), out_bias]
        + [hidden0, feed0, *front_of(1, tables)],
        [far, far, far_low, far] + front_outs + [far],
    )
    row, wide_row = Far((1, D)), Far((1, FF))

    def feed_back(layer, second, up_low, up, hidden, more):
        return call(
            functools.partial(feed_back_kernel, layer),
            "feed_back",
            [second, in_bias, down_bias, up_low, *feed_chunks(layer)]
            + [up, hidden, Layer(norm_gain, layer)],
            [far if more else tall, row, row, wide_row] + more,
        )

    def do_intra1(gate):
        seconds1.append(flip(gate(wide1.array), "batch", 1))
        return intra(1, gate(again), fk1, v1)

    def do_feed_back1(gate):
        made = feed_back(1, gate(second1), cot, cot, hidden1, [far])
        return made, seconds1[0]

    seconds1 = []
    entered1, made = exchange(
        keep, send, flag, core, chip, False, [do_intra1, do_feed_back1]
    )
    fq1, eq1, scores1, num1, kt1 = made[0]
    ((base1, sgain1, sshift1, gib1, feed1), second_next) = made[1]
    att_low1, gnum1, gden1, keep, send = call(
        turn_kernel,
        "turn",
        [masks, num1, kt1, fq1, *entered1, Layer(out_weight, 1), cot],
        [far_low, fat, tall, packed_state, packed_state],
        [pltpu.VMEM((tokens, D), f32)] * 2,
    )

    def intra_back(fq, fk, v, scores, gnum, gden, entered, eq, place):
        return call(
            intra_back_kernel,
            "intra_back",
            [masks, fq, fk, v, scores, gnum, gden, *entered, eq, tables, dct],
            [fat, place, place],
        )

    def do_intra_back1(gate):
        second_x.append(flip(gate(wide0.array), "batch", 1))
        return intra_back(gate(fq1), fk1, v1, scores1, gnum1, gden1, entered1, eq1, far)

    def do_feed_grad1(gate):
        made = feed_grad([after(gate(gnum1), wide1), second_next], [cot_wide, Layer(cot_next)], 1, (0, 2))
        return made, second_x[0]

    second_x = []
    (mine, theirs), made = exchange(
        keep, send, flag, core, chip, True, [do_intra_back1, do_feed_grad1]
    )
    (gq1, gfk1, gval1), ((feed_keep1, feed_send1), second_x) = made
    second_xy = flip(tie(second_x, wide0.array)[1], "batch", 3)
    feed_got1 = flip(feed_send1, "seq", 1)
    mine, theirs, feed_got1 = tie(mine, theirs, feed_got1)
    sums1 = [Halving(feed_keep1[k] + feed_got1[k]) for k in range(2)]
    got = sums1[0].send()
    vector_outs = [Far((1, 3 * D)), row, row]
    packed = sds((tokens, 3 * D), bf16)
    gp1, gqb1, ggain1, gshift1, up0, up_low0, gnum0, gden0, keep, send = call(
        turn_back_kernel,
        "turn_back",
        [masks, mine, theirs, gfk1, gval1, fk1, v1, ek1, tables, dct, gq1]
        + [*qkv_parts(1, (0, 2, 1)), hidden1, Layer(norm_gain, 1), base1]
        + [Layer(out_weight, 0), den0, att0, fq0],
        [packed, *vector_outs, tall, fat, fat, tall, packed_state, packed_state],
    )
    ups0 = [up0]

    def do_feed_back(gate):
        ups0.extend(flip(gate(up0), "batch", bit) for bit in (1, 2))
        return feed_back(0, second0, gate(up_low0), up0, hidden0, []), second_xy, got

    def do_intra_back0(gate):
        ups0.append(flip(gate(up0), "batch", 3))
        return (
            intra_back(gate(fq0), fk0, v0, scores0, gnum0, gden0, entered0, eq0, tall),
            packed_grad(gate(first1), att_low1, gp1, cot, (1, 2)),
            ups0[1:3],
        )

    (mine, theirs), made = exchange(
        keep, send, flag, core, chip, True, [do_feed_back, do_intra_back0]
    )
    ((base0, sgain0, sshift0, gib0), second_xy, got), made = made[0], made[1]
    (gq0, gfk0, gval0), parts1, ups0[1:3] = made
    sums1[0].add(got)
    keep1a, send1a, keep1b, send1b = parts1
    got1a, got1b = flip(send1a.array, "seq", 1), flip(send1b.array, "seq", 1)
    mine, theirs, got1a, got1b = tie(mine, theirs, got1a, got1b)
    gp0, gqb0, ggain0, gshift0, ginputs = call(
        last_kernel,
        "last",
        [masks, mine, theirs, gfk0, gval0, fk0, v0, ek0, tables, dct, gq0]
        + [*qkv_parts(0, (0, 2, 1)), hidden0, Layer(norm_gain, 0), base0],
        [packed, sds((1, 3 * D)), sds((1, D)), sds((1, D)), tall],
    )
    vectors = (ggain0, sgain0, gshift0, sshift0, gqb0, gib0)
    vectors += (ggain1, sgain1, gshift1, sshift1, gqb1, gib1, cot)
    *made, ginputs = packed_grad(
        first0, att_low0, gp0, up_low0, (1, 2), vectors, [Parked(ginputs)]
    )
    made, ups0[3], got = together(made, ups0[3], sums1[1].send())
    sums1[1].add(got)
    keep0a, send0a, keep0b, send0b = made
    got0a, got0b = flip(send0a, "seq", 1), flip(send0b, "seq", 1)
    first1a = flip(keep1a[2:] + got1a[2:], "batch", 1)
    first1b = flip(keep1b[2:] + got1b[2:], "batch", 2)
    grads0, got0a, got0b, got, first1a, first1b = together(
        feed_grad([wide0, *map(Layer, (second_x, second_y, second_xy))], ups0, 0, (0,)),
        got0a, got0b, sums1[0].send(), first1a, first1b,
    )
    feed_keep0, feed_send0 = grads0
    sums1[0].add(got)
    feed_got0 = flip(feed_send0, "seq", 1)
    first0a = flip(keep0a[2:] + got0a[2:], "batch", 1)
    first0b = flip(keep0b[2:] + got0b[2:], "batch", 2)
    (result,) = call(
        result_kernel,
        "result",
        [hidden1, feed1, att_low1, Layer(out_weight, 1), out_bias],
        [far_low],
    )
    feed_got0, first0a, first0b, result, got = together(
        feed_got0, first0a, first0b, result, sums1[1].send()
    )
    sums1[1].add(got)
    sums1 = [part.finish() for part in sums1]
    feed0 = Halving(feed_keep0[0] + feed_got0[0])
    got_feed0 = feed0.send()

    def second(part0, part1, at, bit):
        parts = [sum(x[at] for x in part).reshape(size // 2, -1, D // 2) for part in (part0, part1)]
        both = jnp.concatenate(parts, axis=1).reshape(-1, D // 2)
        return both if bit is None else flip(both, "batch", bit)

    a0, a1 = (keep0a, got0a, first0a), (keep1a, got1a, first1a)
    b0, b1 = (keep0b, got0b, first0b), (keep1b, got1b, first1b)
    second_a, second_b = second(a0, a1, 1, 2), second(b0, b1, 1, 1)
    got_feed0, second_a, second_b = tie(got_feed0, second_a, second_b)

    feed0.add(got_feed0)
    feed0 = feed0.finish()
    packed = Halving(
        jnp.concatenate(
            [second(a0, a1, 0, None) + second_a, second(b0, b1, 0, None) + second_b], axis=1
        )
    )
    other1 = flip(jnp.concatenate([sums1[1], sums1[0]], axis=0), "batch", 2)
    other0, got, other1 = tie(flip(feed0, "batch", 1), packed.send(), other1)
    packed.add(got)
    mine1 = jnp.concatenate(sums1, axis=0) + other1
    other1 = flip(mine1, "batch", 1)
    other0_y = flip(jnp.concatenate([feed0, other0], axis=0), "batch", 2)
    got, other1, other0_y = tie(packed.send(), other1, other0_y)
    packed.add(got)
    feed_pieces, packed_pieces = [feed0, other0, other0_y, mine1, other1], spread(packed.finish())
    slot = D // size
    if quarter_wide == HEAD:
        outs = [Far((2, slot, FF)), Far((2, FF // size, D))]
        ready, *packed_pieces[1:] = together(
            call(join_feed_kernel, "join_feed", feed_pieces, outs), *packed_pieces[1:]
        )
        outs = [
            Far((2, slot, 3 * D)),
            Far((2, slot, D)),
            Far((2, 2, slot)),
            Far((2, 2, slot)),
            Far((3, 2, slot)),
            Far((2, slot)),
            Far((2, slot)),
            Far((2, FF // size)),
        ]
        ready += call(join_packed_kernel, "join_packed", packed_pieces, outs)
        joined = [x.array for x in ready]
    else:
        joined = join(feed_pieces + packed_pieces, size)
    grad_in, grad_down, grad_qkv, grad_out, gain, shift, grad_qkv_b, out_b, down_b, in_b = joined
    return (
        result.array.reshape(rows, length, D),
        ginputs.array.reshape(rows, length, D),
        gain,
        shift,
        grad_qkv,
        grad_qkv_b.swapaxes(0, 1),
        grad_out,
        out_b,
        grad_in,
        in_b,
        grad_down,
        down_b,
    )


def solution(mesh):
    placed = (
        P("batch", "seq", None),
        P("batch", None),
        P("batch", "seq", None),
        P(),
        P(),
        P(),
        P(),
        P(),
        P(),
        P(),
        P(),
        P(),
        P(),
    )
    return jax.shard_map(
        per_device,
        mesh=mesh,
        in_specs=placed,
        out_specs=(
            P("batch", "seq", None),
            P("batch", "seq", None),
            P(None, None, "seq"),
            P(None, None, "seq"),
            P(None, "seq", None),
            P(None, None, "seq"),
            P(None, "seq", None),
            P(None, "seq"),
            P(None, "seq", None),
            P(None, "seq"),
            P(None, "seq", None),
            P(None, "seq"),
        ),
        check_vma=False,
    )
```

```python
import functools
import math

import jax
import jax.numpy as jnp
import numpy as np
from jax import lax
from jax.experimental import pallas as pl
from jax.experimental.pallas import tpu as pltpu
from jax.sharding import PartitionSpec as P

D = 512
HEADS = 8
HEAD = 64
FF = 2048
ROT = 16
LAYERS = 2
NDOC = 4
LEN = 128
PAIRS = HEADS // 2
PACK = 2 * HEAD + 8
WIDE = 512

epsilon = 1e-05
f32, bf16 = jnp.float32, jnp.bfloat16
NN = (((1,), (0,)), ((), ()))
NT = (((1,), (1,)), ((), ()))
TN = (((0,), (0,)), ((), ()))


def dot(a, b, dims=NN):
    return lax.dot_general(a, b, dims, preferred_element_type=f32)


def split(x):
    high = x.astype(bf16)
    return high, (x - high.astype(f32)).astype(bf16)


def sds(shape, dtype=f32):
    return jax.ShapeDtypeStruct(shape, dtype)


def norm_parts(hidden):
    centred = hidden - jnp.mean(hidden, axis=-1, keepdims=True)
    variance = jnp.mean(centred * centred, axis=-1, keepdims=True)
    inverse = lax.rsqrt(variance + epsilon)
    return centred * inverse, inverse


def segment_of(position, starts, row):
    found = jnp.zeros_like(position)
    for k in range(NDOC):
        entry = starts[row, k]
        found = jnp.maximum(found, jnp.where(entry <= position, entry, 0))
    return found


def prepare(starts, masks, tables):
    begin = lax.axis_index("seq") * LEN
    for row in range(masks.shape[1]):
        at_i = begin + lax.broadcasted_iota(jnp.int32, (LEN, 128), 0)
        at_j = begin + lax.broadcasted_iota(jnp.int32, (LEN, 128), 1)
        seg_i, seg_j = segment_of(at_i, starts, row), segment_of(at_j, starts, row)
        last = jnp.int32(0)
        for k in range(NDOC):
            entry = starts[row, k]
            last = jnp.maximum(last, jnp.where(entry <= begin + (LEN - 1), entry, 0))
        masks[0, row] = jnp.where((at_j <= at_i) & (seg_i == seg_j), 1.0, 0.0).astype(f32)
        masks[1, row] = jnp.where(seg_i < begin, 1.0, 0.0).astype(f32)
        masks[2, row] = jnp.where(seg_i == last, 1.0, 0.0).astype(f32)
        lane = lax.broadcasted_iota(jnp.int32, (LEN, 128), 1) % HEAD
        inverse = jnp.zeros((LEN, 128), f32)
        for k in range(ROT // 2):
            here = (lane < ROT) & (lane % (ROT // 2) == k)
            inverse = jnp.where(here, 10000.0 ** (-2.0 * k / ROT), inverse)
        angles = (at_i - seg_i).astype(f32) * inverse
        at = slice(row * LEN, (row + 1) * LEN)
        tables[0, at] = jnp.cos(angles)
        tables[1, at] = jnp.sin(angles)


def masks_of(row, masks):
    return masks[0, row], masks[1, row], masks[2, row]


def low_lanes(rows):
    return lax.broadcasted_iota(jnp.int32, (rows, 128), 1) < HEAD


def read_tables(tables):
    sine = tables[1]
    lane = lax.broadcasted_iota(jnp.int32, sine.shape, 1) % HEAD
    ahead = jnp.where(lane < ROT // 2, -sine, 0.0)
    behind = jnp.where((lane >= ROT // 2) & (lane < ROT), sine, 0.0)
    return tables[0], ahead, behind


def rotate(x, tables):
    base, ahead, behind = tables
    return x * base + pltpu.roll(x, 120, 1) * ahead + pltpu.roll(x, 8, 1) * behind


def rotate_back(g, tables):
    base, ahead, behind = tables
    return g * base + pltpu.roll(g * ahead, 8, 1) + pltpu.roll(g * behind, 120, 1)


def featurize(x, tables, high, low):
    pieces = [rotate(x[:, g * 128 : (g + 1) * 128], tables) for g in range(4)]
    found = []
    for g in range(2):
        a, b = split(jnp.concatenate(pieces[2 * g : 2 * g + 2], axis=1))
        found.append(jnp.exp(dot(a, high) + dot(b, high) + dot(a, low)))
    return jnp.concatenate(found, axis=1)


def unfeaturize(g, tables, high, low):
    found = []
    for k in range(2):
        a, b = split(g[:, k * 256 : (k + 1) * 256])
        back = dot(a, high, NT) + dot(b, high, NT) + dot(a, low, NT)
        found += [rotate_back(back[:, :128], tables), rotate_back(back[:, 128:], tables)]
    return jnp.concatenate(found, axis=1)


def head_ones():
    across = lax.broadcasted_iota(jnp.int32, (256, 256), 0) // HEAD
    along = lax.broadcasted_iota(jnp.int32, (256, 256), 1) // HEAD
    return jnp.where(across == along, 1.0, 0.0).astype(bf16)


def head_sum(x, ones):
    found = []
    for g in range(2):
        a, b = split(x[:, g * 256 : (g + 1) * 256])
        found.append(dot(a, ones) + dot(b, ones))
    return jnp.concatenate(found, axis=1)


def store_halves(keep_ref, send_ref, halves):
    def put(ref, half):
        for row, at, value in halves[half]:
            ref[row, at[0] : at[1], :] = value

    core = lax.axis_index("seq") % 2
    for mine in range(2):

        @pl.when(core == mine)
        def _():
            put(keep_ref, mine)
            put(send_ref, 1 - mine)


def pack_states(rows, left_of, right, norm_of):
    low = low_lanes(HEAD)
    halves = [[], []]
    for row in range(rows):
        at = slice(row * LEN, (row + 1) * LEN)
        left, norm = left_of(row), norm_of(row)
        for pair in range(PAIRS):
            lanes = slice(pair * 128, (pair + 1) * 128)
            both = dot(left[:, lanes], right[at, lanes], TN)
            half, place = pair // 2, pair % 2
            halves[half].append(
                (row, (place * HEAD, (place + 1) * HEAD), jnp.where(low, both[:HEAD], both[HEAD:]))
            )
        for half in range(2):
            pieces = [norm[:, (2 * half + k) * 128 : (2 * half + k + 1) * 128] for k in range(2)]
            block = jnp.concatenate(pieces + [jnp.zeros((6, 128), f32)], axis=0)
            halves[half].append((row, (2 * HEAD, PACK), block))
    return halves


def unpack_state(mine_ref, theirs_ref, row):
    low = low_lanes(HEAD)
    blocks, norms = [], []
    for half in range(2):
        here = lax.axis_index("seq") % 2 == half
        packed = jnp.where(here, mine_ref[row], theirs_ref[row])
        for place in range(2):
            state = packed[place * HEAD : (place + 1) * HEAD]
            both = jnp.concatenate(
                [jnp.where(low, state, 0.0), jnp.where(low, 0.0, state)], axis=0
            )
            blocks.append(split(both))
            norms.append(packed[2 * HEAD + place : 2 * HEAD + place + 1])
    return blocks, jnp.concatenate(norms, axis=1)


def cross_dot(x, block, dims=NN):
    return dot(x, block[0], dims) + dot(x, block[1], dims)


def gelu_parts(lifted):
    phi = 0.5 + 0.5 * lax.erf(lifted * math.sqrt(0.5))
    slope = phi + lifted * (jnp.exp(-0.5 * lifted * lifted) * (1.0 / math.sqrt(2.0 * math.pi)))
    return lifted * phi, slope


def norm_back(grad, xhat, inverse, gain):
    u = grad * gain
    mean_u = jnp.mean(u, axis=-1, keepdims=True)
    mean_ux = jnp.mean(u * xhat, axis=-1, keepdims=True)
    down = (u - mean_u - xhat * mean_ux) * inverse
    return down, jnp.sum(grad * xhat, axis=0, keepdims=True), jnp.sum(grad, axis=0, keepdims=True)


def front_body(layer, masks, hidden, gain, shift, b, tables, dct, wk, wv, outs):
    first_ref, again_ref, second_ref, fk_ref, v_ref, ek_ref, keep_ref, send_ref, wide_ref = outs
    xhat, _ = norm_parts(hidden)
    gains, shifts = gain[...].astype(f32), shift[...].astype(f32)
    first = (xhat * gains[0:1] + shifts[0:1]).astype(bf16)
    first_ref[...] = first
    again_ref[...] = first
    second = (xhat * gains[1:2] + shifts[1:2]).astype(bf16)
    second_ref[...] = second
    wide_ref[...] = second.astype(f32)
    bias = [b[k][layer : layer + 1].astype(f32) for k in range(3)]
    tabs = read_tables(tables)
    high, low = dct[0], dct[1]
    keys = dot(first, wk[...]) + bias[1]
    values = (dot(first, wv[...]) + bias[2]).astype(bf16)
    v_ref[...] = values
    exp_k = featurize(keys, tabs, high, low)
    ek_ref[...] = exp_k
    feat_k = exp_k.astype(bf16)
    fk_ref[...] = feat_k
    rows = hidden.shape[0] // LEN
    wide = feat_k.astype(f32)

    def tailed(row):
        tail = masks_of(row, masks)[2]
        return wide[row * LEN : (row + 1) * LEN] * jnp.concatenate([tail] * 4, axis=1)

    kept = [tailed(row) for row in range(rows)]
    halves = pack_states(
        rows,
        lambda row: kept[row].astype(bf16),
        values,
        lambda row: jnp.sum(kept[row], axis=0, keepdims=True),
    )
    store_halves(keep_ref, send_ref, halves)


def front_kernel(starts, cot, h, gain, shift, b, dct, wk, wv, *outs):
    *outs, masks, tables = outs
    outs[9][...] = cot[...].astype(f32)
    prepare(starts, masks, tables)
    hidden = h[...].astype(f32)
    front_body(0, masks, hidden, gain, shift, b, tables, dct, wk, wv, outs[:9])


def attend(masks, num_ref, kt_ref, fq_ref, mine_ref, theirs_ref, den_ref, att_ref, low_ref):
    rows = num_ref.shape[0] // LEN
    ones = head_ones()
    for row in range(rows):
        at = slice(row * LEN, (row + 1) * LEN)
        cross = masks_of(row, masks)[1]
        cross4 = jnp.concatenate([cross] * 4, axis=1)
        blocks, norm = unpack_state(mine_ref, theirs_ref, row)
        fq = fq_ref[at]
        far = jnp.concatenate(
            [cross_dot(fq[:, p * 128 : (p + 1) * 128], blocks[p]) for p in range(PAIRS)], axis=1
        )
        num = num_ref[at] + cross4 * far
        den = head_sum(fq.astype(f32) * (kt_ref[at] + cross4 * norm), ones)
        att = num / den
        den_ref[at] = den
        att_ref[at] = att
        low_ref[at] = att.astype(bf16)
    begin_writing(den_ref, att_ref, low_ref)


def middle_kernel(
    masks, num, kt, fq0, mine, theirs, ow, ob, h, feed, gain, shift, b, tables, dct, wk, wv,
    den, att, att_low, h2, *outs,
):
    attend(masks, num, kt, fq0, mine, theirs, den, att, att_low)
    hidden = h[...].astype(f32) + (dot(att_low[...], ow[...]) + ob[0:1].astype(f32)) + feed[...]
    h2[...] = hidden
    front_body(1, masks, hidden, gain, shift, b, tables, dct, wk, wv, outs)


def attend_back(masks, rows, ga, den, att, fq, gnum, gden, keep_ref, send_ref):
    den_v = den[...]
    gn = (ga / den_v).astype(bf16)
    gnum[...] = gn
    gd = -head_sum(ga * att[...], head_ones()) / den_v
    gden[...] = gd
    wide = fq[...].astype(f32)

    def crossed(row):
        cross = masks_of(row, masks)[1]
        return wide[row * LEN : (row + 1) * LEN] * jnp.concatenate([cross] * 4, axis=1)

    kept = [crossed(row) for row in range(rows)]
    halves = pack_states(
        rows,
        lambda row: kept[row].astype(bf16),
        gn,
        lambda row: jnp.sum(kept[row] * gd[row * LEN : (row + 1) * LEN], axis=0, keepdims=True),
    )
    store_halves(keep_ref, send_ref, halves)


def turn_kernel(
    masks, num, kt, fq, mine, theirs, ga, att_low, gnum, gden, keep, send, den, att,
):
    attend(masks, num, kt, fq, mine, theirs, den, att, att_low)
    attend_back(masks, fq.shape[0] // LEN, ga[...], den, att, fq, gnum, gden, keep, send)


CHUNKS = FF // WIDE


def feed_kernel(second, ib, db, *refs):
    chunks, (cot, ow, feed, ga) = refs[:-4], refs[-4:]
    total = jnp.broadcast_to(db[0:1].astype(f32), feed.shape)
    for g in range(CHUNKS):
        iw, dw = chunks[2 * g : 2 * g + 2]
        bias = ib[0:1, g * WIDE : (g + 1) * WIDE].astype(f32)
        lifted = dot(second[...], iw[...]) + bias
        total = total + dot(gelu_parts(lifted)[0].astype(bf16), dw[...])
    ga[...] = dot(cot[...], ow[...], NT)
    feed[...] = total


def feed_back_kernel(layer, second, ib, db, up_low, *refs):
    chunks, (up, h, gain, base, gain_out, shift_out, gib, *feed) = (
        refs[: 2 * CHUNKS],
        refs[2 * CHUNKS :],
    )
    total = jnp.broadcast_to(db[layer : layer + 1].astype(f32), base.shape)
    back = jnp.zeros(base.shape, f32)
    low_up = up_low[...]
    for g in range(CHUNKS):
        lanes = slice(g * WIDE, (g + 1) * WIDE)
        iw, dw = (part[...] for part in chunks[2 * g : 2 * g + 2])
        lifted = dot(second[...], iw) + ib[layer : layer + 1, lanes].astype(f32)
        value, slope = gelu_parts(lifted)
        if feed:
            total = total + dot(value.astype(bf16), dw)
        low = (dot(low_up, dw, NT) * slope).astype(bf16)
        gib[:, lanes] = jnp.sum(low.astype(f32), axis=0, keepdims=True)
        back = back + dot(low, iw, NT)
    if feed:
        feed[0][...] = total
    xhat, inverse = norm_parts(h[...].astype(f32))
    gains = gain[...].astype(f32)
    part, gain_out[...], shift_out[...] = norm_back(back, xhat, inverse, gains[1:2])
    base[...] = up[...].astype(f32) + part


def intra_kernel(layer, masks, first, wq, b, tables, dct, fk, v, fq, eq, scores, num, kt):
    queries = dot(first[...], wq[...]) + b[0][layer : layer + 1].astype(f32)
    exp_q = featurize(queries, read_tables(tables), dct[0], dct[1])
    eq[...] = exp_q
    fq[...] = exp_q.astype(bf16)
    low = low_lanes(LEN)
    even = jnp.where(low, 1.0, 0.0).astype(bf16)
    odd = jnp.where(low, 0.0, 1.0).astype(bf16)
    for row in range(fq.shape[0] // LEN):
        at = slice(row * LEN, (row + 1) * LEN)
        intra = masks_of(row, masks)[0]
        kt[at] = dot(intra.astype(bf16), fk[at])
        twice = jnp.concatenate([intra, intra], axis=0)
        for pair in range(PAIRS):
            lanes = slice(pair * 128, (pair + 1) * 128)
            q = fq[at, lanes]
            both = jnp.concatenate([q * even, q * odd], axis=0)
            rounded = (dot(both, fk[at, lanes], NT) * twice).astype(bf16)
            scores[row, pair] = rounded
            out = dot(rounded, v[at, lanes])
            num[at, lanes] = jnp.where(low, out[:LEN], out[LEN:])


def intra_back_kernel(
    masks, fq, fk, v, scores, gnum, gden, mine, theirs, eq, tables, dct, gq, gfk, gval
):
    low = low_lanes(LEN)
    even = jnp.where(low, 1.0, 0.0).astype(bf16)
    odd = jnp.where(low, 0.0, 1.0).astype(bf16)
    grad = []
    for row in range(fq.shape[0] // LEN):
        at = slice(row * LEN, (row + 1) * LEN)
        intra, cross, _ = masks_of(row, masks)
        twice = jnp.concatenate([intra, intra], axis=0)
        blocks, norm = unpack_state(mine, theirs, row)
        queries = []
        for pair in range(PAIRS):
            lanes = slice(pair * 128, (pair + 1) * 128)
            gn, gd, q, k = gnum[at, lanes], gden[at, lanes], fq[at, lanes], fk[at, lanes]
            both = jnp.concatenate([gn * even, gn * odd], axis=0)
            turned = pltpu.roll(gd, HEAD, 1)
            dens = jnp.concatenate(
                [jnp.where(low, gd, turned), jnp.where(low, turned, gd)], axis=0
            )
            gs = ((dot(both, v[at, lanes], NT) + dens) * twice).astype(bf16)
            near = dot(gs, k)
            far = cross_dot(gn, blocks[pair], NT) + gd * norm[:, lanes]
            queries.append(jnp.where(low, near[:LEN], near[LEN:]) + cross * far)
            gfk[at, lanes] = jnp.where(low, dot(gs[:LEN], q, TN), dot(gs[LEN:], q, TN))
            sl = scores[row, pair]
            gval[at, lanes] = jnp.where(low, dot(sl[:LEN], gn, TN), dot(sl[LEN:], gn, TN))
        grad.append(jnp.concatenate(queries, axis=1))
    begin_writing(gfk, gval)
    turned = unfeaturize(
        jnp.concatenate(grad, axis=0) * eq[...], read_tables(tables), dct[0], dct[1]
    )
    gq[...] = turned.astype(bf16)


def packed_back(masks, mine, theirs, gq, gfk, gval, fk, v, ek, tables, dct, gp, gqb):
    keys, values = [], []
    for row in range(fk.shape[0] // LEN):
        at = slice(row * LEN, (row + 1) * LEN)
        tail = masks_of(row, masks)[2]
        blocks, norm = unpack_state(mine, theirs, row)
        key_row, value_row = [], []
        for pair in range(PAIRS):
            lanes = slice(pair * 128, (pair + 1) * 128)
            far = cross_dot(v[at, lanes], blocks[pair], NT) + norm[:, lanes]
            key_row.append(gfk[at, lanes] + tail * far)
            value_row.append(gval[at, lanes] + tail * cross_dot(fk[at, lanes], blocks[pair]))
        keys.append(jnp.concatenate(key_row, axis=1))
        values.append(jnp.concatenate(value_row, axis=1))
    gp[:, 2 * D :] = jnp.concatenate(values, axis=0).astype(bf16)
    gp[:, :D] = gq[...]
    keys = unfeaturize(
        jnp.concatenate(keys, axis=0) * ek[...], read_tables(tables), dct[0], dct[1]
    )
    gp[:, D : 2 * D] = keys.astype(bf16)
    gqb[...] = jnp.sum(gp[...].astype(f32), axis=0, keepdims=True)


def upstream_back(base, hidden, gp, weights, gain, gain_out, shift_out):
    gfirst = sum(
        dot(gp[:, k * D : (k + 1) * D], part[...], NT) for k, part in zip((0, 2, 1), weights)
    )
    xhat, inverse = norm_parts(hidden)
    part, gain_out[...], shift_out[...] = norm_back(
        gfirst, xhat, inverse, gain[...].astype(f32)[0:1]
    )
    return base[...] + part


def turn_back_kernel(
    masks, mine, theirs, gfk, gval, fk, v, ek, tables, dct, gq, wq, wv, wk, h, gain, base, ow, den, att, fq,
    gp, gqb, ggain, gshift, up_ref, up_low, gnum, gden, keep, send,
):
    packed_back(masks, mine, theirs, gq, gfk, gval, fk, v, ek, tables, dct, gp, gqb)
    up = upstream_back(base, h[...], gp, (wq, wv, wk), gain, ggain, gshift)
    up_ref[...] = up
    low = up.astype(bf16)
    up_low[...] = low
    ga = dot(low, ow[...], NT)
    attend_back(masks, fq.shape[0] // LEN, ga, den, att, fq, gnum, gden, keep, send)


def result_kernel(h, feed, att_low, ow, ob, result):
    hidden = h[...] + (dot(att_low[...], ow[...]) + ob[1:2].astype(f32)) + feed[...]
    result[...] = hidden.astype(bf16)


def last_kernel(
    masks, mine, theirs, gfk, gval, fk, v, ek, tables, dct, gq, wq, wv, wk, h, gain, base,
    gp, gqb, ggain, gshift, ginputs,
):
    packed_back(masks, mine, theirs, gq, gfk, gval, fk, v, ek, tables, dct, gp, gqb)
    weights = (wq, wv, wk)
    ginputs[...] = upstream_back(base, h[...].astype(f32), gp, weights, gain, ggain, gshift)


def gathered(size, x, flat, held):
    block = flat.shape[0] // size
    flat[...] = x.astype(f32).T
    for place in range(size):
        source = block_at(size, place)
        held[place * block : (place + 1) * block, :] = flat[
            pl.ds(pl.multiple_of(source * block, block), block), :
        ]
    return held[...].astype(bf16)


def reversed_bits(value, count):
    return sum(((value >> k) & 1) << (count - 1 - k) for k in range(count))


def block_at(size, place):
    return reversed_bits(place, size.bit_length() - 1) ^ lax.axis_index("seq")


def pick_quarter(size, layer, q, ib, chunks, iw_q, ib_q, dw_q):
    wide = FF // size
    rows = lax.broadcasted_iota(jnp.int32, (128, 128), 0) - HEAD * (q % 2)
    lanes = lax.broadcasted_iota(jnp.int32, (128, 128), 1)
    left = jnp.where((rows == lanes) & (lanes < HEAD), 1.0, 0.0).astype(bf16)
    right = jnp.where((rows == lanes - HEAD) & (lanes >= HEAD), 1.0, 0.0).astype(bf16)
    quarter = wide // 4
    for pair in range(size // 2):
        iw, dw = chunks[2 * pair : 2 * pair + 2]
        here = slice(pair * 128, (pair + 1) * 128)
        at = [k * wide + (q // 2) * 128 for k in range(2)]
        cut = [pl.ds(pl.multiple_of(begin, 128), 128) for begin in at]
        iw_q[:, here] = (dot(iw[:, cut[0]], left) + dot(iw[:, cut[1]], right)).astype(bf16)
        cut = [pl.ds(pl.multiple_of(pair * 2 * wide + begin, 128), 128) for begin in at]
        bias = [ib[:, part] for part in cut]
        ib_q[:, here] = (dot(bias[0], left) + dot(bias[1], right))[layer : layer + 1]
        for k in range(2):
            s = 2 * pair + k
            picked = pl.ds(pl.multiple_of(k * wide + q * quarter, quarter), quarter)
            dw_q[s * quarter : (s + 1) * quarter, :] = dw[picked, :]


def feed_grad_kernel(size, layer, groups, quarters, *refs):
    count = len(quarters)
    own = FF // size // 4 == HEAD
    weights, refs = refs[: 1 + 2 * CHUNKS if own else 3 * count], refs[1 + 2 * CHUNKS if own else 3 * count :]
    seconds, ups, refs = refs[:groups], refs[groups : 2 * groups], refs[2 * groups :]
    keep, send, s_all, u_all, act, lift, out, *picked = refs
    tokens = s_all.shape[0] // groups
    block = D // size
    for n, quarter in enumerate(quarters):
        if own:
            q = lax.axis_index("batch") ^ quarter
            pick_quarter(size, layer, q, weights[0], weights[1:], *picked)
            iw, ib, dw = picked
        else:
            iw, ib, dw = weights[3 * n : 3 * n + 3]
        for k in range(groups):
            at = slice(k * tokens, (k + 1) * tokens)
            if n == 0:
                s_all[at], u_all[at] = seconds[k][...].astype(bf16), ups[k][...].astype(bf16)
            lifted = dot(s_all[at], iw[...]) + ib[...].astype(f32)
            value, slope = gelu_parts(lifted)
            act[at] = value.astype(bf16)
            lift[at] = (dot(u_all[at], dw[...], NT) * slope).astype(bf16)
        for part, grads in enumerate(
            (dot(s_all[...], lift[...], TN), dot(act[...], u_all[...], TN))
        ):
            for s in range(size):
                place = reversed_bits(s ^ lax.axis_index("seq"), size.bit_length() - 1)
                at = pl.multiple_of((2 * place + part) * block, block)
                out[pl.ds(at, block), :] = grads[s * block : (s + 1) * block]
        keep[n], send[n] = out[:D], out[D:]


def chosen(refs, index):
    value = refs[0][...]
    for k in range(1, len(refs)):
        value = jnp.where(index == k, refs[k][...], value)
    return value


def join_feed_kernel(feed0, x0, y0, feed1, x1, in_out, down_out):
    me = lax.axis_index("batch")
    block = in_out.shape[1]
    low, two = low_lanes(block), 2 * block
    for layer in range(2):
        if layer == 0:
            held = (feed0, x0, y0.at[:two], y0.at[two:])
        else:
            held = (feed1.at[:two], x1.at[:two], feed1.at[two:], x1.at[two:])
        for pair in range(2):
            left, right = (chosen(held, (2 * pair + k) ^ me) for k in range(2))
            down_out[layer, 2 * pair * block : (2 * pair + 1) * block, :] = left[block:]
            down_out[layer, (2 * pair + 1) * block : (2 * pair + 2) * block, :] = right[block:]
            for tile in range(D // 128):
                lanes = slice(tile * 128, (tile + 1) * 128)
                a, b = left[:block, lanes], right[:block, lanes]
                at = 2 * tile * 256 + pair * 128
                in_out[layer, :, at : at + 128] = jnp.where(low, a, pltpu.roll(b, 64, 1))
                in_out[layer, :, at + 256 : at + 384] = jnp.where(low, pltpu.roll(a, 64, 1), b)


def join_packed_kernel(*refs):
    pieces, outs = refs[:4], refs[4:]
    qkv_out, out_out, gain_out, shift_out, qkvb_out, outb_out, downb_out, inb_out = outs
    me = lax.axis_index("batch")
    block = qkv_out.shape[1]
    for layer in range(2):
        begin = layer * (block + 8)
        for q in range(4):
            packed = chosen(pieces, q ^ me)[begin : begin + block + 8 * (1 - layer)]
            qkv_out[layer, :, q * 384 : (q + 1) * 384] = packed[:block, :384]
            out_out[layer, :, q * 128 : (q + 1) * 128] = packed[:block, 384:]
            if layer == 0 and q < 2:
                lines = packed[block:]
                gain_out[q] = lines[0:2, :block]
                shift_out[q] = lines[2:4, :block]
                for k in range(3):
                    qkvb_out[k, q : q + 1, :] = lines[4 + k : 5 + k, :block]
                outb_out[q : q + 1, :] = lines[7:8, :block]
                downb_out[q : q + 1, :] = lines[7:8, :block]
                inb_out[q : q + 1, :] = lines[0:1, 256 : 256 + inb_out.shape[1]]


PARTS = ((0, 256), (256, 512))


def standing(quarter, bit):
    return jnp.where(bit == 1, (quarter % 2) * 2 + quarter // 2, quarter)


def packed_grad_kernel(size, bits, more, *refs):
    first, att_low, gp, up, *refs = refs[more:]
    *vectors, keep_a, send_a, keep_b, send_b, f1, h1 = refs
    block, under = D // size, 8 if vectors else 0
    half, me = size // 2, lax.axis_index("batch")
    for source, right, wide, begin in ((first, gp, 384, 0), (att_low, up, 128, 384)):
        left = gathered(size, source[...], f1, h1)
        for q in range(4):
            out = dot(left, right[:, q * wide : (q + 1) * wide])
            for (low, high), bit, refs in zip(PARTS, bits, ((keep_a, send_a), (keep_b, send_b))):
                lanes = max(low, begin), min(high, begin + wide)
                if lanes[0] >= lanes[1]:
                    continue
                at = standing(q ^ me, bit)
                for place in range(size):
                    here = (place % half) * (block + under)
                    refs[place // half][
                        at, here : here + block, lanes[0] - low : lanes[1] - low
                    ] = out[
                        place * block : (place + 1) * block, lanes[0] - begin : lanes[1] - begin
                    ]
    if vectors:
        put_lines(size, bits, vectors, up, ((keep_a, send_a), (keep_b, send_b)))


def put_lines(size, bits, vectors, up, parts):
    block, wide, me = D // size, FF // size, lax.axis_index("batch")
    held = []
    for *norms, gqb, gib, ups in ((*vectors[:6], up), vectors[6:]):
        gob = jnp.sum(ups[...].astype(f32), axis=0, keepdims=True)
        rows = [part[...] for part in norms]
        rows += [gqb[:, k * D : (k + 1) * D] for k in range(3)] + [gob]
        held.append((jnp.concatenate(rows, axis=0), jnp.broadcast_to(gib[...], (8, FF))))
    for place in range(size):
        source = block_at(size, place)
        here = (place % (size // 2)) * (block + 8) + block
        a_ref, b_ref = (refs[place // (size // 2)] for refs in parts)
        for layer, (rows, line) in enumerate(held):
            a_ref[standing(layer ^ me, bits[0]), here : here + 8, :128] = pltpu.roll(
                rows, (D - source * block) % D, 1
            )[:, :128]
            b_ref[standing(layer ^ me, bits[1]), here : here + 8, :] = pltpu.roll(
                line, (FF - source * wide) % FF, 1
            )[:, :256]
            a_ref[standing(layer ^ me, bits[0]), here : here + 8, 128:] = jnp.zeros((8, 128), f32)
        for k in (2, 3):
            for ref, bit in ((a_ref, bits[0]), (b_ref, bits[1])):
                ref[standing(k ^ me, bit), here : here + 8, :] = jnp.zeros((8, 256), f32)


class Layer:
    def __init__(self, array, index=None):
        self.array, self.index = array, index
        self.shape = array.shape if index is None else jax.eval_shape(lambda x: x[index], array).shape


class Far:
    def __init__(self, shape, dtype=f32):
        self.shape, self.dtype = shape, dtype


class Parked:
    def __init__(self, array):
        self.array = array


class Scalars:
    def __init__(self, array):
        self.array = array


class Source:
    def __init__(self, here, there, semaphore):
        self.here, self.copy = here, pltpu.make_async_copy(there, here, semaphore)
        self.shape, self.copying = here.shape, True
        self.copy.start()

    def __getitem__(self, at):
        if self.copying:
            self.copy.wait()
            self.copying = False
        return self.here[at]


class Target:
    def __init__(self, here, there, semaphore):
        self.here, self.copy = here, pltpu.make_async_copy(here, there, semaphore)
        self.shape, self.started = here.shape, False

    def __getitem__(self, at):
        return self.here[at]

    def __setitem__(self, at, value):
        assert not self.started
        self.here[at] = value
        if at is Ellipsis:
            self.start()

    def start(self):
        if not self.started:
            self.copy.start()
            self.started = True


def begin_writing(*results):
    for result in results:
        if isinstance(result, Target):
            result.start()


def call(kernel, name, operands, outs, scratch=()):
    arrays = [getattr(operand, "array", operand) for operand in operands]
    copied = [k for k, operand in enumerate(operands) if isinstance(operand, Layer)]
    written = [k for k, out in enumerate(outs) if isinstance(out, Far)]
    parked = [k for k, operand in enumerate(operands) if isinstance(operand, Parked)]
    arrays = [
        a
        if isinstance(o, Scalars)
        else pltpu.with_memory_space_constraint(a, pltpu.HBM if isinstance(o, Layer) else pltpu.VMEM)
        for o, a in zip(operands, arrays)
    ]
    vmem, smem = pl.BlockSpec(memory_space=pltpu.VMEM), pl.BlockSpec(memory_space=pltpu.SMEM)
    hbm = pl.BlockSpec(memory_space=pltpu.HBM)
    own = 1 + len(copied) + len(written)
    shown = len(outs)
    outs = list(outs) + [Far(arrays[k].shape, arrays[k].dtype) for k in parked]

    def body(*refs):
        ins, results = list(refs[: len(operands)]), list(refs[len(operands) :][: len(outs)])
        semaphores, *buffers = refs[len(operands) + len(outs) :]
        results, places = results[:shown], results[shown:]
        copies = [
            pltpu.make_async_copy(ins[k], place, semaphores.at[own - 1 + n])
            for n, (k, place) in enumerate(zip(parked, places))
        ]
        for copy in copies:
            copy.start()
        for n, k in enumerate(copied):
            index = operands[k].index
            there = ins[k] if index is None else ins[k].at[index]
            ins[k] = Source(buffers[n], there, semaphores.at[n])
        for n, k in enumerate(written):
            n += len(copied)
            results[k] = Target(buffers[n], results[k], semaphores.at[n])
        kernel(*ins, *results, *buffers[own - 1 :])
        assert not any(ins[k].copying for k in copied), name
        for k in written:
            results[k].start()
        for k in written:
            results[k].copy.wait()
        for copy in copies:
            copy.wait()

    found = pl.pallas_call(
        body,
        name=name,
        in_specs=[
            smem if isinstance(o, Scalars) else hbm if isinstance(o, Layer) else vmem
            for o in operands
        ],
        out_specs=[hbm if isinstance(o, Far) else vmem for o in outs],
        out_shape=[(pltpu.HBM if isinstance(o, Far) else pltpu.VMEM)(o.shape, o.dtype) for o in outs],
        scratch_shapes=[
            pltpu.SemaphoreType.DMA((max(own - 1 + len(parked), 1),)),
            *[pltpu.VMEM(operands[k].shape, arrays[k].dtype) for k in copied],
            *[pltpu.VMEM(outs[k].shape, outs[k].dtype) for k in written],
            *scratch,
        ],
        cost_estimate=pl.CostEstimate(flops=1024, bytes_accessed=1024, transcendentals=0),
        compiler_params=pltpu.CompilerParams(vmem_limit_bytes=26 * 1024 * 1024),
    )(*arrays)
    return [Layer(x) if isinstance(o, Far) else x for x, o in zip(found, outs)]


def cosine_table():
    frequency = np.arange(HEAD, dtype=np.float64)[:, None]
    columns = np.arange(HEAD, dtype=np.float64)[None, :]
    entries = np.cos(math.pi * (2.0 * columns + 1.0) * frequency / (2.0 * HEAD))
    entries = entries * math.sqrt(2.0 / HEAD)
    entries[0] *= math.sqrt(0.5)
    wide = np.kron(np.eye(4), entries.T)
    high = wide.astype(np.float32).astype(bf16)
    low = (wide.astype(np.float32) - high.astype(np.float32)).astype(bf16)
    return jnp.asarray(np.stack([high, low]))


def rotary_tables(places):
    lane = jnp.arange(128) % HEAD
    half = ROT // 2
    inverse = 10000.0 ** (-((lane % half).astype(f32) * 2.0 / ROT))
    inverse = jnp.where(lane < ROT, inverse, 0.0)
    angles = places.astype(f32)[:, None] * inverse[None, :]
    return jnp.stack([jnp.cos(angles), jnp.sin(angles)])


def flip(value, axis, bit):
    size = lax.axis_size(axis)
    return lax.ppermute(value, axis, [(i, i ^ bit) for i in range(size)])


def tie(*values):
    return lax.optimization_barrier(values)


def after(first, x):
    if isinstance(x, Layer):
        return Layer(tie(first, x.array)[1], x.index)
    return tie(first, x)[1]


jax.tree_util.register_pytree_node(
    Layer, lambda x: ((x.array,), x.index), lambda index, leaves: Layer(*leaves, index)
)


def together(*values):
    leaves, tree = jax.tree.flatten(values)
    return jax.tree.unflatten(tree, tie(*leaves))


def exchange(keep, send, flag, core, chip, backward, works=(), beside_core=()):
    chips = lax.axis_size("seq") // 2
    begin, span = chip * 2 * LEN, 2 * LEN
    got = flip(send, "seq", 1)
    if beside_core:
        got, *came = tie(got, *beside_core)
    even, odd = jnp.where(core == 0, keep, got), jnp.where(core == 0, got, keep)
    if backward:
        total = even + flag(begin + LEN - 1, begin) * odd
    else:
        total = odd + flag(begin + span - 1, begin + LEN) * even
    entered, made, step = None, [], 1
    while step < chips:
        other = flip(total, "seq", 2 * step)
        if len(made) < len(works):
            found = works[len(made)](lambda x, total=total: after(total, x))
            leaves, tree = jax.tree.flatten(found)
            other, *leaves = tie(other, *leaves)
            made.append(jax.tree.unflatten(tree, leaves))
        upper = (chip // step) % 2 == 1
        first = chip - chip % (2 * step)
        middle = first + step
        later, earlier = jnp.where(upper, total, other), jnp.where(upper, other, total)
        if backward:
            passed = jnp.where(upper, 0.0, flag(middle * span - 1, (chip + 1) * span))
            total = earlier + flag(middle * span - 1, first * span) * later
        else:
            passed = jnp.where(upper, flag(chip * span - 1, middle * span), 0.0)
            total = later + flag((middle + step) * span - 1, middle * span) * earlier
        entered = passed * other if entered is None else entered + passed * other
        step *= 2
    if backward:
        for_even, for_odd = odd + flag(begin + span - 1, begin + LEN) * entered, entered
    else:
        for_even, for_odd = entered, even + flag(begin + LEN - 1, begin) * entered
    mine = jnp.where(core == 0, for_even, for_odd)
    theirs = flip(jnp.where(core == 0, for_odd, for_even), "seq", 1)
    return (mine, theirs), made + ([came] if beside_core else [])


def spread(x):
    return [x] + [flip(x, "batch", bit) for bit in (1, 2, 3)]


class Halving:
    def __init__(self, total):
        self.total, self.step = total, 2

    def send(self):
        return flip(self.total[self.total.shape[0] // 2 :], "seq", self.step)

    def tail(self):
        return self.total[self.total.shape[0] // 2 :]

    def add(self, got):
        self.total = self.total[: self.total.shape[0] // 2] + got
        self.step *= 2

    def finish(self):
        while self.step < lax.axis_size("seq"):
            self.add(self.send())
        return self.total


def join(pieces, size):
    order = np.arange(4) ^ lax.axis_index("batch")
    slot = D // size
    feed0, x0, y0, feed1, x1, *packed = pieces
    feed0 = [feed0, x0, y0[: 2 * slot], y0[2 * slot :]]
    feed1 = [feed1[: 2 * slot], x1[: 2 * slot], feed1[2 * slot :], x1[2 * slot :]]
    pieces = [jnp.take(jnp.stack(part), order, axis=0) for part in (feed0, feed1, packed)]
    pieces = [pieces[0], pieces[2][:, : slot + 8], pieces[1], pieces[2][:, slot + 8 :]]
    slot = D // size
    made = [[], [], [], []]
    for feed, packed in (pieces[:2], pieces[2:]):
        made[0].append(
            feed[:, :slot].reshape(4, slot, size, slot).transpose(1, 2, 0, 3).reshape(slot, FF)
        )
        made[1].append(feed[:, slot:].reshape(4 * slot, D))
        packed = packed[:, :slot]
        made[2].append(packed[:, :, :384].swapaxes(0, 1).reshape(slot, 3 * D))
        made[3].append(packed[:, :, 384:].swapaxes(0, 1).reshape(slot, D))
    made = [jnp.stack(part) for part in made]
    lines = pieces[1][:2, slot:]
    vectors = lines[:, :, :slot]
    made += [vectors[:, 0:2], vectors[:, 2:4], vectors[:, 4:7].swapaxes(0, 1)]
    return made + [vectors[:, 7], vectors[:, 7], lines[:, 0, 256 : 256 + FF // size]]


def per_device(
    inputs,
    doc_starts,
    cotangent,
    norm_gain,
    norm_bias,
    qkv_weight,
    qkv_bias,
    out_weight,
    out_bias,
    in_weight,
    in_bias,
    down_weight,
    down_bias,
):
    rows, length = inputs.shape[0], inputs.shape[1]
    tokens = rows * length
    size = lax.axis_size("seq")
    me, column = lax.axis_index("seq"), lax.axis_index("batch")
    core, chip = me % 2, me // 2
    def segment_at(position):
        return jnp.max(jnp.where(doc_starts <= position, doc_starts, 0), axis=1)

    def flag(position, limit):
        return (segment_at(position) < limit).astype(f32)[:, None, None]

    dct = Layer(cosine_table())
    hidden0 = Layer(inputs.reshape(tokens, D))
    cot = Layer(cotangent.reshape(tokens, D))
    qkv_bias_t, out_bias = Layer(qkv_bias.swapaxes(0, 1)), Layer(out_bias)
    in_bias, down_bias = Layer(in_bias), Layer(down_bias)

    tall, fat = sds((tokens, D)), sds((tokens, D), bf16)
    far, far_low = Far((tokens, D)), Far((tokens, D), bf16)
    packed_state = sds((rows, PACK, 128))
    front_outs = [far_low, fat, far_low, far_low, far_low, far, packed_state, packed_state]

    def qkv_parts(layer, order):
        return [
            Layer(qkv_weight, (layer, slice(None), slice(k * D, (k + 1) * D))) for k in order
        ]

    def front_of(layer, *given):
        norms = [Layer(norm_gain, layer), Layer(norm_bias, layer), qkv_bias_t]
        return [*norms, *given, dct, *qkv_parts(layer, (1, 2))]

    quarter_wide = FF // size // 4
    def feed_chunks(layer):
        parts = []
        for g in range(CHUNKS):
            here = slice(g * WIDE, (g + 1) * WIDE)
            parts.append(Layer(in_weight, (layer, slice(None), here)))
            parts.append(Layer(down_weight, (layer, here, slice(None))))
        return parts

    def quarter_weights(layer, quarter):
        shape = (size, 4, quarter_wide)
        pick = functools.partial(lax.dynamic_index_in_dim, index=column ^ quarter, keepdims=False)
        return [
            pick(in_weight[layer].reshape((D,) + shape), axis=2).reshape(D, D),
            pick(in_bias.array[layer].reshape(shape), axis=1).reshape(1, D),
            pick(down_weight[layer].reshape(shape + (D,)), axis=1).reshape(D, D),
        ]

    def feed_grad(seconds, ups, layer, quarters):
        groups = len(seconds)
        scratch = [pltpu.VMEM((groups * tokens, D), bf16)] * 4 + [pltpu.VMEM((2 * D, D), f32)]
        if quarter_wide == HEAD:
            weights = [in_bias, *feed_chunks(layer)]
            scratch += [pltpu.VMEM((D, D), bf16), pltpu.VMEM((1, D), f32), pltpu.VMEM((D, D), bf16)]
        else:
            weights = [w for quarter in quarters for w in quarter_weights(layer, quarter)]
        return call(
            functools.partial(feed_grad_kernel, size, layer, groups, quarters),
            "feed_grad",
            [*weights, *seconds, *ups],
            [sds((len(quarters), D, D))] * 2,
            scratch,
        )

    def packed_grad(first, att_low, gp, up, bits, vectors=(), more=()):
        rows_of = D // 2 + (size // 2 * 8 if vectors else 0)
        return call(
            functools.partial(packed_grad_kernel, size, bits, len(more)),
            "packed_grad",
            [*more, first, att_low, gp, up, *vectors],
            [sds((4, rows_of, D // 2)), (sds if vectors else Far)((4, rows_of, D // 2))] * 2,
            [pltpu.VMEM((D, tokens), f32)] * 2,
        )

    first0, again, second0, fk0, v0, ek0, keep, send, wide0, cot_wide, *prepared = call(
        front_kernel,
        "front",
        [Scalars(doc_starts), cot, hidden0, *front_of(0)],
        front_outs + [far, far, sds((3, rows, LEN, 128)), sds((2, tokens, 128))],
    )
    masks, tables = prepared
    intra_outs = [far_low, far, Far((rows, PAIRS, 2 * LEN, LEN), bf16), tall, tall]

    def near_two(x):
        return [flip(x, "batch", bit) for bit in (1, 2)]

    def last_one(x):
        return flip(x, "batch", 3)

    def do_feed(gate):
        operands = [gate(second0), in_bias, down_bias, *feed_chunks(0), cot, Layer(out_weight, 1)]
        return call(feed_kernel, "feed", operands, [tall, far])

    def do_intra0(gate):
        return intra(0, gate(again), fk0, v0), cots

    cots = [flip(cot_wide.array, "batch", 1), flip(wide0.array, "batch", 2)]

    def intra(layer, first, fk, v):
        operands = [masks, first, *qkv_parts(layer, (0,)), qkv_bias_t, tables, dct, fk, v]
        return call(functools.partial(intra_kernel, layer), "intra", operands, intra_outs)

    entered0, made = exchange(
        keep, send, flag, core, chip, False, [do_feed, do_intra0]
    )
    (feed0, ga1), ((fq0, eq0, scores0, num0, kt0), (cot_next, second_y)) = made
    (
        den0, att0, att_low0, hidden1, first1, again, second1, fk1, v1, ek1, keep, send, wide1,
    ) = call(
        middle_kernel,
        "middle",
        [masks, num0, kt0, fq0, *entered0, Layer(out_weight, 0), out_bias]
        + [hidden0, feed0, *front_of(1, tables)],
        [far, far, far_low, far] + front_outs + [far],
    )
    row, wide_row = Far((1, D)), Far((1, FF))

    def feed_back(layer, second, up_low, up, hidden, more):
        return call(
            functools.partial(feed_back_kernel, layer),
            "feed_back",
            [second, in_bias, down_bias, up_low, *feed_chunks(layer)]
            + [up, hidden, Layer(norm_gain, layer)],
            [far if more else tall, row, row, wide_row] + more,
        )

    def do_intra1(gate):
        seconds1.append(flip(gate(wide1.array), "batch", 1))
        return intra(1, gate(again), fk1, v1)

    def do_feed_back1(gate):
        made = feed_back(1, gate(second1), cot, cot, hidden1, [far])
        return made, seconds1[0]

    seconds1 = []
    entered1, made = exchange(
        keep, send, flag, core, chip, False, [do_intra1, do_feed_back1]
    )
    fq1, eq1, scores1, num1, kt1 = made[0]
    ((base1, sgain1, sshift1, gib1, feed1), second_next) = made[1]
    att_low1, gnum1, gden1, keep, send = call(
        turn_kernel,
        "turn",
        [masks, num1, kt1, fq1, *entered1, ga1],
        [far_low, fat, tall, packed_state, packed_state],
        [pltpu.VMEM((tokens, D), f32)] * 2,
    )

    def intra_back(fq, fk, v, scores, gnum, gden, entered, eq, place):
        return call(
            intra_back_kernel,
            "intra_back",
            [masks, fq, fk, v, scores, gnum, gden, *entered, eq, tables, dct],
            [fat, place, place],
        )

    def do_intra_back1(gate):
        second_x.append(flip(gate(wide0.array), "batch", 1))
        return intra_back(gate(fq1), fk1, v1, scores1, gnum1, gden1, entered1, eq1, far)

    def do_feed_grad1(gate):
        made = feed_grad([after(gate(gnum1), wide1), second_next], [cot_wide, Layer(cot_next)], 1, (0, 2))
        return made, second_x[0]

    second_x = []
    (mine, theirs), made = exchange(
        keep, send, flag, core, chip, True, [do_intra_back1, do_feed_grad1]
    )
    (gq1, gfk1, gval1), ((feed_keep1, feed_send1), second_x) = made
    second_xy = flip(tie(second_x, wide0.array)[1], "batch", 3)
    feed_got1 = flip(feed_send1, "seq", 1)
    mine, theirs, feed_got1 = tie(mine, theirs, feed_got1)
    sums1 = [Halving(feed_keep1[k] + feed_got1[k]) for k in range(2)]
    got = sums1[0].send()
    vector_outs = [Far((1, 3 * D)), row, row]
    packed = sds((tokens, 3 * D), bf16)
    gp1, gqb1, ggain1, gshift1, up0, up_low0, gnum0, gden0, keep, send = call(
        turn_back_kernel,
        "turn_back",
        [masks, mine, theirs, gfk1, gval1, fk1, v1, ek1, tables, dct, gq1]
        + [*qkv_parts(1, (0, 2, 1)), hidden1, Layer(norm_gain, 1), base1]
        + [Layer(out_weight, 0), den0, att0, fq0],
        [packed, *vector_outs, tall, fat, fat, tall, packed_state, packed_state],
    )
    ups0 = [up0]

    def do_feed_back(gate):
        ups0.extend(flip(gate(up0), "batch", bit) for bit in (1, 2))
        return feed_back(0, second0, gate(up_low0), up0, hidden0, []), second_xy, got

    def do_intra_back0(gate):
        ups0.append(flip(gate(up0), "batch", 3))
        return (
            intra_back(gate(fq0), fk0, v0, scores0, gnum0, gden0, entered0, eq0, tall),
            packed_grad(gate(first1), att_low1, gp1, cot, (1, 2)),
            ups0[1:3],
        )

    (mine, theirs), made = exchange(
        keep, send, flag, core, chip, True, [do_feed_back, do_intra_back0]
    )
    ((base0, sgain0, sshift0, gib0), second_xy, got), made = made[0], made[1]
    (gq0, gfk0, gval0), parts1, ups0[1:3] = made
    sums1[0].add(got)
    keep1a, send1a, keep1b, send1b = parts1
    got1a, got1b = flip(send1a.array, "seq", 1), flip(send1b.array, "seq", 1)
    mine, theirs, got1a, got1b = tie(mine, theirs, got1a, got1b)
    gp0, gqb0, ggain0, gshift0, ginputs = call(
        last_kernel,
        "last",
        [masks, mine, theirs, gfk0, gval0, fk0, v0, ek0, tables, dct, gq0]
        + [*qkv_parts(0, (0, 2, 1)), hidden0, Layer(norm_gain, 0), base0],
        [packed, sds((1, 3 * D)), sds((1, D)), sds((1, D)), tall],
    )
    vectors = (ggain0, sgain0, gshift0, sshift0, gqb0, gib0)
    vectors += (ggain1, sgain1, gshift1, sshift1, gqb1, gib1, cot)
    *made, ginputs = packed_grad(
        first0, att_low0, gp0, up_low0, (1, 2), vectors, [Parked(ginputs)]
    )
    made, ups0[3], got = together(made, ups0[3], sums1[1].send())
    sums1[1].add(got)
    keep0a, send0a, keep0b, send0b = made
    got0a, got0b = flip(send0a, "seq", 1), flip(send0b, "seq", 1)
    first1a = flip(keep1a[2:] + got1a[2:], "batch", 1)
    first1b = flip(keep1b[2:] + got1b[2:], "batch", 2)
    grads0, got0a, got0b, got, first1a, first1b = together(
        feed_grad([wide0, *map(Layer, (second_x, second_y, second_xy))], ups0, 0, (0,)),
        got0a, got0b, sums1[0].send(), first1a, first1b,
    )
    feed_keep0, feed_send0 = grads0
    sums1[0].add(got)
    feed_got0 = flip(feed_send0, "seq", 1)
    first0a = flip(keep0a[2:] + got0a[2:], "batch", 1)
    first0b = flip(keep0b[2:] + got0b[2:], "batch", 2)
    (result,) = call(
        result_kernel,
        "result",
        [hidden1, feed1, att_low1, Layer(out_weight, 1), out_bias],
        [far_low],
    )
    feed_got0, first0a, first0b, result, got = together(
        feed_got0, first0a, first0b, result, sums1[1].send()
    )
    sums1[1].add(got)
    sums1 = [part.finish() for part in sums1]
    feed0 = Halving(feed_keep0[0] + feed_got0[0])
    got_feed0 = feed0.send()

    def second(part0, part1, at, bit):
        parts = [sum(x[at] for x in part).reshape(size // 2, -1, D // 2) for part in (part0, part1)]
        both = jnp.concatenate(parts, axis=1).reshape(-1, D // 2)
        return both if bit is None else flip(both, "batch", bit)

    a0, a1 = (keep0a, got0a, first0a), (keep1a, got1a, first1a)
    b0, b1 = (keep0b, got0b, first0b), (keep1b, got1b, first1b)
    second_a, second_b = second(a0, a1, 1, 2), second(b0, b1, 1, 1)
    got_feed0, second_a, second_b = tie(got_feed0, second_a, second_b)

    feed0.add(got_feed0)
    feed0 = feed0.finish()
    packed = Halving(
        jnp.concatenate(
            [second(a0, a1, 0, None) + second_a, second(b0, b1, 0, None) + second_b], axis=1
        )
    )
    other1 = flip(jnp.concatenate([sums1[1], sums1[0]], axis=0), "batch", 2)
    other0, got, other1 = tie(flip(feed0, "batch", 1), packed.send(), other1)
    packed.add(got)
    mine1 = jnp.concatenate(sums1, axis=0) + other1
    other1 = flip(mine1, "batch", 1)
    other0_y = flip(jnp.concatenate([feed0, other0], axis=0), "batch", 2)
    got, other1, other0_y = tie(packed.send(), other1, other0_y)
    packed.add(got)
    feed_pieces, packed_pieces = [feed0, other0, other0_y, mine1, other1], spread(packed.finish())
    slot = D // size
    if quarter_wide == HEAD:
        outs = [Far((2, slot, FF)), Far((2, FF // size, D))]
        ready, *packed_pieces[1:] = together(
            call(join_feed_kernel, "join_feed", feed_pieces, outs), *packed_pieces[1:]
        )
        outs = [
            Far((2, slot, 3 * D)),
            Far((2, slot, D)),
            Far((2, 2, slot)),
            Far((2, 2, slot)),
            Far((3, 2, slot)),
            Far((2, slot)),
            Far((2, slot)),
            Far((2, FF // size)),
        ]
        ready += call(join_packed_kernel, "join_packed", packed_pieces, outs)
        joined = [x.array for x in ready]
    else:
        joined = join(feed_pieces + packed_pieces, size)
    grad_in, grad_down, grad_qkv, grad_out, gain, shift, grad_qkv_b, out_b, down_b, in_b = joined
    return (
        result.array.reshape(rows, length, D),
        ginputs.array.reshape(rows, length, D),
        gain,
        shift,
        grad_qkv,
        grad_qkv_b.swapaxes(0, 1),
        grad_out,
        out_b,
        grad_in,
        in_b,
        grad_down,
        down_b,
    )


def solution(mesh):
    placed = (
        P("batch", "seq", None),
        P("batch", None),
        P("batch", "seq", None),
        P(),
        P(),
        P(),
        P(),
        P(),
        P(),
        P(),
        P(),
        P(),
        P(),
    )
    return jax.shard_map(
        per_device,
        mesh=mesh,
        in_specs=placed,
        out_specs=(
            P("batch", "seq", None),
            P("batch", "seq", None),
            P(None, None, "seq"),
            P(None, None, "seq"),
            P(None, "seq", None),
            P(None, None, "seq"),
            P(None, "seq", None),
            P(None, "seq"),
            P(None, "seq", None),
            P(None, "seq"),
            P(None, "seq", None),
            P(None, "seq"),
        ),
        check_vma=False,
    )
```
